512 devices in a mesh: dp: 32 (over y, x_lo, core), shard: 16 (over z, x_hi).
Axes of the slice: x: 4 (x_hi: 2, x_lo: 2; x = x_hi * 2 + x_lo), y: 8, z: 8, core: 2. Of those that a mesh axis runs over, the one named last changes fastest.
Arguments:
- residual: bfloat16 [16384, 8192], P('shard', 'dp'), may hold values from -66 to 66
- norm_gain: float32 [8192], P('shard'), may hold values from 0.5 to 2
- value_weight: bfloat16 [8192, 512], P('shard'), may hold values from -0.0625 to 0.0625
- rotation: float32 [8192, 8192], P('shard', 'dp'), may hold values from -1.3 to 1.3
- target: bfloat16 [16384, 512], P('shard'), may hold values from -6 to 6
Outputs:
- grad_rotation: float32 [8192, 8192], P('shard', 'dp')
- rotation_next: float32 [8192, 8192], P('shard', 'dp')
The draws below stay inside these ranges and needn't reach their ends.
All inputs are finite; a program needn't handle non-finite values. Where the reference program divides by a largest or mean magnitude, that divisor is 1e-20 or more.
Results may differ from the reference program's by a relative error of at most 0.0039.
Values may be sent and summed in bfloat16 or wider, within the bound.
A program may use at most 64 MiB of HBM per device.

```python
import math
import jax
import jax.numpy as jnp
from jax import lax

D = 8192
ITERS = 2
K = 512
TOKENS = 16384


def draw_residual(key, part):
    key = jax.random.fold_in(key, 11)
    noise_key, scale_key = jax.random.split(key, 2)
    entries = jnp.clip(jax.random.normal(noise_key, (TOKENS, D), jnp.float32), -6.0, 6.0)
    spread = jnp.exp(jax.random.uniform(scale_key, (TOKENS, 1), jnp.float32, 0.0, math.log(10.0)))
    return (entries * spread).astype(jnp.bfloat16)


def draw_rotation(key, part):
    key = jax.random.fold_in(key, 23)
    row_key, column_key, noise_key = jax.random.split(key, 3)
    rows_index = jnp.arange(D, dtype=jnp.int32)[:, None]
    cols_index = jnp.arange(D, dtype=jnp.int32)[None, :]
    parity = jnp.zeros((D, D), jnp.int32)
    for bit_number in range(D.bit_length()):
        row_bits = jnp.bitwise_and(jnp.right_shift(rows_index, bit_number), 1)
        col_bits = jnp.bitwise_and(jnp.right_shift(cols_index, bit_number), 1)
        parity = jnp.bitwise_xor(parity, jnp.bitwise_and(row_bits, col_bits))
    pattern = 1.0 - 2.0 * parity.astype(jnp.float32)
    row_signs = 1.0 - 2.0 * jax.random.randint(row_key, (D, 1), 0, 2).astype(jnp.float32)
    column_signs = 1.0 - 2.0 * jax.random.randint(column_key, (1, D), 0, 2).astype(jnp.float32)
    noise = 0.05 * jnp.clip(jax.random.normal(noise_key, (D, D), jnp.float32), -6.0, 6.0)
    return pattern * row_signs * column_signs + noise


def levels(rng, dims, cuts, low, high):
    def one(position, parts):
        heights = jax.random.uniform(jax.random.fold_in(jax.random.fold_in(rng, 6), position), (parts,), jnp.float32, low / len(cuts), high / len(cuts))
        return jnp.repeat(jnp.exp(heights), dims[position] // parts).reshape((-1,) + (1,) * (len(dims) - position - 1))

    level = one(*cuts[0])
    for cut in cuts[1:]:
        level = level * one(*cut)
    return level


def centred(stream_key, shape, scale, reach, cuts=(), kind=jnp.bfloat16):
    factor_of = levels(stream_key, shape, cuts, -0.22, 0.18) if cuts else 1.0
    values = jax.random.normal(stream_key, shape, jnp.float32) * scale * factor_of
    return jnp.minimum(jnp.maximum(values, -reach), reach).astype(kind)


def setup_inputs(seed: int = 0) -> dict:
    seeds = jax.random.split(jax.random.key(seed), 6)
    residual = draw_residual(jax.random.fold_in(seeds[5], 71), 0)
    norm_gain = jnp.clip(jnp.exp(math.log(2.0) - 1.3862944 * jax.random.uniform(seeds[1], (D,), jnp.float32) ** levels(seeds[1], (D,), ((0, 16),), -0.2, 0.2)), 0.5, 2.0)
    value_weight = centred(seeds[2], (D, K), D ** -0.5, 0.0625, ((0, 16),))
    rotation = draw_rotation(jax.random.fold_in(seeds[5], 71), 0)
    target = centred(seeds[4], (TOKENS, K), 1.0, 6.0, ((0, 16),))
    return {"residual": residual, "norm_gain": norm_gain, "value_weight": value_weight, "rotation": rotation, "target": target}


two_pi = 2.0 * math.pi
precise = lax.Precision.HIGHEST

def soft_round(values):
    return values - jnp.sin(two_pi * values) / two_pi

def reference(residual, norm_gain, value_weight, rotation, target):
    hidden = residual.astype(jnp.float32)
    inv_rms = lax.rsqrt(lax.optimization_barrier(jnp.sum(hidden * hidden, axis=1, keepdims=True)) / D + 1e-05)
    row_peak = lax.optimization_barrier(jnp.max(jnp.abs(hidden), axis=1, keepdims=True)) + 1e-06
    act_quant = (row_peak * inv_rms / 7.0 * soft_round(7.0 * hidden / row_peak)).astype(jnp.bfloat16)
    scaled_weight = norm_gain[:, None] * value_weight.astype(jnp.float32) / math.sqrt(D)
    rotated = jnp.dot(rotation.T, scaled_weight, precision=precise)
    weight_scale = (lax.optimization_barrier(jnp.max(jnp.abs(rotated), axis=0, keepdims=True)) + 1e-06) / 7.0
    weight_quant = (weight_scale * soft_round(rotated / weight_scale)).astype(jnp.bfloat16)
    outputs = jnp.dot(act_quant, weight_quant, preferred_element_type=jnp.float32)
    out_grad = (outputs - target.astype(jnp.float32)).astype(jnp.bfloat16)
    weight_grad = jnp.dot(act_quant.T, out_grad, preferred_element_type=jnp.float32)
    grad_rotation = jnp.dot(scaled_weight, weight_grad.T, precision=precise)
    grad_square = jnp.sum(grad_rotation * grad_rotation)
    step_size = 0.4 * math.sqrt(K) / jnp.sqrt(D * grad_square + 1e-06)
    rotated_grad = jnp.dot(rotation, weight_grad, precision=precise)
    first_terms = jnp.dot(rotated_grad.T, rotation, precision=precise)
    first_step = jnp.dot(scaled_weight, first_terms, precision=precise) - jnp.dot(rotated_grad, rotated.T, precision=precise)
    current = rotation - step_size * first_step
    for sweep_index in range(1, ITERS):
        summed = rotation + current
        left_terms = jnp.dot(rotated_grad.T, summed, precision=precise)
        right_terms = jnp.dot(scaled_weight.T, summed, precision=precise)
        applied = jnp.dot(scaled_weight, left_terms, precision=precise) - jnp.dot(rotated_grad, right_terms, precision=precise)
        current = rotation - 0.5 * step_size * applied
    return (grad_rotation, current)
```

```python
import math

import jax
import jax.numpy as jnp
from jax import lax
from jax.experimental import pallas as pl
from jax.experimental.pallas import tpu as pltpu
from jax.sharding import PartitionSpec as P

D = 8192
N = 16
MESH = pl.DeviceIdType.MESH
F32 = jnp.float32
BF16 = jnp.bfloat16
HIGHEST = lax.Precision.HIGHEST

SINE = (
    0.9999999944722865,
    -6.579735439437006,
    12.987842893121643,
    -12.207428862935943,
    6.687066146603468,
    -2.366367060643953,
    0.5091905906829214,
)

NN = (((1,), (0,)), ((), ()))
NT = (((1,), (1,)), ((), ()))
TN = (((0,), (0,)), ((), ()))


def dot(a, b, dims=NN, precision=None):
    return lax.dot_general(a, b, dims, precision=precision, preferred_element_type=F32)


def soft(v):
    r = v - jnp.floor(v + 0.5)
    s = r * r
    p = jnp.full_like(s, SINE[-1])
    for c in SINE[-2::-1]:
        p = p * s + c
    return v - r * p


def twin(a):
    return jnp.concatenate([a, a], axis=1)


(
    STAT_C, STAT_D, Q_R, PEAK_C, PEAK_D, W_G, Q_G, OUT_C, OUT_R, OG_G, OG_C, G_R, G_G, V_C, V_R, V_G, VC_C,
    P_R, P_G, SQ_C, SQ_D, SQ_S, U_R, U_G, UD_G, UD_C, M_R, M_G, MD_G, MD_C,
) = range(30)
COUNT = 30


def kernel(
    res, gain, weight, rot, target, grad_out, next_out,
    st, rb, act, stat, stat_c, stat_d,
    q_send, q_recv, q_all, w_all,
    peak, peak_c, peak_d,
    out_send, out_c, out_half, out_recv, og_all,
    g_send, g_recv, g_all,
    v_send, v_c, v_half, v_recv, v_all,
    p_send, p_recv, p_all,
    sq, sq_c, sq_d, sq_s,
    u_send, u_recv, u_part, u_all,
    m_send, m_recv, m_part, m_all,
    sends, recvs,
):
    dp, me = lax.axis_index("dp"), lax.axis_index("shard")
    chip, core = lax.div(dp, 2), lax.rem(dp, 2)
    other = 1 - core
    twin_id = (chip * 2 + other, me)

    def shard_id(k):
        return lax.rem(me + k, N)

    def chip_id(k):
        return lax.rem(chip + k, N)

    def shard_dev(k):
        return (dp, shard_id(k))

    def chip_dev(k):
        return (chip_id(k) * 2 + core, me)

    def each(body):
        def step(k, _):
            body(k)
            return 0

        lax.fori_loop(1, N, step, 0)

    def start(src, dst, which, device):
        pltpu.make_async_remote_copy(
            src_ref=src, dst_ref=dst, send_sem=sends.at[which], recv_sem=recvs.at[which],
            device_id=device, device_id_type=MESH,
        ).start()

    sent = []

    def arrived(ref, which):
        pltpu.make_async_copy(ref, ref, recvs.at[which]).wait()
        sent.append((ref, which))

    def scatter(src, dst, which, over_shard):
        def body(k):
            if over_shard:
                start(src.at[shard_id(k)], dst.at[k - 1], which, shard_dev(k))
            else:
                start(src.at[chip_id(k)], dst.at[k - 1], which, chip_dev(k))

        each(body)

    def spread(ref, dst, which, over_shard):
        def body(k):
            start(ref, dst, which, shard_dev(k) if over_shard else chip_dev(k))

        each(body)

    def to_twin(src, dst, which):
        start(src, dst, which, twin_id)

    def total(own, recv):
        acc = own.astype(F32)
        for k in range(N - 1):
            acc = acc + recv[k].astype(F32)
        return acc

    barrier = pltpu.get_barrier_semaphore()
    pl.semaphore_signal(barrier, inc=1, device_id=twin_id, device_id_type=MESH)

    def greet(k):
        pl.semaphore_signal(barrier, inc=1, device_id=shard_dev(k), device_id_type=MESH)
        pl.semaphore_signal(barrier, inc=1, device_id=chip_dev(k), device_id_type=MESH)

    each(greet)

    st[...] = weight[...].astype(F32).T * gain[...] * (1.0 / math.sqrt(D))
    q_send[...] = dot(st[...], rot[...], NN, HIGHEST).reshape(N, 32, 256)
    pl.semaphore_wait(barrier, 2 * N - 1)
    scatter(q_send, q_recv, Q_R, True)

    for k in range(8):
        h = res[128 * k : 128 * k + 128, :].astype(F32)
        a, b = h[:, :128], h[:, 128:]
        stat[k : k + 1, :] = jnp.sum((a * a + b * b).T, axis=0, keepdims=True)
        stat[8 + k : 9 + k, :] = jnp.max(
            jnp.maximum(jnp.abs(a), jnp.abs(b)).T, axis=0, keepdims=True
        )
    to_twin(stat, stat_c, STAT_C)
    rb[...] = rot[...].astype(BF16)
    slot = core * N + chip
    stb = st[...].astype(BF16)
    mine = st[pl.ds(pl.multiple_of(slot * 16, 16), 16), :].astype(BF16)
    u_gram = dot(mine, stb, NT)
    for h in range(2):
        for b in range(4):
            block = u_gram[8 * h : 8 * h + 8, 128 * b : 128 * b + 128]
            u_send[8 * h + b] = block
            u_send[8 * h + 4 + b] = block
    arrived(stat_c, STAT_C)

    def combine(a, b):
        return jnp.concatenate([a[:8] + b[:8], jnp.maximum(a[8:], b[8:])], axis=0)

    both = combine(stat[...], stat_c[...])
    stat_d[0] = both
    each(lambda k: start(stat_d.at[0], stat_d.at[k], STAT_D, chip_dev(k)))

    arrived(q_recv, Q_R)
    q_mine = total(q_send[me], q_recv)
    top = jnp.maximum(jnp.abs(q_mine[:, :128]), jnp.abs(q_mine[:, 128:]))
    top = jnp.max(jnp.concatenate([top] * 4, axis=0).T, axis=0, keepdims=True)
    peak[...] = jnp.broadcast_to(top, (8, 128))
    to_twin(peak, peak_c, PEAK_C)

    arrived(stat_d.at[pl.ds(1, N - 1)], STAT_D)
    for k in range(1, N):
        both = combine(both, stat_d[k])
    row_peak = both[8:] + 1e-06
    inv_rms = lax.rsqrt(both[:8] / D + 1e-05)
    rows_in = 7.0 / row_peak
    rows_out = row_peak * inv_rms / 7.0

    arrived(peak_c, PEAK_C)
    top = jnp.maximum(peak[...], peak_c[...])
    peak_d[0] = top
    each(lambda k: start(peak_d.at[0], peak_d.at[k], PEAK_D, chip_dev(k)))

    for k in range(8):
        into = twin(jnp.broadcast_to(rows_in[k : k + 1, :], (128, 128)).T)
        outof = twin(jnp.broadcast_to(rows_out[k : k + 1, :], (128, 128)).T)
        h = res[128 * k : 128 * k + 128, :].astype(F32)
        act[128 * k : 128 * k + 128, :] = (outof * soft(into * h)).astype(BF16)

    arrived(peak_d.at[pl.ds(1, N - 1)], PEAK_D)
    for k in range(1, N):
        top = jnp.maximum(top, peak_d[k])
    column = jnp.broadcast_to(top[:1, :], (128, 128)).T[:32, :]
    scale = twin((column + 1e-06) / 7.0)
    w_all[me] = (scale * soft(q_mine / scale)).astype(BF16)
    spread(w_all.at[me], w_all.at[me], W_G, True)
    q_all[me] = q_mine.astype(BF16)
    spread(q_all.at[me], q_all.at[me], Q_G, True)
    scatter(u_send, u_recv, U_R, True)

    wanted = slot * 16 + lax.broadcasted_iota(jnp.int32, (16, 512), 0)
    one_hot = jnp.where(lax.broadcasted_iota(jnp.int32, (16, 512), 1) == wanted, 1.0, 0.0)
    target_mine = dot(one_hot.astype(BF16), target[...], NT)

    arrived(w_all.at[pl.ds(0, N - 1)], W_G)

    def half_of(ref, c):
        return ref[pl.ds(c * 8, 8)].reshape(256, 256)

    out_send[...] = dot(half_of(w_all, other), act[...], NT).astype(BF16)
    to_twin(out_send, out_c, OUT_C)
    own = dot(half_of(w_all, core), act[...], NT)
    arrived(out_c, OUT_C)
    out_half[...] = (own + out_c[...].astype(F32)).astype(BF16).reshape(N, 16, 1024)
    scatter(out_half, out_recv, OUT_R, False)

    arrived(u_recv, U_R)
    u_part[me] = total(u_send[me], u_recv)
    spread(u_part.at[me], u_part.at[me], U_G, True)

    arrived(out_recv, OUT_R)
    og_all[slot] = (total(out_half[chip], out_recv) - target_mine).astype(BF16)
    spread(og_all.at[slot], og_all.at[slot], OG_G, False)
    arrived(u_part.at[pl.ds(0, N - 1)], U_G)
    u_all[slot] = jnp.concatenate(
        [
            jnp.concatenate([u_part[8 * h + b] for b in range(4)], axis=1)
            for h in range(2)
        ],
        axis=0,
    ).astype(BF16)
    arrived(og_all.at[pl.ds(0, N - 1)], OG_G)
    og_half = og_all.at[pl.ds(core * N, N)]
    to_twin(og_half, og_half, OG_C)

    def g_part(c):
        og = og_all[pl.ds(c * N, N)].reshape(256, 1024)
        g_send[pl.ds(c * 8, 8)] = dot(og, act[...]).astype(BF16).reshape(8, 32, 256)

    g_part(core)
    arrived(og_all.at[pl.ds(0, N)], OG_C)
    g_part(other)
    scatter(g_send, g_recv, G_R, True)
    spread(u_all.at[slot], u_all.at[slot], UD_G, False)
    arrived(g_recv, G_R)
    g_all[me] = total(g_send[me], g_recv).astype(BF16)
    spread(g_all.at[me], g_all.at[me], G_G, True)
    s_full = st[...].T
    s_high = s_full.astype(BF16)
    s_low = (s_full - s_high.astype(F32)).astype(BF16)
    arrived(u_all.at[pl.ds(0, N - 1)], UD_G)
    u_half = u_all.at[pl.ds(core * N, N)]
    to_twin(u_half, u_half, UD_C)
    arrived(g_all.at[pl.ds(0, N - 1)], G_G)

    v_send[...] = dot(half_of(g_all, other), rb[...], NT).astype(BF16)
    to_twin(v_send, v_c, V_C)
    own = dot(half_of(g_all, core), rb[...], NT)
    arrived(v_c, V_C)
    v_half[...] = (own + v_c[...].astype(F32)).astype(BF16).reshape(N, 16, 512)
    scatter(v_half, v_recv, V_R, False)

    g_full = g_all[...].reshape(512, 256)
    grad = dot(s_high, g_full) + dot(s_low, g_full)
    grad_out[...] = grad
    square = jnp.sum((grad * grad).reshape(64, 8, 256), axis=0)
    sq[...] = square[:, :128] + square[:, 128:]
    to_twin(sq, sq_c, SQ_C)

    arrived(v_recv, V_R)
    v_all[slot] = total(v_half[chip], v_recv).astype(BF16)
    spread(v_all.at[slot], v_all.at[slot], V_G, False)
    arrived(sq_c, SQ_C)
    sq_d[0] = sq[...] + sq_c[...]
    each(lambda k: start(sq_d.at[0], sq_d.at[k], SQ_D, chip_dev(k)))
    arrived(v_all.at[pl.ds(0, N - 1)], V_G)
    v_own = v_all.at[pl.ds(core * N, N)]
    to_twin(v_own, v_own, VC_C)

    def p_part(c):
        vt = v_all[pl.ds(c * N, N)].reshape(256, 512)
        p_send[pl.ds(c * 8, 8)] = dot(vt, rb[...]).astype(BF16).reshape(8, 32, 256)

    p_part(core)
    arrived(v_all.at[pl.ds(0, N)], VC_C)
    p_part(other)
    scatter(p_send, p_recv, P_R, True)

    vt = v_all[...].reshape(512, 512)
    v_mine = v_all[slot]
    for part, right in enumerate((vt, st[...].astype(BF16))):
        gram = dot(v_mine, right, NT)
        for h in range(2):
            for b in range(4):
                m_send[8 * h + 4 * part + b] = gram[
                    8 * h : 8 * h + 8, 128 * b : 128 * b + 128
                ]
    scatter(m_send, m_recv, M_R, True)
    arrived(sq_d.at[pl.ds(1, N - 1)], SQ_D)
    square = sq_d[0]
    for k in range(1, N):
        square = square + sq_d[k]
    sq_s[0] = square
    each(lambda k: start(sq_s.at[0], sq_s.at[k], SQ_S, shard_dev(k)))
    arrived(m_recv, M_R)
    m_part[me] = total(m_send[me], m_recv)
    spread(m_part.at[me], m_part.at[me], M_G, True)
    arrived(m_part.at[pl.ds(0, N - 1)], M_G)
    m_all[slot] = jnp.concatenate(
        [
            jnp.concatenate([m_part[8 * h + b] for b in range(8)], axis=1)
            for h in range(2)
        ],
        axis=0,
    ).astype(BF16)
    spread(m_all.at[slot], m_all.at[slot], MD_G, False)
    arrived(p_recv, P_R)
    p_all[me] = total(p_send[me], p_recv).astype(BF16)
    spread(p_all.at[me], p_all.at[me], P_G, True)

    arrived(sq_s.at[pl.ds(1, N - 1)], SQ_S)
    for k in range(1, N):
        square = square + sq_s[k]
    square = jnp.sum(jnp.sum(square, axis=1, keepdims=True), axis=0, keepdims=True)
    step = 0.4 * math.sqrt(512) * lax.rsqrt(D * square + 1e-06)
    arrived(u_all.at[pl.ds(0, N)], UD_C)
    arrived(q_all.at[pl.ds(0, N - 1)], Q_G)
    q_full = q_all[...].reshape(512, 256)
    uu = u_all[...].reshape(512, 512)

    arrived(m_all.at[pl.ds(0, N - 1)], MD_G)
    m_half = m_all.at[pl.ds(core * N, N)]
    to_twin(m_half, m_half, MD_C)
    arrived(p_all.at[pl.ds(0, N - 1)], P_G)
    p_full = p_all[...].reshape(512, 256)
    arrived(m_all.at[pl.ds(0, N)], MD_C)
    m_full = m_all[...].reshape(512, 1024)
    vv, vu = m_full[:, :512], m_full[:, 512:]
    left = 2.0 * p_full.astype(F32) - step * (dot(vu, p_full) - dot(vv, q_full))
    right = 2.0 * q_full.astype(F32) - step * (dot(uu, p_full) - dot(vu, q_full, TN))
    applied = dot(s_high, left.astype(BF16)) - dot(vt, right.astype(BF16), TN)
    next_out[...] = rot[...] - 0.5 * step * applied

    for ref, which in sent:
        pltpu.make_async_copy(ref, ref, sends.at[which]).wait()


def shards(residual, norm_gain, value_weight, rotation, target):
    vmem = pl.BlockSpec(memory_space=pltpu.VMEM)
    scratch = [
        ((512, 512), F32),
        ((512, 256), BF16),
        ((1024, 256), BF16),
        ((16, 128), F32), ((16, 128), F32), ((N, 16, 128), F32),
        ((N, 32, 256), F32), ((N - 1, 32, 256), F32), ((N, 32, 256), BF16), ((N, 32, 256), BF16),
        ((8, 128), F32), ((8, 128), F32), ((N, 8, 128), F32),
        ((256, 1024), BF16), ((256, 1024), BF16), ((N, 16, 1024), BF16), ((N - 1, 16, 1024), BF16),
        ((2 * N, 16, 1024), BF16),
        ((N, 32, 256), BF16), ((N - 1, 32, 256), BF16), ((N, 32, 256), BF16),
        ((256, 512), BF16), ((256, 512), BF16), ((N, 16, 512), BF16), ((N - 1, 16, 512), BF16),
        ((2 * N, 16, 512), BF16),
        ((N, 32, 256), BF16), ((N - 1, 32, 256), BF16), ((N, 32, 256), BF16),
        ((8, 128), F32), ((8, 128), F32), ((N, 8, 128), F32), ((N, 8, 128), F32),
        ((N, 8, 128), F32), ((N - 1, 8, 128), F32), ((N, 8, 128), F32), ((2 * N, 16, 512), BF16),
        ((N, 8, 128), F32), ((N - 1, 8, 128), F32), ((N, 8, 128), F32), ((2 * N, 16, 1024), BF16),
    ]
    return pl.pallas_call(
        kernel,
        out_shape=[jax.ShapeDtypeStruct((512, 256), F32)] * 2,
        in_specs=[vmem] * 5,
        out_specs=[vmem] * 2,
        scratch_shapes=[pltpu.VMEM(shape, kind) for shape, kind in scratch]
        + [pltpu.SemaphoreType.DMA((COUNT,)), pltpu.SemaphoreType.DMA((COUNT,))],
        compiler_params=pltpu.CompilerParams(
            collective_id=0, has_side_effects=True, vmem_limit_bytes=48 * 2**20
        ),
        cost_estimate=pl.CostEstimate(
            flops=2 * 10**9, bytes_accessed=4 * 2**20, transcendentals=0
        ),
    )(residual, norm_gain.reshape(1, -1), value_weight, rotation, target)


def solution(mesh):
    in_specs = (P("shard", "dp"), P("shard"), P("shard", None), P("shard", "dp"), P("shard", None))
    out_specs = (P("shard", "dp"), P("shard", "dp"))
    return jax.shard_map(
        lambda *a: tuple(shards(*a)), mesh=mesh, in_specs=in_specs, out_specs=out_specs, check_vma=False
    )
```

```python
import math

import jax
import jax.numpy as jnp
from jax import lax
from jax.experimental import pallas as pl
from jax.experimental.pallas import tpu as pltpu
from jax.sharding import PartitionSpec as P

D = 8192
N = 16
MESH = pl.DeviceIdType.MESH
F32 = jnp.float32
BF16 = jnp.bfloat16
HIGHEST = lax.Precision.HIGHEST

SINE = (
    0.9999999944722865,
    -6.579735439437006,
    12.987842893121643,
    -12.207428862935943,
    6.687066146603468,
    -2.366367060643953,
    0.5091905906829214,
)

NN = (((1,), (0,)), ((), ()))
NT = (((1,), (1,)), ((), ()))
TN = (((0,), (0,)), ((), ()))


def dot(a, b, dims=NN, precision=None):
    return lax.dot_general(a, b, dims, precision=precision, preferred_element_type=F32)


def soft(v):
    r = v - jnp.floor(v + 0.5)
    s = r * r
    p = jnp.full_like(s, SINE[-1])
    for c in SINE[-2::-1]:
        p = p * s + c
    return v - r * p


def twin(a):
    return jnp.concatenate([a, a], axis=1)


(
    STAT_C, STAT_D, Q_R, PEAK_C, PEAK_D, W_G, Q_G, G_R, G_G,
    P_R, P_G, SQ_C, SQ_D, SQ_S, U_R, U_G, UD_G, UD_C, M_R, M_G,
) = range(20)
OUT, V = 20, 31
OG, VG, MG = 42, 53, 64
COUNT = 75
FAR = (4, 3, 5, 2, 6, 1, 7)
NEAR = FAR[::-1]


def kernel(
    res_in, gain_in, weight_in, rot_in, target_in, grad_out, next_out,
    res, gain, weight, rot, target, inputs,
    st, rb, act, stat, stat_c, stat_d,
    q_send, q_recv, q_all, w_all,
    peak, peak_c, peak_d,
    out_send, out_c, out_x, out_xr, out_y, out_yr, og_all,
    g_send, g_recv, g_all,
    v_send, v_c, v_x, v_xr, v_y, v_yr, v_all,
    p_send, p_recv, p_all,
    sq, sq_c, sq_d, sq_s,
    u_send, u_recv, u_part, u_all,
    m_send, m_recv, m_part, m_all,
    sends, recvs,
):
    dp, me = lax.axis_index("dp"), lax.axis_index("shard")
    chip, core = lax.div(dp, 2), lax.rem(dp, 2)
    y, xl = lax.div(chip, 2), lax.rem(chip, 2)
    other, xo = 1 - core, 1 - xl
    slot = core * N + xl * 8 + y
    twin_id = (chip * 2 + other, me)
    x_id = ((y * 2 + xo) * 2 + core, me)

    loads = []
    for n, (src, dst) in enumerate(
        ((weight_in, weight), (rot_in, rot), (gain_in, gain), (res_in, res), (target_in, target))
    ):
        rows = src.shape[0]
        cuts = 4 if rows > 1 else 1
        for c in range(cuts):
            part = pl.ds(c * (rows // cuts), rows // cuts)
            pltpu.make_async_copy(src.at[part], dst.at[part], inputs.at[n]).start()
        loads.append(pltpu.make_async_copy(src, dst, inputs.at[n]))

    def y_id(k):
        return ((lax.rem(y + k, 8) * 2 + xl) * 2 + core, me)

    def shard_id(k):
        return lax.rem(me + k, N)

    def chip_id(k):
        return lax.rem(chip + k, N)

    def shard_dev(k):
        return (dp, shard_id(k))

    def chip_dev(k):
        return (chip_id(k) * 2 + core, me)

    def each(body):
        def step(k, _):
            body(k)
            return 0

        lax.fori_loop(1, N, step, 0)

    def start(src, dst, which, device):
        pltpu.make_async_remote_copy(
            src_ref=src, dst_ref=dst, send_sem=sends.at[which], recv_sem=recvs.at[which],
            device_id=device, device_id_type=MESH,
        ).start()

    sent = []

    def arrived(ref, which):
        pltpu.make_async_copy(ref, ref, recvs.at[which]).wait()
        sent.append((ref, which))

    def scatter(src, dst, which, over_shard):
        def body(k):
            if over_shard:
                start(src.at[shard_id(k)], dst.at[k - 1], which, shard_dev(k))
            else:
                start(src.at[chip_id(k)], dst.at[k - 1], which, chip_dev(k))

        each(body)

    def spread(ref, dst, which, over_shard):
        def body(k):
            start(ref, dst, which, shard_dev(k) if over_shard else chip_dev(k))

        each(body)

    def to_twin(src, dst, which):
        start(src, dst, which, twin_id)

    def reduce_dp(part, send, from_twin, x_send, x_recv, y_send, y_recv, base, between=None):
        width = send.shape[2]
        for n, h in enumerate((xo, xl)):
            send[n] = part(other, h).astype(BF16)
            to_twin(send.at[n], from_twin.at[n], base + n)
        own = [part(core, xo), part(core, xl)]
        arrived(from_twin.at[0], base)
        both = own[0] + from_twin[0].astype(F32)
        x_send[...] = both.astype(BF16).reshape(8, 16, width)
        for k in FAR + (0,):
            start(x_send.at[lax.rem(y + k, 8)], x_recv.at[k], base + 2 + k, x_id)
        arrived(from_twin.at[1], base + 1)
        both = own[1] + from_twin[1].astype(F32)
        y_send[...] = both.reshape(8, 16, width)
        for k in FAR:
            arrived(x_recv.at[k], base + 2 + k)
            x_recv[k] = (y_send[lax.rem(y + k, 8)] + x_recv[k].astype(F32)).astype(BF16)
            start(x_recv.at[k], y_recv.at[k - 1], base + 10, y_id(k))
        if between is not None:
            between()
        arrived(x_recv.at[0], base + 2)
        acc = y_send[y] + x_recv[0].astype(F32)
        arrived(y_recv, base + 10)
        for k in range(7):
            acc = acc + y_recv[k].astype(F32)
        return acc

    def gather_own(ref, base):
        own = ref.at[slot]
        for k in FAR:
            start(own, own, base + k, y_id(k))
        start(own, own, base + 8, x_id)
        for k in NEAR:
            block = ref.at[core * N + xl * 8 + lax.rem(y + 8 - k, 8)]
            arrived(block, base + k)
            start(block, block, base + 8, x_id)
        near = ref.at[pl.ds(core * N + xl * 8, 8)]
        to_twin(near, near, base + 9)
        far = ref.at[pl.ds(core * N + xo * 8, 8)]
        arrived(far, base + 8)
        to_twin(far, far, base + 10)

    def gather_other(ref, base):
        arrived(ref.at[pl.ds(0, 8)], base + 9)
        arrived(ref.at[pl.ds(0, 8)], base + 10)

    def total(own, recv):
        acc = own.astype(F32)
        for k in range(N - 1):
            acc = acc + recv[k].astype(F32)
        return acc

    barrier = pltpu.get_barrier_semaphore()
    pl.semaphore_signal(barrier, inc=1, device_id=twin_id, device_id_type=MESH)

    def greet(k):
        pl.semaphore_signal(barrier, inc=1, device_id=shard_dev(k), device_id_type=MESH)
        pl.semaphore_signal(barrier, inc=1, device_id=chip_dev(k), device_id_type=MESH)

    each(greet)

    loads[0].wait()
    loads[2].wait()
    st[...] = weight[...].astype(F32).T * gain[...] * (1.0 / math.sqrt(D))
    loads[1].wait()
    q = dot(st[...], rot[...], NN, HIGHEST).reshape(N, 32, 256)
    high = q.astype(BF16)
    q_send[:, :32] = high
    high = high.astype(F32)
    rest = jnp.floor((q - high) * (15 * 256.0) / (jnp.abs(high) + 1e-30) + 0.5)
    rest = jnp.clip(rest, -7.0, 7.0)
    q_send[:, 32:] = (rest[:, :16] * 16.0 + rest[:, 16:]).astype(BF16)
    pl.semaphore_wait(barrier, 2 * N - 1)
    scatter(q_send, q_recv, Q_R, True)

    loads[3].wait()
    for k in range(8):
        h = res[128 * k : 128 * k + 128, :].astype(F32)
        a, b = h[:, :128], h[:, 128:]
        stat[k : k + 1, :] = jnp.sum((a * a + b * b).T, axis=0, keepdims=True)
        stat[8 + k : 9 + k, :] = jnp.max(
            jnp.maximum(jnp.abs(a), jnp.abs(b)).T, axis=0, keepdims=True
        )
    to_twin(stat, stat_c, STAT_C)
    rb[...] = rot[...].astype(BF16)
    stb = st[...].astype(BF16)
    mine = st[pl.ds(pl.multiple_of(slot * 16, 16), 16), :].astype(BF16)
    u_gram = dot(mine, stb, NT)
    for h in range(2):
        for b in range(4):
            block = u_gram[8 * h : 8 * h + 8, 128 * b : 128 * b + 128]
            u_send[8 * h + b] = block
            u_send[8 * h + 4 + b] = block
    arrived(stat_c, STAT_C)

    def combine(a, b):
        return jnp.concatenate([a[:8] + b[:8], jnp.maximum(a[8:], b[8:])], axis=0)

    both = combine(stat[...], stat_c[...])
    stat_d[0] = both
    each(lambda k: start(stat_d.at[0], stat_d.at[k], STAT_D, chip_dev(k)))

    arrived(q_recv, Q_R)

    def decode(a):
        high, rest = a[:32].astype(F32), a[32:].astype(F32)
        upper = jnp.floor(rest * 0.0625 + 0.5)
        rest = jnp.concatenate([upper, rest - 16.0 * upper], axis=0)
        return high + rest * (jnp.abs(high) * (1.0 / (15 * 256)))

    q_mine = decode(q_send[me])
    for k in range(N - 1):
        q_mine = q_mine + decode(q_recv[k])
    top = jnp.maximum(jnp.abs(q_mine[:, :128]), jnp.abs(q_mine[:, 128:]))
    top = jnp.max(jnp.concatenate([top] * 4, axis=0).T, axis=0, keepdims=True)
    peak[...] = jnp.broadcast_to(top, (8, 128))
    to_twin(peak, peak_c, PEAK_C)

    arrived(stat_d.at[pl.ds(1, N - 1)], STAT_D)
    for k in range(1, N):
        both = combine(both, stat_d[k])
    row_peak = both[8:] + 1e-06
    inv_rms = lax.rsqrt(both[:8] / D + 1e-05)
    rows_in = 7.0 / row_peak
    rows_out = row_peak * inv_rms / 7.0

    arrived(peak_c, PEAK_C)
    top = jnp.maximum(peak[...], peak_c[...])
    peak_d[0] = top
    each(lambda k: start(peak_d.at[0], peak_d.at[k], PEAK_D, chip_dev(k)))

    for k in range(8):
        into = twin(jnp.broadcast_to(rows_in[k : k + 1, :], (128, 128)).T)
        outof = twin(jnp.broadcast_to(rows_out[k : k + 1, :], (128, 128)).T)
        h = res[128 * k : 128 * k + 128, :].astype(F32)
        act[128 * k : 128 * k + 128, :] = (outof * soft(into * h)).astype(BF16)

    arrived(peak_d.at[pl.ds(1, N - 1)], PEAK_D)
    for k in range(1, N):
        top = jnp.maximum(top, peak_d[k])
    column = jnp.broadcast_to(top[:1, :], (128, 128)).T[:32, :]
    scale = twin((column + 1e-06) / 7.0)
    w_all[me] = (scale * soft(q_mine / scale)).astype(BF16)
    spread(w_all.at[me], w_all.at[me], W_G, True)
    q_all[me] = q_mine.astype(BF16)
    spread(q_all.at[me], q_all.at[me], Q_G, True)
    scatter(u_send, u_recv, U_R, True)

    loads[4].wait()
    wanted = slot * 16 + lax.broadcasted_iota(jnp.int32, (16, 512), 0)
    one_hot = jnp.where(lax.broadcasted_iota(jnp.int32, (16, 512), 1) == wanted, 1.0, 0.0)
    target_mine = dot(one_hot.astype(BF16), target[...], NT)

    arrived(w_all.at[pl.ds(0, N - 1)], W_G)

    def quarter(ref, c, h):
        return ref[pl.ds(c * 8 + h * 4, 4)].reshape(128, 256)

    def weight_gram():
        arrived(u_recv, U_R)
        u_part[me] = total(u_send[me], u_recv)
        spread(u_part.at[me], u_part.at[me], U_G, True)

    out_mine = reduce_dp(
        lambda c, h: dot(quarter(w_all, c, h), act[...], NT),
        out_send, out_c, out_x, out_xr, out_y, out_yr, OUT, weight_gram,
    )
    og_all[slot] = (out_mine - target_mine).astype(BF16)
    gather_own(og_all, OG)

    def g_part(c):
        og = og_all[pl.ds(c * N, N)].reshape(256, 1024)
        g_send[pl.ds(c * 8, 8)] = dot(og, act[...]).astype(BF16).reshape(8, 32, 256)

    g_part(core)
    gather_other(og_all, OG)
    g_part(other)
    scatter(g_send, g_recv, G_R, True)
    arrived(u_part.at[pl.ds(0, N - 1)], U_G)
    u_all[slot] = jnp.concatenate(
        [
            jnp.concatenate([u_part[8 * h + b] for b in range(4)], axis=1)
            for h in range(2)
        ],
        axis=0,
    ).astype(BF16)

    spread(u_all.at[slot], u_all.at[slot], UD_G, False)
    arrived(g_recv, G_R)
    g_all[me] = total(g_send[me], g_recv).astype(BF16)
    spread(g_all.at[me], g_all.at[me], G_G, True)
    s_full = st[...].T
    s_high = s_full.astype(BF16)
    s_low = (s_full - s_high.astype(F32)).astype(BF16)
    arrived(u_all.at[pl.ds(0, N - 1)], UD_G)
    u_half = u_all.at[pl.ds(core * N, N)]
    to_twin(u_half, u_half, UD_C)
    arrived(g_all.at[pl.ds(0, N - 1)], G_G)

    def gradient():
        g_full = g_all[...].reshape(512, 256)
        grad = dot(s_high, g_full) + dot(s_low, g_full)
        grad_out[...] = grad
        square = jnp.sum((grad * grad).reshape(64, 8, 256), axis=0)
        sq[...] = square[:, :128] + square[:, 128:]
        to_twin(sq, sq_c, SQ_C)

    v_mine = reduce_dp(
        lambda c, h: dot(quarter(g_all, c, h), rb[...], NT),
        v_send, v_c, v_x, v_xr, v_y, v_yr, V, gradient,
    )
    v_all[slot] = v_mine.astype(BF16)
    gather_own(v_all, VG)
    arrived(sq_c, SQ_C)
    sq_d[0] = sq[...] + sq_c[...]
    each(lambda k: start(sq_d.at[0], sq_d.at[k], SQ_D, chip_dev(k)))

    def p_part(c):
        vt = v_all[pl.ds(c * N, N)].reshape(256, 512)
        p_send[pl.ds(c * 8, 8)] = dot(vt, rb[...]).astype(BF16).reshape(8, 32, 256)

    p_part(core)
    gather_other(v_all, VG)

    vt = v_all[...].reshape(512, 512)
    v_mine = v_all[slot]
    for part, right in enumerate((vt, st[...].astype(BF16))):
        gram = dot(v_mine, right, NT)
        for h in range(2):
            for b in range(4):
                m_send[8 * h + 4 * part + b] = gram[
                    8 * h : 8 * h + 8, 128 * b : 128 * b + 128
                ]
    scatter(m_send, m_recv, M_R, True)
    p_part(other)
    scatter(p_send, p_recv, P_R, True)
    arrived(m_recv, M_R)
    m_part[me] = total(m_send[me], m_recv)
    spread(m_part.at[me], m_part.at[me], M_G, True)
    arrived(sq_d.at[pl.ds(1, N - 1)], SQ_D)
    square = sq_d[0]
    for k in range(1, N):
        square = square + sq_d[k]
    sq_s[0] = square
    each(lambda k: start(sq_s.at[0], sq_s.at[k], SQ_S, shard_dev(k)))
    arrived(p_recv, P_R)
    p_all[me] = total(p_send[me], p_recv).astype(BF16)
    spread(p_all.at[me], p_all.at[me], P_G, True)
    arrived(m_part.at[pl.ds(0, N - 1)], M_G)
    m_all[slot] = jnp.concatenate(
        [
            jnp.concatenate([m_part[8 * h + b] for b in range(8)], axis=1)
            for h in range(2)
        ],
        axis=0,
    ).astype(BF16)
    gather_own(m_all, MG)

    arrived(sq_s.at[pl.ds(1, N - 1)], SQ_S)
    for k in range(1, N):
        square = square + sq_s[k]
    square = jnp.sum(jnp.sum(square, axis=1, keepdims=True), axis=0, keepdims=True)
    step = 0.4 * math.sqrt(512) * lax.rsqrt(D * square + 1e-06)
    arrived(u_all.at[pl.ds(0, N)], UD_C)
    arrived(q_all.at[pl.ds(0, N - 1)], Q_G)
    q_full = q_all[...].reshape(512, 256)
    uu = u_all[...].reshape(512, 512)

    arrived(p_all.at[pl.ds(0, N - 1)], P_G)
    p_full = p_all[...].reshape(512, 256)
    gather_other(m_all, MG)
    m_full = m_all[...].reshape(512, 1024)
    vv, vu = m_full[:, :512], m_full[:, 512:]
    left = 2.0 * p_full.astype(F32) - step * (dot(vu, p_full) - dot(vv, q_full))
    right = 2.0 * q_full.astype(F32) - step * (dot(uu, p_full) - dot(vu, q_full, TN))
    applied = dot(s_high, left.astype(BF16)) - dot(vt, right.astype(BF16), TN)
    next_out[...] = rot[...] - 0.5 * step * applied

    for ref, which in sent:
        pltpu.make_async_copy(ref, ref, sends.at[which]).wait()


def shards(residual, norm_gain, value_weight, rotation, target):
    vmem = pl.BlockSpec(memory_space=pltpu.VMEM)
    scratch = [
        ((1024, 256), BF16), ((1, 512), F32), ((512, 512), BF16), ((512, 256), F32), ((1024, 512), BF16),
        ((512, 512), F32),
        ((512, 256), BF16),
        ((1024, 256), BF16),
        ((16, 128), F32), ((16, 128), F32), ((N, 16, 128), F32),
        ((N, 48, 256), BF16), ((N - 1, 48, 256), BF16), ((N, 32, 256), BF16), ((N, 32, 256), BF16),
        ((8, 128), F32), ((8, 128), F32), ((N, 8, 128), F32),
        ((2, 128, 1024), BF16), ((2, 128, 1024), BF16), ((8, 16, 1024), BF16), ((8, 16, 1024), BF16),
        ((8, 16, 1024), F32), ((7, 16, 1024), BF16),
        ((2 * N, 16, 1024), BF16),
        ((N, 32, 256), BF16), ((N - 1, 32, 256), BF16), ((N, 32, 256), BF16),
        ((2, 128, 512), BF16), ((2, 128, 512), BF16), ((8, 16, 512), BF16), ((8, 16, 512), BF16),
        ((8, 16, 512), F32), ((7, 16, 512), BF16),
        ((2 * N, 16, 512), BF16),
        ((N, 32, 256), BF16), ((N - 1, 32, 256), BF16), ((N, 32, 256), BF16),
        ((8, 128), F32), ((8, 128), F32), ((N, 8, 128), F32), ((N, 8, 128), F32),
        ((N, 8, 128), F32), ((N - 1, 8, 128), F32), ((N, 8, 128), F32), ((2 * N, 16, 512), BF16),
        ((N, 8, 128), F32), ((N - 1, 8, 128), F32), ((N, 8, 128), F32), ((2 * N, 16, 1024), BF16),
    ]
    buffers = [pltpu.VMEM(shape, kind) for shape, kind in scratch]
    return pl.pallas_call(
        kernel,
        out_shape=[jax.ShapeDtypeStruct((512, 256), F32)] * 2,
        in_specs=[pl.BlockSpec(memory_space=pltpu.HBM)] * 5,
        out_specs=[vmem] * 2,
        scratch_shapes=buffers[:5] + [pltpu.SemaphoreType.DMA((5,))] + buffers[5:]
        + [pltpu.SemaphoreType.DMA((COUNT,)), pltpu.SemaphoreType.DMA((COUNT,))],
        compiler_params=pltpu.CompilerParams(
            collective_id=0, has_side_effects=True, vmem_limit_bytes=48 * 2**20
        ),
        cost_estimate=pl.CostEstimate(
            flops=2 * 10**9, bytes_accessed=4 * 2**20, transcendentals=0
        ),
    )(residual, norm_gain.reshape(1, -1), value_weight, rotation, target)


def solution(mesh):
    in_specs = (P("shard", "dp"), P("shard"), P("shard", None), P("shard", "dp"), P("shard", None))
    out_specs = (P("shard", "dp"), P("shard", "dp"))
    return jax.shard_map(
        lambda *a: tuple(shards(*a)), mesh=mesh, in_specs=in_specs, out_specs=out_specs, check_vma=False
    )
```

```python
import math

import jax
import jax.numpy as jnp
from jax import lax
from jax.experimental import pallas as pl
from jax.experimental.pallas import tpu as pltpu
from jax.sharding import PartitionSpec as P

D = 8192
LIMIT = 63 * 2**20
N = 16
MESH = pl.DeviceIdType.MESH
F32 = jnp.float32
BF16 = jnp.bfloat16
HIGHEST = lax.Precision.HIGHEST

SINE = (
    0.9999999944722865,
    -6.579735439437006,
    12.987842893121643,
    -12.207428862935943,
    6.687066146603468,
    -2.366367060643953,
    0.5091905906829214,
)

NN = (((1,), (0,)), ((), ()))
NT = (((1,), (1,)), ((), ()))
TN = (((0,), (0,)), ((), ()))


def dot(a, b, dims=NN, precision=None):
    return lax.dot_general(a, b, dims, precision=precision, preferred_element_type=F32)


def soft(v):
    r = v - jnp.floor(v + 0.5)
    s = r * r
    p = jnp.full_like(s, SINE[-1])
    for c in SINE[-2::-1]:
        p = p * s + c
    return v - r * p


def twin(a):
    return jnp.concatenate([a, a], axis=1)


(
    STAT_C, STAT_D, Q_R, PEAK_C, PEAK_D, W_G, Q_G,
    SQ_C, SQ_D, SQ_S, U_R, U_G, UD_G, UD_C, M_R, M_G, N_R, N_G, ND_G, ND_C,
) = range(20)
OUT, V = 20, 31
OG, VG, MG = 42, 53, 64
G_R, G_G, P_R, P_G = 75, 77, 79, 81
COUNT = 83
FAR = (4, 3, 5, 2, 6, 1, 7)
NEAR = FAR[::-1]


def kernel(
    res_in, gain_in, weight_in, rot_in, target_in, grad_to, next_to,
    res, gain, weight, rot, target, grad_out, next_out, local,
    st, rb, act, stat, stat_c, stat_d,
    q_send, q_recv, q_all, w_all,
    peak, peak_c, peak_d,
    out_send, out_c, out_x, out_xr, out_y, out_yr, og_all,
    g_send, g_recv, g_all,
    v_send, v_c, v_x, v_xr, v_y, v_yr, v_all,
    p_send, p_recv, p_all,
    sq, sq_c, sq_d, sq_s,
    u_send, u_recv, u_part, u_all,
    m_send, m_recv, m_part, m_all,
    n_send, n_recv, n_part, n_all,
    sends, recvs,
):
    dp, me = lax.axis_index("dp"), lax.axis_index("shard")
    chip, core = lax.div(dp, 2), lax.rem(dp, 2)
    y, xl = lax.div(chip, 2), lax.rem(chip, 2)
    other, xo = 1 - core, 1 - xl
    slot = core * N + xl * 8 + y
    twin_id = (chip * 2 + other, me)
    x_id = ((y * 2 + xo) * 2 + core, me)

    loads = []
    for n, (src, dst) in enumerate(
        ((weight_in, weight), (rot_in, rot), (gain_in, gain), (res_in, res), (target_in, target))
    ):
        rows = src.shape[0]
        cuts = 4 if rows > 1 else 1
        for c in range(cuts):
            part = pl.ds(c * (rows // cuts), rows // cuts)
            pltpu.make_async_copy(src.at[part], dst.at[part], local.at[n]).start()
        loads.append(pltpu.make_async_copy(src, dst, local.at[n]))

    def y_id(k):
        return ((lax.rem(y + k, 8) * 2 + xl) * 2 + core, me)

    def shard_id(k):
        return lax.rem(me + k, N)

    def chip_id(k):
        return lax.rem(chip + k, N)

    def shard_dev(k):
        return (dp, shard_id(k))

    def chip_dev(k):
        return (chip_id(k) * 2 + core, me)

    def each(body):
        def step(k, _):
            body(k)
            return 0

        lax.fori_loop(1, N, step, 0)

    def start(src, dst, which, device):
        pltpu.make_async_remote_copy(
            src_ref=src, dst_ref=dst, send_sem=sends.at[which], recv_sem=recvs.at[which],
            device_id=device, device_id_type=MESH,
        ).start()

    sent = []

    def arrived(ref, which):
        pltpu.make_async_copy(ref, ref, recvs.at[which]).wait()
        sent.append((ref, which))

    def scatter(src, dst, which):
        each(lambda k: start(src.at[shard_id(k)], dst.at[k - 1], which, shard_dev(k)))

    def spread(ref, which, device):
        each(lambda k: start(ref, ref, which, device(k)))

    def to_twin(src, dst, which):
        start(src, dst, which, twin_id)

    def reduce_dp(part, send, from_twin, x_send, x_recv, y_send, y_recv, base, between, ready=None):
        width = send.shape[2]
        if ready is not None:
            own = [part(core, xo), part(core, xl)]
            ready()
        for n, h in enumerate((xo, xl)):
            send[n] = part(other, h).astype(BF16)
            to_twin(send.at[n], from_twin.at[n], base + n)
        if ready is None:
            own = [part(core, xo), part(core, xl)]
        arrived(from_twin.at[0], base)
        both = own[0] + from_twin[0].astype(F32)
        x_send[...] = both.astype(BF16).reshape(8, 16, width)
        for k in FAR + (0,):
            start(x_send.at[lax.rem(y + k, 8)], x_recv.at[k], base + 2 + k, x_id)
        arrived(from_twin.at[1], base + 1)
        both = own[1] + from_twin[1].astype(F32)
        y_send[...] = both.reshape(8, 16, width)
        for k in FAR:
            arrived(x_recv.at[k], base + 2 + k)
            x_recv[k] = (y_send[lax.rem(y + k, 8)] + x_recv[k].astype(F32)).astype(BF16)
            start(x_recv.at[k], y_recv.at[k - 1], base + 10, y_id(k))
        between()
        arrived(x_recv.at[0], base + 2)
        acc = y_send[y] + x_recv[0].astype(F32)
        arrived(y_recv, base + 10)
        for k in range(7):
            acc = acc + y_recv[k].astype(F32)
        return acc

    def gather_own(ref, base, between=None):
        own = ref.at[slot]
        for k in FAR:
            start(own, own, base + k, y_id(k))
        start(own, own, base + 8, x_id)
        if between is not None:
            between()
        for k in NEAR:
            block = ref.at[core * N + xl * 8 + lax.rem(y + 8 - k, 8)]
            arrived(block, base + k)
            start(block, block, base + 8, x_id)
        near = ref.at[pl.ds(core * N + xl * 8, 8)]
        to_twin(near, near, base + 9)
        far = ref.at[pl.ds(core * N + xo * 8, 8)]
        arrived(far, base + 8)
        to_twin(far, far, base + 10)

    def gather_other(ref, base):
        arrived(ref.at[pl.ds(0, 8)], base + 9)
        arrived(ref.at[pl.ds(0, 8)], base + 10)

    def total(own, recv):
        acc = own.astype(F32)
        for k in range(N - 1):
            acc = acc + recv[k].astype(F32)
        return acc

    barrier = pltpu.get_barrier_semaphore()
    pl.semaphore_signal(barrier, inc=1, device_id=twin_id, device_id_type=MESH)

    def greet(k):
        pl.semaphore_signal(barrier, inc=1, device_id=shard_dev(k), device_id_type=MESH)
        pl.semaphore_signal(barrier, inc=1, device_id=chip_dev(k), device_id_type=MESH)

    each(greet)

    loads[0].wait()
    loads[2].wait()
    st[...] = weight[...].astype(F32).T * gain[...] * (1.0 / math.sqrt(D))
    loads[1].wait()
    q = dot(st[...], rot[...], NN, HIGHEST).reshape(2, N, 16, 256)
    high = q.astype(BF16)
    q_send[:, :16] = high[0]
    q_send[:, 16:32] = high[1]
    high = high.astype(F32)
    rest = jnp.floor((q - high) * (15 * 256.0) / (jnp.abs(high) + 1e-30) + 0.5)
    rest = jnp.clip(rest, -7.0, 7.0)
    q_send[:, 32:] = (rest[0] * 16.0 + rest[1]).astype(BF16)
    pl.semaphore_wait(barrier, 2 * N - 1)
    scatter(q_send, q_recv, Q_R)

    loads[3].wait()
    for k in range(8):
        h = res[128 * k : 128 * k + 128, :].astype(F32)
        a, b = h[:, :128], h[:, 128:]
        stat[k : k + 1, :] = jnp.sum((a * a + b * b).T, axis=0, keepdims=True)
        stat[8 + k : 9 + k, :] = jnp.max(
            jnp.maximum(jnp.abs(a), jnp.abs(b)).T, axis=0, keepdims=True
        )
    to_twin(stat, stat_c, STAT_C)
    rb[...] = rot[...].astype(BF16)
    stb = st[...].astype(BF16)
    mine = st[pl.ds(pl.multiple_of(slot * 16, 16), 16), :].astype(BF16)
    u_gram = dot(mine, stb, NT)
    for h in range(2):
        for b in range(4):
            block = u_gram[8 * h : 8 * h + 8, 128 * b : 128 * b + 128]
            u_send[8 * h + b] = block
            u_send[8 * h + 4 + b] = block
    arrived(stat_c, STAT_C)

    def combine(a, b):
        return jnp.concatenate([a[:8] + b[:8], jnp.maximum(a[8:], b[8:])], axis=0)

    both = combine(stat[...], stat_c[...])
    stat_d[0] = both
    each(lambda k: start(stat_d.at[0], stat_d.at[k], STAT_D, chip_dev(k)))

    arrived(q_recv, Q_R)

    def decode(a):
        high, rest = a[:32].astype(F32), a[32:].astype(F32)
        upper = jnp.floor(rest * 0.0625 + 0.5)
        rest = jnp.concatenate([upper, rest - 16.0 * upper], axis=0)
        return high + rest * (jnp.abs(high) * (1.0 / (15 * 256)))

    q_mine = decode(q_send[me])
    for k in range(N - 1):
        q_mine = q_mine + decode(q_recv[k])
    top = jnp.maximum(jnp.abs(q_mine[:, :128]), jnp.abs(q_mine[:, 128:]))
    top = jnp.max(jnp.concatenate([top] * 4, axis=0).T, axis=0, keepdims=True)
    peak[...] = jnp.broadcast_to(top, (8, 128))
    to_twin(peak, peak_c, PEAK_C)

    arrived(stat_d.at[pl.ds(1, N - 1)], STAT_D)
    for k in range(1, N):
        both = combine(both, stat_d[k])
    row_peak = both[8:] + 1e-06
    inv_rms = lax.rsqrt(both[:8] / D + 1e-05)
    rows_in = 7.0 / row_peak
    rows_out = row_peak * inv_rms / 7.0

    arrived(peak_c, PEAK_C)
    top = jnp.maximum(peak[...], peak_c[...])
    peak_d[0] = top
    each(lambda k: start(peak_d.at[0], peak_d.at[k], PEAK_D, chip_dev(k)))

    for k in range(8):
        into = twin(jnp.broadcast_to(rows_in[k : k + 1, :], (128, 128)).T)
        outof = twin(jnp.broadcast_to(rows_out[k : k + 1, :], (128, 128)).T)
        h = res[128 * k : 128 * k + 128, :].astype(F32)
        act[128 * k : 128 * k + 128, :] = (outof * soft(into * h)).astype(BF16)

    arrived(peak_d.at[pl.ds(1, N - 1)], PEAK_D)
    for k in range(1, N):
        top = jnp.maximum(top, peak_d[k])
    column = jnp.broadcast_to(top[:1, :], (128, 128)).T[:32, :]
    scale = twin((column + 1e-06) / 7.0)
    w_all[:, me] = (scale * soft(q_mine / scale)).astype(BF16).reshape(2, 16, 256)
    spread(w_all.at[:, me], W_G, shard_dev)
    q_all[:, me] = q_mine.astype(BF16).reshape(2, 16, 256)
    spread(q_all.at[:, me], Q_G, shard_dev)
    scatter(u_send, u_recv, U_R)

    loads[4].wait()
    wanted = slot * 16 + lax.broadcasted_iota(jnp.int32, (16, 512), 0)
    one_hot = jnp.where(lax.broadcasted_iota(jnp.int32, (16, 512), 1) == wanted, 1.0, 0.0)
    target_mine = dot(one_hot.astype(BF16), target[...], NT)

    arrived(w_all.at[:, pl.ds(0, N - 1)], W_G)

    def quarter(ref, c, h):
        return ref[c, pl.ds(h * 8, 8)].reshape(128, 256)

    def weight_gram():
        arrived(u_recv, U_R)
        u_part[me] = total(u_send[me], u_recv)
        spread(u_part.at[me], U_G, shard_dev)

    out_mine = reduce_dp(
        lambda c, h: dot(quarter(w_all, c, h), act[...], NT),
        out_send, out_c, out_x, out_xr, out_y, out_yr, OUT, weight_gram,
    )
    og_all[slot] = (out_mine - target_mine).astype(BF16)
    gather_own(og_all, OG)

    def send_half(src, dst, which, c):
        each(lambda k: start(src.at[c, shard_id(k)], dst.at[c, k - 1], which, shard_dev(k)))

    def share_half(src, recv, ref, which, after, c):
        arrived(recv.at[c], which)
        acc = src[c, me].astype(F32)
        for k in range(N - 1):
            acc = acc + recv[c, k].astype(F32)
        ref[c, me] = acc.astype(BF16)
        spread(ref.at[c, me], after, shard_dev)

    def g_part(c):
        og = og_all[pl.ds(c * N, N)].reshape(256, 1024)
        g_send[c] = dot(og, act[...]).astype(BF16).reshape(N, 16, 256)

    g_part(core)
    send_half(g_send, g_recv, G_R, core)
    gather_other(og_all, OG)
    g_part(other)
    send_half(g_send, g_recv, G_R + 1, other)

    def assemble(part, count):
        rows = [
            jnp.concatenate([part[8 * h + b] for b in range(count)], axis=1)
            for h in range(2)
        ]
        return jnp.concatenate(rows, axis=0).astype(BF16)

    def to_twin_half(ref, which):
        half = ref.at[pl.ds(core * N, N)]
        to_twin(half, half, which)

    arrived(u_part.at[pl.ds(0, N - 1)], U_G)
    u_all[slot] = assemble(u_part, 4)
    spread(u_all.at[slot], UD_G, chip_dev)
    share_half(g_send, g_recv, g_all, G_R, G_G, core)
    share_half(g_send, g_recv, g_all, G_R + 1, G_G + 1, other)
    s_full = st[...].T
    s_high = s_full.astype(BF16)
    s_low = (s_full - s_high.astype(F32)).astype(BF16)
    arrived(u_all.at[pl.ds(0, N - 1)], UD_G)
    to_twin_half(u_all, UD_C)

    def gradient():
        g_full = g_all[...].reshape(512, 256)
        grad = dot(s_high, g_full) + dot(s_low, g_full)
        grad_out[...] = grad
        pltpu.make_async_copy(grad_out, grad_to, local.at[5]).start()
        square = jnp.sum((grad * grad).reshape(64, 8, 256), axis=0)
        sq[...] = square[:, :128] + square[:, 128:]
        to_twin(sq, sq_c, SQ_C)

    arrived(g_all.at[0, pl.ds(0, N - 1)], G_G)
    v_mine = reduce_dp(
        lambda c, h: dot(quarter(g_all, c, h), rb[...], NT),
        v_send, v_c, v_x, v_xr, v_y, v_yr, V, gradient,
        lambda: arrived(g_all.at[0, pl.ds(0, N - 1)], G_G + 1),
    ).astype(BF16)
    v_all[slot] = v_mine

    def blocks(ref, gram):
        for h in range(2):
            for b in range(8):
                block = 128 * (b % 4)
                ref[8 * h + b] = gram[8 * h : 8 * h + 8, block : block + 128]

    def gram_with_weight():
        blocks(n_send, dot(v_mine, stb, NT))
        scatter(n_send, n_recv, N_R)

    gather_own(v_all, VG, gram_with_weight)
    arrived(sq_c, SQ_C)
    sq_d[0] = sq[...] + sq_c[...]
    each(lambda k: start(sq_d.at[0], sq_d.at[k], SQ_D, chip_dev(k)))

    def p_part(c):
        vt = v_all[pl.ds(c * N, N)].reshape(256, 512)
        p_send[c] = dot(vt, rb[...]).astype(BF16).reshape(N, 16, 256)

    arrived(n_recv, N_R)
    n_part[me] = total(n_send[me], n_recv)
    spread(n_part.at[me], N_G, shard_dev)
    p_part(core)
    send_half(p_send, p_recv, P_R, core)
    gather_other(v_all, VG)
    vt = v_all[...].reshape(512, 512)
    blocks(m_send, dot(v_mine, vt, NT))
    scatter(m_send, m_recv, M_R)
    p_part(other)
    send_half(p_send, p_recv, P_R + 1, other)

    arrived(n_part.at[pl.ds(0, N - 1)], N_G)
    n_all[slot] = assemble(n_part, 4)
    spread(n_all.at[slot], ND_G, chip_dev)
    arrived(m_recv, M_R)
    m_part[me] = total(m_send[me], m_recv)
    spread(m_part.at[me], M_G, shard_dev)
    arrived(sq_d.at[pl.ds(1, N - 1)], SQ_D)
    square = sq_d[0]
    for k in range(1, N):
        square = square + sq_d[k]
    sq_s[0] = square
    each(lambda k: start(sq_s.at[0], sq_s.at[k], SQ_S, shard_dev(k)))
    share_half(p_send, p_recv, p_all, P_R, P_G, core)
    v_full = vt.astype(F32).T.astype(BF16)
    arrived(m_part.at[pl.ds(0, N - 1)], M_G)
    m_all[slot] = assemble(m_part, 4)
    share_half(p_send, p_recv, p_all, P_R + 1, P_G + 1, other)
    gather_own(m_all, MG)

    arrived(n_all.at[pl.ds(0, N - 1)], ND_G)
    to_twin_half(n_all, ND_C)
    arrived(sq_s.at[pl.ds(1, N - 1)], SQ_S)
    for k in range(1, N):
        square = square + sq_s[k]
    square = jnp.sum(jnp.sum(square, axis=1, keepdims=True), axis=0, keepdims=True)
    step = 0.4 * math.sqrt(512) * lax.rsqrt(D * square + 1e-06)
    arrived(u_all.at[pl.ds(0, N)], UD_C)
    arrived(q_all.at[:, pl.ds(0, N - 1)], Q_G)
    q_full = q_all[...].reshape(512, 256)
    uu = u_all[...].reshape(512, 512)
    gather_other(m_all, MG)
    vv = m_all[...].reshape(512, 512)
    arrived(n_all.at[pl.ds(0, N)], ND_C)
    vu = n_all[...].reshape(512, 512)
    left = step * dot(vv, q_full)
    right = 2.0 * q_full.astype(F32) + step * dot(vu, q_full, TN)
    arrived(p_all.at[0, pl.ds(0, N - 1)], P_G)
    arrived(p_all.at[0, pl.ds(0, N - 1)], P_G + 1)
    p_full = p_all[...].reshape(512, 256)
    left = left + 2.0 * p_full.astype(F32) - step * dot(vu, p_full)
    right = right - step * dot(uu, p_full)
    left, right = left.astype(BF16), right.astype(BF16)
    for c in range(4):
        rows = slice(128 * c, 128 * c + 128)
        applied = dot(s_high[rows], left) - dot(v_full[rows], right)
        next_out[rows] = rot[rows] - 0.5 * step * applied
        pltpu.make_async_copy(next_out.at[rows], next_to.at[rows], local.at[6]).start()

    for ref, which in sent:
        pltpu.make_async_copy(ref, ref, sends.at[which]).wait()
    pltpu.make_async_copy(grad_out, grad_to, local.at[5]).wait()
    pltpu.make_async_copy(next_out, next_to, local.at[6]).wait()


def shards(residual, norm_gain, value_weight, rotation, target):
    hbm = pl.BlockSpec(memory_space=pltpu.HBM)
    scratch = [
        ((1024, 256), BF16), ((1, 512), F32), ((512, 512), BF16), ((512, 256), F32), ((1024, 512), BF16),
        ((512, 256), F32), ((512, 256), F32),
        ((512, 512), F32),
        ((512, 256), BF16),
        ((1024, 256), BF16),
        ((16, 128), F32), ((16, 128), F32), ((N, 16, 128), F32),
        ((N, 48, 256), BF16), ((N - 1, 48, 256), BF16), ((2, N, 16, 256), BF16), ((2, N, 16, 256), BF16),
        ((8, 128), F32), ((8, 128), F32), ((N, 8, 128), F32),
        ((2, 128, 1024), BF16), ((2, 128, 1024), BF16), ((8, 16, 1024), BF16), ((8, 16, 1024), BF16),
        ((8, 16, 1024), F32), ((7, 16, 1024), BF16),
        ((2 * N, 16, 1024), BF16),
        ((2, N, 16, 256), BF16), ((2, N - 1, 16, 256), BF16), ((2, N, 16, 256), BF16),
        ((2, 128, 512), BF16), ((2, 128, 512), BF16), ((8, 16, 512), BF16), ((8, 16, 512), BF16),
        ((8, 16, 512), F32), ((7, 16, 512), BF16),
        ((2 * N, 16, 512), BF16),
        ((2, N, 16, 256), BF16), ((2, N - 1, 16, 256), BF16), ((2, N, 16, 256), BF16),
        ((8, 128), F32), ((8, 128), F32), ((N, 8, 128), F32), ((N, 8, 128), F32),
        ((N, 8, 128), F32), ((N - 1, 8, 128), F32), ((N, 8, 128), F32), ((2 * N, 16, 512), BF16),
        ((N, 8, 128), F32), ((N - 1, 8, 128), F32), ((N, 8, 128), F32), ((2 * N, 16, 512), BF16),
        ((N, 8, 128), F32), ((N - 1, 8, 128), F32), ((N, 8, 128), F32), ((2 * N, 16, 512), BF16),
    ]
    buffers = [pltpu.VMEM(shape, kind) for shape, kind in scratch]
    return pl.pallas_call(
        kernel,
        out_shape=[jax.ShapeDtypeStruct((512, 256), F32)] * 2,
        in_specs=[hbm] * 5,
        out_specs=[hbm] * 2,
        scratch_shapes=buffers[:7] + [pltpu.SemaphoreType.DMA((7,))] + buffers[7:]
        + [pltpu.SemaphoreType.DMA((COUNT,)), pltpu.SemaphoreType.DMA((COUNT,))],
        compiler_params=pltpu.CompilerParams(
            collective_id=0, has_side_effects=True, vmem_limit_bytes=LIMIT
        ),
        cost_estimate=pl.CostEstimate(
            flops=2 * 10**9, bytes_accessed=4 * 2**20, transcendentals=0
        ),
    )(residual, norm_gain.reshape(1, -1), value_weight, rotation, target)


def solution(mesh):
    in_specs = (P("shard", "dp"), P("shard"), P("shard", None), P("shard", "dp"), P("shard", None))
    out_specs = (P("shard", "dp"), P("shard", "dp"))
    return jax.shard_map(
        lambda *a: tuple(shards(*a)), mesh=mesh, in_specs=in_specs, out_specs=out_specs, check_vma=False
    )
```

```python
import math

import jax
import jax.numpy as jnp
from jax import lax
from jax.experimental import pallas as pl
from jax.experimental.pallas import tpu as pltpu
from jax.sharding import PartitionSpec as P

D = 8192
LIMIT = 63 * 2**20
N = 16
MESH = pl.DeviceIdType.MESH
F32 = jnp.float32
BF16 = jnp.bfloat16

SINE = (
    0.9999999944722865,
    -6.579735439437006,
    12.987842893121643,
    -12.207428862935943,
    6.687066146603468,
    -2.366367060643953,
    0.5091905906829214,
)

NN = (((1,), (0,)), ((), ()))
NT = (((1,), (1,)), ((), ()))
TN = (((0,), (0,)), ((), ()))


def dot(a, b, dims=NN):
    return lax.dot_general(a, b, dims, preferred_element_type=F32)


def soft(v):
    r = v - jnp.floor(v + 0.5)
    s = r * r
    p = jnp.full_like(s, SINE[-1])
    for c in SINE[-2::-1]:
        p = p * s + c
    return v - r * p


def twin(a):
    return jnp.concatenate([a, a], axis=1)


(
    STAT_C, STAT_D, Q_R, PEAK_C, PEAK_D, W_G, Q_G,
    SQ_C, SQ_D, SQ_S, U_R, U_G, UD_G, UD_C, M_R, M_G, N_R, N_G, W_H,
) = range(19)
OUT, V = 20, 31
OG, VG, MG = 42, 53, 64
G_R, G_G, P_R, P_G = 75, 77, 79, 81
NG = 83
COUNT = 94
FAR = (4, 3, 5, 2, 6, 1, 7)
NEAR = FAR[::-1]


def kernel(
    res_in, gain_in, weight_in, rot_in, target_in, grad_to, next_to,
    res, gain, weight, rot, target, grad_out, next_out, local,
    gains, wt, rb, act, stat, stat_c, stat_d,
    q_send, q_recv, q_all, w_all,
    peak, peak_c, peak_d,
    out_send, out_c, out_x, out_xr, out_y, out_yr, og_all,
    g_send, g_recv, g_all,
    v_send, v_c, v_x, v_xr, v_y, v_yr, v_all,
    p_send, p_recv, p_all,
    sq, sq_c, sq_d, sq_s,
    u_send, u_recv, u_part, u_all,
    m_send, m_recv, m_part, m_all,
    n_send, n_recv, n_part, n_all,
    sends, recvs,
):
    dp, me = lax.axis_index("dp"), lax.axis_index("shard")
    chip, core = lax.div(dp, 2), lax.rem(dp, 2)
    y, xl = lax.div(chip, 2), lax.rem(chip, 2)
    other, xo = 1 - core, 1 - xl
    slot = core * N + xl * 8 + y
    twin_id = (chip * 2 + other, me)
    x_id = ((y * 2 + xo) * 2 + core, me)

    loads = []
    for n, (src, dst) in enumerate(
        ((weight_in, weight), (rot_in, rot), (gain_in, gain), (res_in, res), (target_in, target))
    ):
        rows = src.shape[0]
        cuts = 4 if rows > 1 else 1
        for c in range(cuts):
            part = pl.ds(c * (rows // cuts), rows // cuts)
            pltpu.make_async_copy(src.at[part], dst.at[part], local.at[n]).start()
        loads.append(pltpu.make_async_copy(src, dst, local.at[n]))

    def y_id(k):
        return ((lax.rem(y + k, 8) * 2 + xl) * 2 + core, me)

    def shard_id(k):
        return lax.rem(me + k, N)

    def chip_id(k):
        return lax.rem(chip + k, N)

    def shard_dev(k):
        return (dp, shard_id(k))

    def chip_dev(k):
        return (chip_id(k) * 2 + core, me)

    def each(body):
        def step(k, _):
            body(k)
            return 0

        lax.fori_loop(1, N, step, 0)

    def start(src, dst, which, device):
        pltpu.make_async_remote_copy(
            src_ref=src, dst_ref=dst, send_sem=sends.at[which], recv_sem=recvs.at[which],
            device_id=device, device_id_type=MESH,
        ).start()

    sent = []

    def arrived(ref, which):
        pltpu.make_async_copy(ref, ref, recvs.at[which]).wait()
        sent.append((ref, which))

    def scatter(src, dst, which):
        each(lambda k: start(src.at[shard_id(k)], dst.at[k - 1], which, shard_dev(k)))

    def spread(ref, which, device):
        each(lambda k: start(ref, ref, which, device(k)))

    def to_twin(src, dst, which):
        start(src, dst, which, twin_id)

    def reduce_dp(part, send, from_twin, x_send, x_recv, y_send, y_recv, base, between, ready, own_first):
        width = send.shape[2]
        if own_first:
            own = [part(core, xo), part(core, xl)]
            ready()
        for n, h in enumerate((xo, xl)):
            send[n] = part(other, h).astype(BF16)
            to_twin(send.at[n], from_twin.at[n], base + n)
        if not own_first:
            ready()
            own = [part(core, xo), part(core, xl)]
        arrived(from_twin.at[0], base)
        both = own[0] + from_twin[0].astype(F32)
        x_send[...] = both.astype(BF16).reshape(8, 16, width)
        for k in FAR + (0,):
            start(x_send.at[lax.rem(y + k, 8)], x_recv.at[k], base + 2 + k, x_id)
        arrived(from_twin.at[1], base + 1)
        both = own[1] + from_twin[1].astype(F32)
        y_send[...] = both.reshape(8, 16, width)
        for k in FAR:
            arrived(x_recv.at[k], base + 2 + k)
            x_recv[k] = (y_send[lax.rem(y + k, 8)] + x_recv[k].astype(F32)).astype(BF16)
            start(x_recv.at[k], y_recv.at[k - 1], base + 10, y_id(k))
        between()
        arrived(x_recv.at[0], base + 2)
        acc = y_send[y] + x_recv[0].astype(F32)
        arrived(y_recv, base + 10)
        for k in range(7):
            acc = acc + y_recv[k].astype(F32)
        return acc

    def gather_y(ref, base):
        own = ref.at[slot]
        for k in FAR:
            start(own, own, base + k, y_id(k))
        start(own, own, base + 8, x_id)

    def gather_x(ref, base):
        for k in NEAR:
            block = ref.at[core * N + xl * 8 + lax.rem(y + 8 - k, 8)]
            arrived(block, base + k)
            start(block, block, base + 8, x_id)

    def gather_core(ref, base):
        near = ref.at[pl.ds(core * N + xl * 8, 8)]
        to_twin(near, near, base + 9)
        far = ref.at[pl.ds(core * N + xo * 8, 8)]
        arrived(far, base + 8)
        to_twin(far, far, base + 10)

    def gather_other(ref, base):
        arrived(ref.at[pl.ds(0, 8)], base + 9)
        arrived(ref.at[pl.ds(0, 8)], base + 10)

    def total(own, recv):
        acc = own.astype(F32)
        for k in range(N - 1):
            acc = acc + recv[k].astype(F32)
        return acc

    barrier = pltpu.get_barrier_semaphore()
    pl.semaphore_signal(barrier, inc=1, device_id=twin_id, device_id_type=MESH)

    def greet(k):
        pl.semaphore_signal(barrier, inc=1, device_id=shard_dev(k), device_id_type=MESH)
        pl.semaphore_signal(barrier, inc=1, device_id=chip_dev(k), device_id_type=MESH)

    each(greet)

    loads[0].wait()
    loads[2].wait()
    wt[...] = weight[...].astype(F32).T.astype(BF16)
    norm = gain[...] * (1.0 / math.sqrt(D))
    for c in range(4):
        rows = slice(128 * c, 128 * c + 128)
        gains[rows] = twin(jnp.broadcast_to(norm[:, rows], (128, 128)).T)
    loads[1].wait()
    scaled = rot[...] * gains[...]
    first = scaled.astype(BF16)
    second = (scaled - first.astype(F32)).astype(BF16)
    q = (dot(wt[...], first) + dot(wt[...], second)).reshape(2, N, 16, 256)
    high = q.astype(BF16)
    q_send[:, :16] = high[0]
    q_send[:, 16:32] = high[1]
    high = high.astype(F32)
    rest = jnp.floor((q - high) * (15 * 256.0) / (jnp.abs(high) + 1e-30) + 0.5)
    rest = jnp.clip(rest, -7.0, 7.0)
    q_send[:, 32:] = (rest[0] * 16.0 + rest[1]).astype(BF16)
    pl.semaphore_wait(barrier, 2 * N - 1)
    scatter(q_send, q_recv, Q_R)

    loads[3].wait()
    for k in range(8):
        h = res[128 * k : 128 * k + 128, :].astype(F32)
        a, b = h[:, :128], h[:, 128:]
        stat[k : k + 1, :] = jnp.sum((a * a + b * b).T, axis=0, keepdims=True)
        stat[8 + k : 9 + k, :] = jnp.max(
            jnp.maximum(jnp.abs(a), jnp.abs(b)).T, axis=0, keepdims=True
        )
    to_twin(stat, stat_c, STAT_C)
    rb[...] = rot[...].astype(BF16)
    stb = (wt[...].astype(F32) * norm).astype(BF16)
    mine = wt[pl.ds(pl.multiple_of(slot * 16, 16), 16), :].astype(F32) * norm
    u_gram = dot(mine.astype(BF16), stb, NT)
    for h in range(2):
        for b in range(4):
            block = u_gram[8 * h : 8 * h + 8, 128 * b : 128 * b + 128]
            u_send[8 * h + b] = block
            u_send[8 * h + 4 + b] = block
    arrived(stat_c, STAT_C)

    def combine(a, b):
        return jnp.concatenate([a[:8] + b[:8], jnp.maximum(a[8:], b[8:])], axis=0)

    both = combine(stat[...], stat_c[...])
    stat_d[0] = both
    each(lambda k: start(stat_d.at[0], stat_d.at[k], STAT_D, chip_dev(k)))

    arrived(q_recv, Q_R)

    def decode(a):
        high, rest = a[:32].astype(F32), a[32:].astype(F32)
        upper = jnp.floor(rest * 0.0625 + 0.5)
        rest = jnp.concatenate([upper, rest - 16.0 * upper], axis=0)
        return high + rest * (jnp.abs(high) * (1.0 / (15 * 256)))

    q_mine = decode(q_send[me])
    for k in range(N - 1):
        q_mine = q_mine + decode(q_recv[k])
    top = jnp.maximum(jnp.abs(q_mine[:, :128]), jnp.abs(q_mine[:, 128:]))
    top = jnp.max(jnp.concatenate([top] * 4, axis=0).T, axis=0, keepdims=True)
    peak[...] = jnp.broadcast_to(top, (8, 128))
    to_twin(peak, peak_c, PEAK_C)

    arrived(stat_d.at[pl.ds(1, N - 1)], STAT_D)
    for k in range(1, N):
        both = combine(both, stat_d[k])
    row_peak = both[8:] + 1e-06
    inv_rms = lax.rsqrt(both[:8] / D + 1e-05)
    rows_in = 7.0 / row_peak
    rows_out = row_peak * inv_rms / 7.0

    arrived(peak_c, PEAK_C)
    top = jnp.maximum(peak[...], peak_c[...])
    peak_d[0] = top
    each(lambda k: start(peak_d.at[0], peak_d.at[k], PEAK_D, chip_dev(k)))

    for k in range(8):
        into = twin(jnp.broadcast_to(rows_in[k : k + 1, :], (128, 128)).T)
        outof = twin(jnp.broadcast_to(rows_out[k : k + 1, :], (128, 128)).T)
        h = res[128 * k : 128 * k + 128, :].astype(F32)
        act[128 * k : 128 * k + 128, :] = (outof * soft(into * h)).astype(BF16)

    arrived(peak_d.at[pl.ds(1, N - 1)], PEAK_D)
    for k in range(1, N):
        top = jnp.maximum(top, peak_d[k])
    column = jnp.broadcast_to(top[:1, :], (128, 128)).T[:32, :]
    scale = twin((column + 1e-06) / 7.0)
    w_all[:, me] = (scale * soft(q_mine / scale)).astype(BF16).reshape(2, 16, 256)
    spread(w_all.at[other, me], W_G, shard_dev)
    spread(w_all.at[core, me], W_H, shard_dev)
    q_all[:, me] = q_mine.astype(BF16).reshape(2, 16, 256)
    scatter(u_send, u_recv, U_R)

    loads[4].wait()
    wanted = slot * 16 + lax.broadcasted_iota(jnp.int32, (16, 512), 0)
    one_hot = jnp.where(lax.broadcasted_iota(jnp.int32, (16, 512), 1) == wanted, 1.0, 0.0)
    target_mine = dot(one_hot.astype(BF16), target[...], NT)

    arrived(w_all.at[0, pl.ds(0, N - 1)], W_G)

    def quarter(ref, c, h):
        return ref[c, pl.ds(h * 8, 8)].reshape(128, 256)

    def weight_gram():
        arrived(u_recv, U_R)
        u_part[me] = total(u_send[me], u_recv)
        spread(u_part.at[me], U_G, shard_dev)

    out_mine = reduce_dp(
        lambda c, h: dot(quarter(w_all, c, h), act[...], NT),
        out_send, out_c, out_x, out_xr, out_y, out_yr, OUT, weight_gram,
        lambda: arrived(w_all.at[0, pl.ds(0, N - 1)], W_H), False,
    )
    og_all[slot] = (out_mine - target_mine).astype(BF16)
    gather_y(og_all, OG)
    gather_x(og_all, OG)
    gather_core(og_all, OG)

    def send_half(src, dst, which, c):
        each(lambda k: start(src.at[c, shard_id(k)], dst.at[c, k - 1], which, shard_dev(k)))

    def share_half(src, recv, ref, which, after, c):
        arrived(recv.at[c], which)
        acc = src[c, me].astype(F32)
        for k in range(N - 1):
            acc = acc + recv[c, k].astype(F32)
        ref[c, me] = acc.astype(BF16)
        spread(ref.at[c, me], after, shard_dev)

    def g_part(c):
        og = og_all[pl.ds(c * N, N)].reshape(256, 1024)
        g_send[c] = dot(og, act[...]).astype(BF16).reshape(N, 16, 256)

    g_part(core)
    send_half(g_send, g_recv, G_R, core)
    gather_other(og_all, OG)
    g_part(other)
    send_half(g_send, g_recv, G_R + 1, other)

    def assemble(part, count):
        rows = [
            jnp.concatenate([part[8 * h + b] for b in range(count)], axis=1)
            for h in range(2)
        ]
        return jnp.concatenate(rows, axis=0).astype(BF16)

    def to_twin_half(ref, which):
        half = ref.at[pl.ds(core * N, N)]
        to_twin(half, half, which)

    arrived(u_part.at[pl.ds(0, N - 1)], U_G)
    u_all[slot] = assemble(u_part, 4)
    spread(u_all.at[slot], UD_G, chip_dev)
    share_half(g_send, g_recv, g_all, G_R, G_G, core)
    share_half(g_send, g_recv, g_all, G_R + 1, G_G + 1, other)
    arrived(u_all.at[pl.ds(0, N - 1)], UD_G)
    to_twin_half(u_all, UD_C)

    def gradient():
        spread(q_all.at[:, me], Q_G, shard_dev)
        g_full = g_all[...].reshape(512, 256)
        grad = dot(weight[...], g_full)
        grad_out[...] = grad
        grad = grad * gains[...]
        pltpu.make_async_copy(grad_out, grad_to, local.at[5]).start()
        square = jnp.sum((grad * grad).reshape(64, 8, 256), axis=0)
        sq[...] = square[:, :128] + square[:, 128:]
        to_twin(sq, sq_c, SQ_C)

    arrived(g_all.at[0, pl.ds(0, N - 1)], G_G)
    v_mine = reduce_dp(
        lambda c, h: dot(quarter(g_all, c, h), rb[...], NT),
        v_send, v_c, v_x, v_xr, v_y, v_yr, V, gradient,
        lambda: arrived(g_all.at[0, pl.ds(0, N - 1)], G_G + 1), True,
    ).astype(BF16)
    v_all[slot] = v_mine

    def blocks(ref, gram):
        for h in range(2):
            for b in range(8):
                block = 128 * (b % 4)
                ref[8 * h + b] = gram[8 * h : 8 * h + 8, block : block + 128]

    gather_y(v_all, VG)
    blocks(n_send, dot(v_mine, stb, NT))
    scatter(n_send, n_recv, N_R)
    gather_x(v_all, VG)
    arrived(n_recv, N_R)
    n_part[me] = total(n_send[me], n_recv)
    spread(n_part.at[me], N_G, shard_dev)
    gather_core(v_all, VG)
    arrived(sq_c, SQ_C)
    sq_d[0] = sq[...] + sq_c[...]
    each(lambda k: start(sq_d.at[0], sq_d.at[k], SQ_D, chip_dev(k)))

    def p_part(c):
        vt = v_all[pl.ds(c * N, N)].reshape(256, 512)
        p_send[c] = dot(vt, rb[...]).astype(BF16).reshape(N, 16, 256)

    p_part(core)
    send_half(p_send, p_recv, P_R, core)
    gather_other(v_all, VG)
    vt = v_all[...].reshape(512, 512)
    blocks(m_send, dot(v_mine, vt, NT))
    scatter(m_send, m_recv, M_R)
    p_part(other)
    send_half(p_send, p_recv, P_R + 1, other)

    arrived(n_part.at[pl.ds(0, N - 1)], N_G)
    n_all[slot] = assemble(n_part, 4)
    gather_y(n_all, NG)
    arrived(m_recv, M_R)
    m_part[me] = total(m_send[me], m_recv)
    spread(m_part.at[me], M_G, shard_dev)
    share_half(p_send, p_recv, p_all, P_R, P_G, core)
    gather_x(n_all, NG)
    arrived(sq_d.at[pl.ds(1, N - 1)], SQ_D)
    square = sq_d[0]
    for k in range(1, N):
        square = square + sq_d[k]
    sq_s[0] = square
    each(lambda k: start(sq_s.at[0], sq_s.at[k], SQ_S, shard_dev(k)))
    share_half(p_send, p_recv, p_all, P_R + 1, P_G + 1, other)
    arrived(m_part.at[pl.ds(0, N - 1)], M_G)
    m_all[slot] = assemble(m_part, 4)
    gather_y(m_all, MG)
    gather_core(n_all, NG)
    v_full = vt.astype(F32).T.astype(BF16)
    gather_x(m_all, MG)
    gather_core(m_all, MG)

    arrived(sq_s.at[pl.ds(1, N - 1)], SQ_S)
    for k in range(1, N):
        square = square + sq_s[k]
    square = jnp.sum(jnp.sum(square, axis=1, keepdims=True), axis=0, keepdims=True)
    step = 0.4 * math.sqrt(512) * lax.rsqrt(D * square + 1e-06)
    arrived(u_all.at[pl.ds(0, N)], UD_C)
    arrived(q_all.at[:, pl.ds(0, N - 1)], Q_G)
    q_full = q_all[...].reshape(512, 256)
    uu = u_all[...].reshape(512, 512)
    gather_other(n_all, NG)
    vu = n_all[...].reshape(512, 512)
    right = 2.0 * q_full.astype(F32) + step * dot(vu, q_full, TN)
    gather_other(m_all, MG)
    vv = m_all[...].reshape(512, 512)
    left = step * dot(vv, q_full)
    arrived(p_all.at[0, pl.ds(0, N - 1)], P_G)
    arrived(p_all.at[0, pl.ds(0, N - 1)], P_G + 1)
    p_full = p_all[...].reshape(512, 256)
    left = left + 2.0 * p_full.astype(F32) - step * dot(vu, p_full)
    right = right - step * dot(uu, p_full)
    left, right = left.astype(BF16), right.astype(BF16)
    for c in range(4):
        rows = slice(128 * c, 128 * c + 128)
        applied = gains[rows] * dot(weight[rows], left) - dot(v_full[rows], right)
        next_out[rows] = 0.5 * step * applied
        pltpu.make_async_copy(next_out.at[rows], next_to.at[rows], local.at[6]).start()

    for ref, which in sent:
        pltpu.make_async_copy(ref, ref, sends.at[which]).wait()
    pltpu.make_async_copy(grad_out, grad_to, local.at[5]).wait()
    pltpu.make_async_copy(next_out, next_to, local.at[6]).wait()


def shards(residual, norm_gain, value_weight, rotation, target):
    hbm = pl.BlockSpec(memory_space=pltpu.HBM)
    scratch = [
        ((1024, 256), BF16), ((1, 512), F32), ((512, 512), BF16), ((512, 256), F32), ((1024, 512), BF16),
        ((512, 256), F32), ((512, 256), F32),
        ((512, 256), F32),
        ((512, 512), BF16),
        ((512, 256), BF16),
        ((1024, 256), BF16),
        ((16, 128), F32), ((16, 128), F32), ((N, 16, 128), F32),
        ((N, 48, 256), BF16), ((N - 1, 48, 256), BF16), ((2, N, 16, 256), BF16), ((2, N, 16, 256), BF16),
        ((8, 128), F32), ((8, 128), F32), ((N, 8, 128), F32),
        ((2, 128, 1024), BF16), ((2, 128, 1024), BF16), ((8, 16, 1024), BF16), ((8, 16, 1024), BF16),
        ((8, 16, 1024), F32), ((7, 16, 1024), BF16),
        ((2 * N, 16, 1024), BF16),
        ((2, N, 16, 256), BF16), ((2, N - 1, 16, 256), BF16), ((2, N, 16, 256), BF16),
        ((2, 128, 512), BF16), ((2, 128, 512), BF16), ((8, 16, 512), BF16), ((8, 16, 512), BF16),
        ((8, 16, 512), F32), ((7, 16, 512), BF16),
        ((2 * N, 16, 512), BF16),
        ((2, N, 16, 256), BF16), ((2, N - 1, 16, 256), BF16), ((2, N, 16, 256), BF16),
        ((8, 128), F32), ((8, 128), F32), ((N, 8, 128), F32), ((N, 8, 128), F32),
        ((N, 8, 128), F32), ((N - 1, 8, 128), F32), ((N, 8, 128), F32), ((2 * N, 16, 512), BF16),
        ((N, 8, 128), F32), ((N - 1, 8, 128), F32), ((N, 8, 128), F32), ((2 * N, 16, 512), BF16),
        ((N, 8, 128), F32), ((N - 1, 8, 128), F32), ((N, 8, 128), F32), ((2 * N, 16, 512), BF16),
    ]
    buffers = [pltpu.VMEM(shape, kind) for shape, kind in scratch]
    grad, correction = pl.pallas_call(
        kernel,
        out_shape=[jax.ShapeDtypeStruct((512, 256), F32)] * 2,
        in_specs=[hbm] * 5,
        out_specs=[hbm] * 2,
        scratch_shapes=buffers[:7] + [pltpu.SemaphoreType.DMA((7,))] + buffers[7:]
        + [pltpu.SemaphoreType.DMA((COUNT,)), pltpu.SemaphoreType.DMA((COUNT,))],
        compiler_params=pltpu.CompilerParams(
            collective_id=0, has_side_effects=True, vmem_limit_bytes=LIMIT
        ),
        cost_estimate=pl.CostEstimate(
            flops=2 * 10**9, bytes_accessed=4 * 2**20, transcendentals=0
        ),
    )(residual, norm_gain.reshape(1, -1), value_weight, rotation, target)
    return grad * (norm_gain * (1.0 / math.sqrt(D)))[:, None], rotation - correction


def solution(mesh):
    in_specs = (P("shard", "dp"), P("shard"), P("shard", None), P("shard", "dp"), P("shard", None))
    out_specs = (P("shard", "dp"), P("shard", "dp"))
    return jax.shard_map(
        lambda *a: tuple(shards(*a)), mesh=mesh, in_specs=in_specs, out_specs=out_specs, check_vma=False
    )
```

```python
import math

import jax
import jax.numpy as jnp
from jax import lax
from jax.experimental import pallas as pl
from jax.experimental.pallas import tpu as pltpu
from jax.sharding import PartitionSpec as P

D = 8192
LIMIT = 63 * 2**20
N = 16
MESH = pl.DeviceIdType.MESH
F32 = jnp.float32
BF16 = jnp.bfloat16

SINE = (
    0.9999999944722865,
    -6.579735439437006,
    12.987842893121643,
    -12.207428862935943,
    6.687066146603468,
    -2.366367060643953,
    0.5091905906829214,
)

NN = (((1,), (0,)), ((), ()))
NT = (((1,), (1,)), ((), ()))
TN = (((0,), (0,)), ((), ()))


def dot(a, b, dims=NN):
    return lax.dot_general(a, b, dims, preferred_element_type=F32)


def soft(v):
    r = v - jnp.floor(v + 0.5)
    s = r * r
    p = jnp.full_like(s, SINE[-1])
    for c in SINE[-2::-1]:
        p = p * s + c
    return v - r * p


def twin(a):
    return jnp.concatenate([a, a], axis=1)


(
    STAT_C, STAT_D, Q_R, PEAK_C, PEAK_D, W_G, Q_G,
    SQ_C, SQ_D, SQ_S, U_R, U_G, UD_G, UD_C, M_R, M_G, N_R, N_G, W_H,
) = range(19)
OUT, V = 20, 31
OG, VG, MG = 42, 53, 64
G_R, G_G, P_R, P_G = 75, 77, 79, 81
NG = 83
COUNT = 94
FAR = (4, 3, 5, 2, 6, 1, 7)
NEAR = FAR[::-1]


def kernel(
    res_in, gain_in, weight_in, rot_in, target_in, grad_to, next_to,
    res, gain, weight, rot, target, grad_out, next_out, local,
    gains, wt, rb, rb_t, act, act_t, stat, stat_c, stat_d,
    q_send, q_recv, q_all, w_all,
    peak, peak_c, peak_d,
    out_send, out_c, out_x, out_xr, out_y, out_yr, og_all,
    g_send, g_recv, g_all,
    v_send, v_c, v_x, v_xr, v_y, v_yr, v_all,
    p_send, p_recv, p_all,
    sq, sq_c, sq_d, sq_s,
    u_send, u_recv, u_part, u_all,
    m_send, m_recv, m_part, m_all,
    n_send, n_recv, n_part, n_all,
    sends, recvs,
):
    dp, me = lax.axis_index("dp"), lax.axis_index("shard")
    chip, core = lax.div(dp, 2), lax.rem(dp, 2)
    y, xl = lax.div(chip, 2), lax.rem(chip, 2)
    other, xo = 1 - core, 1 - xl
    slot = core * N + xl * 8 + y
    twin_id = (chip * 2 + other, me)
    x_id = ((y * 2 + xo) * 2 + core, me)

    loads = []
    for n, (src, dst) in enumerate(
        ((weight_in, weight), (rot_in, rot), (gain_in, gain), (res_in, res), (target_in, target))
    ):
        rows = src.shape[0]
        cuts = 4 if rows > 1 else 1
        for c in range(cuts):
            part = pl.ds(c * (rows // cuts), rows // cuts)
            pltpu.make_async_copy(src.at[part], dst.at[part], local.at[n]).start()
        loads.append(pltpu.make_async_copy(src, dst, local.at[n]))

    def y_id(k):
        return ((lax.rem(y + k, 8) * 2 + xl) * 2 + core, me)

    def shard_id(k):
        return lax.rem(me + k, N)

    def chip_id(k):
        return lax.rem(chip + k, N)

    def shard_dev(k):
        return (dp, shard_id(k))

    def chip_dev(k):
        return (chip_id(k) * 2 + core, me)

    def each(body):
        def step(k, _):
            body(k)
            return 0

        lax.fori_loop(1, N, step, 0)

    def start(src, dst, which, device):
        pltpu.make_async_remote_copy(
            src_ref=src, dst_ref=dst, send_sem=sends.at[which], recv_sem=recvs.at[which],
            device_id=device, device_id_type=MESH,
        ).start()

    sent = []

    def arrived(ref, which):
        pltpu.make_async_copy(ref, ref, recvs.at[which]).wait()
        sent.append((ref, which))

    def scatter(src, dst, which):
        each(lambda k: start(src.at[shard_id(k)], dst.at[k - 1], which, shard_dev(k)))

    def spread(ref, which, device):
        each(lambda k: start(ref, ref, which, device(k)))

    def to_twin(src, dst, which):
        start(src, dst, which, twin_id)

    def reduce_dp(part, send, from_twin, x_send, x_recv, y_send, y_recv, base, between, ready, own_first):
        width = send.shape[2]
        if own_first:
            own = [part(core, xo), part(core, xl)]
            ready()
        for n, h in enumerate((xo, xl)):
            send[n] = part(other, h).astype(BF16)
            to_twin(send.at[n], from_twin.at[n], base + n)
        if not own_first:
            ready()
            own = [part(core, xo), part(core, xl)]
        arrived(from_twin.at[0], base)
        both = own[0] + from_twin[0].astype(F32)
        x_send[...] = both.astype(BF16).reshape(8, 16, width)
        for k in FAR + (0,):
            start(x_send.at[lax.rem(y + k, 8)], x_recv.at[k], base + 2 + k, x_id)
        arrived(from_twin.at[1], base + 1)
        both = own[1] + from_twin[1].astype(F32)
        y_send[...] = both.reshape(8, 16, width)
        for k in FAR:
            arrived(x_recv.at[k], base + 2 + k)
            x_recv[k] = (y_send[lax.rem(y + k, 8)] + x_recv[k].astype(F32)).astype(BF16)
            start(x_recv.at[k], y_recv.at[k - 1], base + 10, y_id(k))
        between()
        arrived(x_recv.at[0], base + 2)
        acc = y_send[y] + x_recv[0].astype(F32)
        arrived(y_recv, base + 10)
        for k in range(7):
            acc = acc + y_recv[k].astype(F32)
        return acc

    def gather_y(ref, base):
        own = ref.at[slot]
        for k in FAR:
            start(own, own, base + k, y_id(k))
        start(own, own, base + 8, x_id)

    def gather_x(ref, base):
        for k in NEAR:
            block = ref.at[core * N + xl * 8 + lax.rem(y + 8 - k, 8)]
            arrived(block, base + k)
            start(block, block, base + 8, x_id)

    def gather_near(ref, base):
        near = ref.at[pl.ds(core * N + xl * 8, 8)]
        to_twin(near, near, base + 9)

    def gather_far(ref, base):
        far = ref.at[pl.ds(core * N + xo * 8, 8)]
        arrived(far, base + 8)
        to_twin(far, far, base + 10)

    def gather_other(ref, base):
        arrived(ref.at[pl.ds(0, 8)], base + 9)
        arrived(ref.at[pl.ds(0, 8)], base + 10)

    def gather_and_send(ref, base, make, src, dst, which):
        gather_near(ref, base)
        make(core, xl)
        send_quarter(src, dst, which, core, xl)
        gather_far(ref, base)
        make(core, xo)
        send_quarter(src, dst, which, core, xo)
        arrived(ref.at[pl.ds(0, 8)], base + 9)
        make(other, xl)
        send_quarter(src, dst, which + 1, other, xl)
        arrived(ref.at[pl.ds(0, 8)], base + 10)

    def total(own, recv):
        acc = own.astype(F32)
        for k in range(N - 1):
            acc = acc + recv[k].astype(F32)
        return acc

    barrier = pltpu.get_barrier_semaphore()
    pl.semaphore_signal(barrier, inc=1, device_id=twin_id, device_id_type=MESH)

    def greet(k):
        pl.semaphore_signal(barrier, inc=1, device_id=shard_dev(k), device_id_type=MESH)
        pl.semaphore_signal(barrier, inc=1, device_id=chip_dev(k), device_id_type=MESH)

    each(greet)

    loads[0].wait()
    loads[2].wait()
    wt[...] = weight[...].astype(F32).T.astype(BF16)
    norm = gain[...] * (1.0 / math.sqrt(D))
    for c in range(4):
        rows = slice(128 * c, 128 * c + 128)
        gains[rows] = twin(jnp.broadcast_to(norm[:, rows], (128, 128)).T)
    loads[1].wait()
    scaled = rot[...] * gains[...]
    first = scaled.astype(BF16)
    second = (scaled - first.astype(F32)).astype(BF16)
    q = (dot(wt[...], first) + dot(wt[...], second)).reshape(2, N, 16, 256)
    high = q.astype(BF16)
    q_send[:, :16] = high[0]
    q_send[:, 16:32] = high[1]
    high = high.astype(F32)
    rest = jnp.floor((q - high) * (15 * 256.0) / (jnp.abs(high) + 1e-30) + 0.5)
    rest = jnp.clip(rest, -7.0, 7.0)
    q_send[:, 32:] = (rest[0] * 16.0 + rest[1]).astype(BF16)
    pl.semaphore_wait(barrier, 2 * N - 1)
    scatter(q_send, q_recv, Q_R)

    loads[3].wait()
    for k in range(8):
        h = res[128 * k : 128 * k + 128, :].astype(F32)
        a, b = h[:, :128], h[:, 128:]
        stat[k : k + 1, :] = jnp.sum((a * a + b * b).T, axis=0, keepdims=True)
        stat[8 + k : 9 + k, :] = jnp.max(
            jnp.maximum(jnp.abs(a), jnp.abs(b)).T, axis=0, keepdims=True
        )
    to_twin(stat, stat_c, STAT_C)
    rb[...] = rot[...].astype(BF16)
    stb = (wt[...].astype(F32) * norm).astype(BF16)
    mine = wt[pl.ds(pl.multiple_of(slot * 16, 16), 16), :].astype(F32) * norm
    u_gram = dot(mine.astype(BF16), stb, NT)
    for h in range(2):
        for b in range(4):
            block = u_gram[8 * h : 8 * h + 8, 128 * b : 128 * b + 128]
            u_send[8 * h + b] = block
            u_send[8 * h + 4 + b] = block
    arrived(stat_c, STAT_C)

    def combine(a, b):
        return jnp.concatenate([a[:8] + b[:8], jnp.maximum(a[8:], b[8:])], axis=0)

    both = combine(stat[...], stat_c[...])
    stat_d[0] = both
    each(lambda k: start(stat_d.at[0], stat_d.at[k], STAT_D, chip_dev(k)))

    arrived(q_recv, Q_R)

    def decode(a):
        high, rest = a[:32].astype(F32), a[32:].astype(F32)
        upper = jnp.floor(rest * 0.0625 + 0.5)
        rest = jnp.concatenate([upper, rest - 16.0 * upper], axis=0)
        return high + rest * (jnp.abs(high) * (1.0 / (15 * 256)))

    q_mine = decode(q_send[me])
    for k in range(N - 1):
        q_mine = q_mine + decode(q_recv[k])
    top = jnp.maximum(jnp.abs(q_mine[:, :128]), jnp.abs(q_mine[:, 128:]))
    top = jnp.max(jnp.concatenate([top] * 4, axis=0).T, axis=0, keepdims=True)
    peak[...] = jnp.broadcast_to(top, (8, 128))
    to_twin(peak, peak_c, PEAK_C)

    arrived(stat_d.at[pl.ds(1, N - 1)], STAT_D)
    for k in range(1, N):
        both = combine(both, stat_d[k])
    row_peak = both[8:] + 1e-06
    inv_rms = lax.rsqrt(both[:8] / D + 1e-05)
    rows_in = 7.0 / row_peak
    rows_out = row_peak * inv_rms / 7.0

    arrived(peak_c, PEAK_C)
    top = jnp.maximum(peak[...], peak_c[...])
    peak_d[0] = top
    each(lambda k: start(peak_d.at[0], peak_d.at[k], PEAK_D, chip_dev(k)))

    for k in range(8):
        into = twin(jnp.broadcast_to(rows_in[k : k + 1, :], (128, 128)).T)
        outof = twin(jnp.broadcast_to(rows_out[k : k + 1, :], (128, 128)).T)
        h = res[128 * k : 128 * k + 128, :].astype(F32)
        act[128 * k : 128 * k + 128, :] = (outof * soft(into * h)).astype(BF16)

    arrived(peak_d.at[pl.ds(1, N - 1)], PEAK_D)
    for k in range(1, N):
        top = jnp.maximum(top, peak_d[k])
    column = jnp.broadcast_to(top[:1, :], (128, 128)).T[:32, :]
    scale = twin((column + 1e-06) / 7.0)
    w_all[:, me] = (scale * soft(q_mine / scale)).astype(BF16).reshape(2, 16, 256)
    spread(w_all.at[other, me], W_G, shard_dev)
    spread(w_all.at[core, me], W_H, shard_dev)
    q_all[:, me] = q_mine.astype(BF16).reshape(2, 16, 256)
    scatter(u_send, u_recv, U_R)

    act_t[...] = act[...].astype(F32).T.astype(BF16)
    rb_t[...] = rot[...].T.astype(BF16)
    loads[4].wait()
    wanted = slot * 16 + lax.broadcasted_iota(jnp.int32, (16, 512), 0)
    one_hot = jnp.where(lax.broadcasted_iota(jnp.int32, (16, 512), 1) == wanted, 1.0, 0.0)
    target_mine = dot(one_hot.astype(BF16), target[...], NT)

    arrived(w_all.at[0, pl.ds(0, N - 1)], W_G)

    def quarter(ref, c, h):
        return ref[c, pl.ds(h * 8, 8)].reshape(128, 256)

    def weight_gram():
        arrived(u_recv, U_R)
        u_part[me] = total(u_send[me], u_recv)
        spread(u_part.at[me], U_G, shard_dev)

    out_mine = reduce_dp(
        lambda c, h: dot(quarter(w_all, c, h), act_t[...]),
        out_send, out_c, out_x, out_xr, out_y, out_yr, OUT, weight_gram,
        lambda: arrived(w_all.at[0, pl.ds(0, N - 1)], W_H), False,
    )
    og_all[slot] = (out_mine - target_mine).astype(BF16)
    gather_y(og_all, OG)
    gather_x(og_all, OG)

    def send_quarter(src, dst, which, c, h):
        def step(j, _):
            to = h * 8 + j

            @pl.when(to != me)
            def _():
                k = lax.rem(to + N - me, N)
                start(src.at[c, to], dst.at[c, k - 1], which, (dp, to))

            return 0

        lax.fori_loop(0, 8, step, 0)

    def share_half(src, recv, ref, which, after, c):
        arrived(recv.at[c], which)
        acc = src[c, me].astype(F32)
        for k in range(N - 1):
            acc = acc + recv[c, k].astype(F32)
        ref[c, me] = acc.astype(BF16)
        spread(ref.at[c, me], after, shard_dev)

    def g_part(c, h):
        og = og_all[pl.ds(c * N + h * 8, 8)].reshape(128, 1024)
        g_send[c, pl.ds(h * 8, 8)] = dot(og, act[...]).astype(BF16).reshape(8, 16, 256)

    gather_and_send(og_all, OG, g_part, g_send, g_recv, G_R)
    g_part(other, xo)
    send_quarter(g_send, g_recv, G_R + 1, other, xo)

    def assemble(part, count):
        rows = [
            jnp.concatenate([part[8 * h + b] for b in range(count)], axis=1)
            for h in range(2)
        ]
        return jnp.concatenate(rows, axis=0).astype(BF16)

    def to_twin_half(ref, which):
        half = ref.at[pl.ds(core * N, N)]
        to_twin(half, half, which)

    arrived(u_part.at[pl.ds(0, N - 1)], U_G)
    u_all[slot] = assemble(u_part, 4)
    spread(u_all.at[slot], UD_G, chip_dev)
    share_half(g_send, g_recv, g_all, G_R, G_G, core)
    share_half(g_send, g_recv, g_all, G_R + 1, G_G + 1, other)
    arrived(u_all.at[pl.ds(0, N - 1)], UD_G)
    to_twin_half(u_all, UD_C)

    def gradient():
        spread(q_all.at[:, me], Q_G, shard_dev)
        g_full = g_all[...].reshape(512, 256)
        grad = gains[...] * dot(weight[...], g_full)
        grad_out[...] = grad
        pltpu.make_async_copy(grad_out, grad_to, local.at[5]).start()
        square = jnp.sum((grad * grad).reshape(64, 8, 256), axis=0)
        sq[...] = square[:, :128] + square[:, 128:]
        to_twin(sq, sq_c, SQ_C)

    arrived(g_all.at[0, pl.ds(0, N - 1)], G_G)
    v_mine = reduce_dp(
        lambda c, h: dot(quarter(g_all, c, h), rb_t[...]),
        v_send, v_c, v_x, v_xr, v_y, v_yr, V, gradient,
        lambda: arrived(g_all.at[0, pl.ds(0, N - 1)], G_G + 1), True,
    ).astype(BF16)
    v_all[slot] = v_mine

    def blocks(ref, gram):
        for h in range(2):
            for b in range(8):
                block = 128 * (b % 4)
                ref[8 * h + b] = gram[8 * h : 8 * h + 8, block : block + 128]

    gather_y(v_all, VG)
    blocks(n_send, dot(v_mine, stb, NT))
    scatter(n_send, n_recv, N_R)
    gather_x(v_all, VG)
    arrived(n_recv, N_R)
    n_part[me] = total(n_send[me], n_recv)
    spread(n_part.at[me], N_G, shard_dev)

    def p_part(c, h):
        block = v_all[pl.ds(c * N + h * 8, 8)].reshape(128, 512)
        p_send[c, pl.ds(h * 8, 8)] = dot(block, rb[...]).astype(BF16).reshape(8, 16, 256)

    gather_and_send(v_all, VG, p_part, p_send, p_recv, P_R)
    vt = v_all[...].reshape(512, 512)
    blocks(m_send, dot(v_mine, vt, NT))
    scatter(m_send, m_recv, M_R)
    p_part(other, xo)
    send_quarter(p_send, p_recv, P_R + 1, other, xo)
    arrived(sq_c, SQ_C)
    sq_d[0] = sq[...] + sq_c[...]
    each(lambda k: start(sq_d.at[0], sq_d.at[k], SQ_D, chip_dev(k)))

    arrived(n_part.at[pl.ds(0, N - 1)], N_G)
    n_all[slot] = assemble(n_part, 4)
    gather_y(n_all, NG)
    arrived(m_recv, M_R)
    m_part[me] = total(m_send[me], m_recv)
    spread(m_part.at[me], M_G, shard_dev)
    share_half(p_send, p_recv, p_all, P_R, P_G, core)
    gather_x(n_all, NG)
    arrived(sq_d.at[pl.ds(1, N - 1)], SQ_D)
    square = sq_d[0]
    for k in range(1, N):
        square = square + sq_d[k]
    sq_s[0] = square
    each(lambda k: start(sq_s.at[0], sq_s.at[k], SQ_S, shard_dev(k)))
    share_half(p_send, p_recv, p_all, P_R + 1, P_G + 1, other)
    arrived(m_part.at[pl.ds(0, N - 1)], M_G)
    m_all[slot] = assemble(m_part, 4)
    gather_y(m_all, MG)
    gather_near(n_all, NG)
    gather_far(n_all, NG)
    v_full = vt.astype(F32).T.astype(BF16)
    gather_x(m_all, MG)
    gather_near(m_all, MG)
    gather_far(m_all, MG)

    arrived(sq_s.at[pl.ds(1, N - 1)], SQ_S)
    for k in range(1, N):
        square = square + sq_s[k]
    square = jnp.sum(jnp.sum(square, axis=1, keepdims=True), axis=0, keepdims=True)
    step = 0.4 * math.sqrt(512) * lax.rsqrt(D * square + 1e-06)
    arrived(u_all.at[pl.ds(0, N)], UD_C)
    arrived(q_all.at[:, pl.ds(0, N - 1)], Q_G)
    q_full = q_all[...].reshape(512, 256)
    uu = u_all[...].reshape(512, 512)
    gather_other(n_all, NG)
    vu = n_all[...].reshape(512, 512)
    right = 2.0 * q_full.astype(F32) + step * dot(vu, q_full, TN)
    gather_other(m_all, MG)
    vv = m_all[...].reshape(512, 512)
    left = step * dot(vv, q_full)
    arrived(p_all.at[0, pl.ds(0, N - 1)], P_G)
    arrived(p_all.at[0, pl.ds(0, N - 1)], P_G + 1)
    p_full = p_all[...].reshape(512, 256)
    left = left + 2.0 * p_full.astype(F32) - step * dot(vu, p_full)
    right = right - step * dot(uu, p_full)
    left, right = left.astype(BF16), right.astype(BF16)
    for c in range(4):
        rows = slice(128 * c, 128 * c + 128)
        applied = gains[rows] * dot(weight[rows], left) - dot(v_full[rows], right)
        next_out[rows] = rot[rows] - 0.5 * step * applied
        pltpu.make_async_copy(next_out.at[rows], next_to.at[rows], local.at[6]).start()

    for ref, which in sent:
        pltpu.make_async_copy(ref, ref, sends.at[which]).wait()
    pltpu.make_async_copy(grad_out, grad_to, local.at[5]).wait()
    pltpu.make_async_copy(next_out, next_to, local.at[6]).wait()


def hand_over(grad_in, next_in, grad_to, next_to, sems):
    pairs = ((grad_in, grad_to), (next_in, next_to))
    for n, (src, dst) in enumerate(pairs):
        for c in range(8):
            rows = pl.ds(64 * c, 64)
            pltpu.make_async_copy(src.at[rows], dst.at[rows], sems.at[n]).start()
    for n, (src, dst) in enumerate(pairs):
        pltpu.make_async_copy(src, dst, sems.at[n]).wait()


def shards(residual, norm_gain, value_weight, rotation, target):
    hbm = pl.BlockSpec(memory_space=pltpu.HBM)
    scratch = [
        ((1024, 256), BF16), ((1, 512), F32), ((512, 512), BF16), ((512, 256), F32), ((1024, 512), BF16),
        ((512, 256), F32), ((512, 256), F32),
        ((512, 256), F32),
        ((512, 512), BF16),
        ((512, 256), BF16), ((256, 512), BF16),
        ((1024, 256), BF16), ((256, 1024), BF16),
        ((16, 128), F32), ((16, 128), F32), ((N, 16, 128), F32),
        ((N, 48, 256), BF16), ((N - 1, 48, 256), BF16), ((2, N, 16, 256), BF16), ((2, N, 16, 256), BF16),
        ((8, 128), F32), ((8, 128), F32), ((N, 8, 128), F32),
        ((2, 128, 1024), BF16), ((2, 128, 1024), BF16), ((8, 16, 1024), BF16), ((8, 16, 1024), BF16),
        ((8, 16, 1024), F32), ((7, 16, 1024), BF16),
        ((2 * N, 16, 1024), BF16),
        ((2, N, 16, 256), BF16), ((2, N - 1, 16, 256), BF16), ((2, N, 16, 256), BF16),
        ((2, 128, 512), BF16), ((2, 128, 512), BF16), ((8, 16, 512), BF16), ((8, 16, 512), BF16),
        ((8, 16, 512), F32), ((7, 16, 512), BF16),
        ((2 * N, 16, 512), BF16),
        ((2, N, 16, 256), BF16), ((2, N - 1, 16, 256), BF16), ((2, N, 16, 256), BF16),
        ((8, 128), F32), ((8, 128), F32), ((N, 8, 128), F32), ((N, 8, 128), F32),
        ((N, 8, 128), F32), ((N - 1, 8, 128), F32), ((N, 8, 128), F32), ((2 * N, 16, 512), BF16),
        ((N, 8, 128), F32), ((N - 1, 8, 128), F32), ((N, 8, 128), F32), ((2 * N, 16, 512), BF16),
        ((N, 8, 128), F32), ((N - 1, 8, 128), F32), ((N, 8, 128), F32), ((2 * N, 16, 512), BF16),
    ]
    buffers = [pltpu.VMEM(shape, kind) for shape, kind in scratch]
    results = [jax.ShapeDtypeStruct((512, 256), F32)] * 2
    computed = pl.pallas_call(
        kernel,
        out_shape=results,
        in_specs=[hbm] * 5,
        out_specs=[hbm] * 2,
        scratch_shapes=buffers[:7] + [pltpu.SemaphoreType.DMA((7,))] + buffers[7:]
        + [pltpu.SemaphoreType.DMA((COUNT,)), pltpu.SemaphoreType.DMA((COUNT,))],
        compiler_params=pltpu.CompilerParams(
            collective_id=0, has_side_effects=True, vmem_limit_bytes=LIMIT
        ),
        cost_estimate=pl.CostEstimate(
            flops=2 * 10**9, bytes_accessed=4 * 2**20, transcendentals=0
        ),
    )(residual, norm_gain.reshape(1, -1), value_weight, rotation, target)
    return pl.pallas_call(
        hand_over,
        out_shape=results,
        in_specs=[hbm] * 2,
        out_specs=[hbm] * 2,
        scratch_shapes=[pltpu.SemaphoreType.DMA((2,))],
        compiler_params=pltpu.CompilerParams(vmem_limit_bytes=LIMIT),
        cost_estimate=pl.CostEstimate(flops=0, bytes_accessed=2 * 2**20, transcendentals=0),
    )(*computed)


def solution(mesh):
    in_specs = (P("shard", "dp"), P("shard"), P("shard", None), P("shard", "dp"), P("shard", None))
    out_specs = (P("shard", "dp"), P("shard", "dp"))
    return jax.shard_map(
        lambda *a: tuple(shards(*a)), mesh=mesh, in_specs=in_specs, out_specs=out_specs, check_vma=False
    )
```

```python
import math

import jax
import jax.numpy as jnp
from jax import lax
from jax.experimental import pallas as pl
from jax.experimental.pallas import tpu as pltpu
from jax.sharding import PartitionSpec as P

D = 8192
LIMIT = 63 * 2**20
N = 16
MESH = pl.DeviceIdType.MESH
F32 = jnp.float32
BF16 = jnp.bfloat16

SINE = (
    0.9999999944722865,
    -6.579735439437006,
    12.987842893121643,
    -12.207428862935943,
    6.687066146603468,
    -2.366367060643953,
    0.5091905906829214,
)

NN = (((1,), (0,)), ((), ()))
NT = (((1,), (1,)), ((), ()))
TN = (((0,), (0,)), ((), ()))


def dot(a, b, dims=NN):
    return lax.dot_general(a, b, dims, preferred_element_type=F32)


def soft(v):
    r = v - jnp.floor(v + 0.5)
    s = r * r
    p = jnp.full_like(s, SINE[-1])
    for c in SINE[-2::-1]:
        p = p * s + c
    return v - r * p


def twin(a):
    return jnp.concatenate([a, a], axis=1)


(
    STAT_C, STAT_D, Q_R, PEAK_C, PEAK_D, W_G, Q_G,
    SQ_C, SQ_D, SQ_S, U_R, U_G, UD_G, UD_C, M_R, M_G, N_R, N_G, W_H,
) = range(19)
OUT, V = 20, 31
OG, VG, MG = 42, 53, 64
G_R, G_G, P_R, P_G = 75, 77, 79, 81
NG = 83
COUNT = 94
FAR = (4, 3, 5, 2, 6, 1, 7)
NEAR = FAR[::-1]


def kernel(
    res_in, gain_in, weight_in, rot_in, target_in, grad_to, next_to,
    res, gain, weight, rot, target, grad_out, next_out, local,
    gains, wt, rb, rb_t, act, act_t, stat, stat_c, stat_d,
    q_send, q_recv, q_all, w_all,
    peak, peak_c, peak_d,
    out_send, out_c, out_x, out_xr, out_y, out_yr, og_all,
    g_send, g_recv, g_all,
    v_send, v_c, v_x, v_xr, v_y, v_yr, v_all,
    p_send, p_recv, p_all,
    sq, sq_c, sq_d, sq_s,
    u_send, u_recv, u_part, u_all,
    m_send, m_recv, m_part, m_all,
    n_send, n_recv, n_part, n_all,
    sends, recvs,
):
    dp, me = lax.axis_index("dp"), lax.axis_index("shard")
    chip, core = lax.div(dp, 2), lax.rem(dp, 2)
    y, xl = lax.div(chip, 2), lax.rem(chip, 2)
    other, xo = 1 - core, 1 - xl
    slot = core * N + xl * 8 + y
    twin_id = (chip * 2 + other, me)
    x_id = ((y * 2 + xo) * 2 + core, me)

    loads = []
    for n, (src, dst) in enumerate(
        ((weight_in, weight), (rot_in, rot), (gain_in, gain), (res_in, res), (target_in, target))
    ):
        rows = src.shape[0]
        cuts = 4 if rows > 1 else 1
        for c in range(cuts):
            part = pl.ds(c * (rows // cuts), rows // cuts)
            pltpu.make_async_copy(src.at[part], dst.at[part], local.at[n]).start()
        loads.append(pltpu.make_async_copy(src, dst, local.at[n]))

    def y_id(k):
        return ((lax.rem(y + k, 8) * 2 + xl) * 2 + core, me)

    def shard_id(k):
        return lax.rem(me + k, N)

    def chip_id(k):
        return lax.rem(chip + k, N)

    def shard_dev(k):
        return (dp, shard_id(k))

    def chip_dev(k):
        return (chip_id(k) * 2 + core, me)

    def each(body):
        def step(k, _):
            body(k)
            return 0

        lax.fori_loop(1, N, step, 0, unroll=True)

    def start(src, dst, which, device):
        pltpu.make_async_remote_copy(
            src_ref=src, dst_ref=dst, send_sem=sends.at[which], recv_sem=recvs.at[which],
            device_id=device, device_id_type=MESH,
        ).start()

    sent = []

    def arrived(ref, which):
        pltpu.make_async_copy(ref, ref, recvs.at[which]).wait()
        sent.append((ref, which))

    def flush():
        for ref, which in sent:
            pltpu.make_async_copy(ref, ref, sends.at[which]).wait()
        sent.clear()

    def scatter(src, dst, which):
        each(lambda k: start(src.at[shard_id(k)], dst.at[k - 1], which, shard_dev(k)))

    def spread(ref, which, device):
        each(lambda k: start(ref, ref, which, device(k)))

    def to_twin(src, dst, which):
        start(src, dst, which, twin_id)

    def reduce_dp(part, send, from_twin, x_send, x_recv, y_send, y_recv, base, between, ready, own_first):
        width = send.shape[2]
        if own_first:
            own = [part(core, xo), part(core, xl)]
            ready()
        for n, h in enumerate((xo, xl)):
            send[n] = part(other, h).astype(BF16)
            to_twin(send.at[n], from_twin.at[n], base + n)
        if not own_first:
            ready()
            own = [part(core, xo), part(core, xl)]
        arrived(from_twin.at[0], base)
        both = own[0] + from_twin[0].astype(F32)
        x_send[...] = both.astype(BF16).reshape(8, 16, width)
        for k in FAR + (0,):
            start(x_send.at[lax.rem(y + k, 8)], x_recv.at[k], base + 2 + k, x_id)
        arrived(from_twin.at[1], base + 1)
        both = own[1] + from_twin[1].astype(F32)
        y_send[...] = both.reshape(8, 16, width)
        for k in FAR:
            arrived(x_recv.at[k], base + 2 + k)
            x_recv[k] = (y_send[lax.rem(y + k, 8)] + x_recv[k].astype(F32)).astype(BF16)
            start(x_recv.at[k], y_recv.at[k - 1], base + 10, y_id(k))
        between()
        arrived(x_recv.at[0], base + 2)
        acc = y_send[y] + x_recv[0].astype(F32)
        arrived(y_recv, base + 10)
        for k in range(7):
            acc = acc + y_recv[k].astype(F32)
        return acc

    def gather_y(ref, base):
        own = ref.at[slot]
        for k in FAR:
            start(own, own, base + k, y_id(k))
        start(own, own, base + 8, x_id)

    def gather_x(ref, base):
        for k in NEAR:
            block = ref.at[core * N + xl * 8 + lax.rem(y + 8 - k, 8)]
            arrived(block, base + k)
            start(block, block, base + 8, x_id)

    def gather_near(ref, base):
        near = ref.at[pl.ds(core * N + xl * 8, 8)]
        to_twin(near, near, base + 9)

    def gather_far(ref, base):
        far = ref.at[pl.ds(core * N + xo * 8, 8)]
        arrived(far, base + 8)
        to_twin(far, far, base + 10)

    def gather_other(ref, base):
        arrived(ref.at[pl.ds(0, 8)], base + 9)
        arrived(ref.at[pl.ds(0, 8)], base + 10)

    def gather_and_send(ref, base, make, src, dst, which):
        gather_near(ref, base)
        make(core, xl)
        send_quarter(src, dst, which, core, xl)
        gather_far(ref, base)
        make(core, xo)
        send_quarter(src, dst, which, core, xo)
        arrived(ref.at[pl.ds(0, 8)], base + 9)
        make(other, xl)
        send_quarter(src, dst, which + 1, other, xl)
        arrived(ref.at[pl.ds(0, 8)], base + 10)

    def total(own, recv):
        acc = own.astype(F32)
        for k in range(N - 1):
            acc = acc + recv[k].astype(F32)
        return acc

    barrier = pltpu.get_barrier_semaphore()
    pl.semaphore_signal(barrier, inc=1, device_id=twin_id, device_id_type=MESH)

    def greet(k):
        pl.semaphore_signal(barrier, inc=1, device_id=shard_dev(k), device_id_type=MESH)
        pl.semaphore_signal(barrier, inc=1, device_id=chip_dev(k), device_id_type=MESH)

    each(greet)

    loads[0].wait()
    loads[2].wait()
    wt[...] = weight[...].astype(F32).T.astype(BF16)
    norm = gain[...] * (1.0 / math.sqrt(D))
    for c in range(4):
        rows = slice(128 * c, 128 * c + 128)
        gains[rows] = twin(jnp.broadcast_to(norm[:, rows], (128, 128)).T)
    loads[1].wait()
    scaled = rot[...] * gains[...]
    first = scaled.astype(BF16)
    second = (scaled - first.astype(F32)).astype(BF16)
    q = (dot(wt[...], first) + dot(wt[...], second)).reshape(2, N, 16, 256)
    high = q.astype(BF16)
    q_send[:, :16] = high[0]
    q_send[:, 16:32] = high[1]
    high = high.astype(F32)
    rest = jnp.floor((q - high) * (15 * 256.0) / (jnp.abs(high) + 1e-30) + 0.5)
    rest = jnp.clip(rest, -7.0, 7.0)
    q_send[:, 32:] = (rest[0] * 16.0 + rest[1]).astype(BF16)
    pl.semaphore_wait(barrier, 2 * N - 1)
    scatter(q_send, q_recv, Q_R)

    loads[3].wait()
    for k in range(8):
        h = res[128 * k : 128 * k + 128, :].astype(F32)
        a, b = h[:, :128], h[:, 128:]
        stat[k : k + 1, :] = jnp.sum((a * a + b * b).T, axis=0, keepdims=True)
        stat[8 + k : 9 + k, :] = jnp.max(
            jnp.maximum(jnp.abs(a), jnp.abs(b)).T, axis=0, keepdims=True
        )
    to_twin(stat, stat_c, STAT_C)
    rb[...] = rot[...].astype(BF16)
    stb = (wt[...].astype(F32) * norm).astype(BF16)
    mine = wt[pl.ds(pl.multiple_of(slot * 16, 16), 16), :].astype(F32) * norm
    u_gram = dot(mine.astype(BF16), stb, NT)
    for h in range(2):
        for b in range(4):
            block = u_gram[8 * h : 8 * h + 8, 128 * b : 128 * b + 128]
            u_send[8 * h + b] = block
            u_send[8 * h + 4 + b] = block
    arrived(stat_c, STAT_C)

    def combine(a, b):
        return jnp.concatenate([a[:8] + b[:8], jnp.maximum(a[8:], b[8:])], axis=0)

    both = combine(stat[...], stat_c[...])
    stat_d[0] = both
    each(lambda k: start(stat_d.at[0], stat_d.at[k], STAT_D, chip_dev(k)))

    arrived(q_recv, Q_R)

    def decode(a):
        high, rest = a[:32].astype(F32), a[32:].astype(F32)
        upper = jnp.floor(rest * 0.0625 + 0.5)
        rest = jnp.concatenate([upper, rest - 16.0 * upper], axis=0)
        return high + rest * (jnp.abs(high) * (1.0 / (15 * 256)))

    q_mine = decode(q_send[me])
    for k in range(N - 1):
        q_mine = q_mine + decode(q_recv[k])
    top = jnp.maximum(jnp.abs(q_mine[:, :128]), jnp.abs(q_mine[:, 128:]))
    top = jnp.max(jnp.concatenate([top] * 4, axis=0).T, axis=0, keepdims=True)
    peak[...] = jnp.broadcast_to(top, (8, 128))
    to_twin(peak, peak_c, PEAK_C)

    arrived(stat_d.at[pl.ds(1, N - 1)], STAT_D)
    for k in range(1, N):
        both = combine(both, stat_d[k])
    row_peak = both[8:] + 1e-06
    inv_rms = lax.rsqrt(both[:8] / D + 1e-05)
    rows_in = 7.0 / row_peak
    rows_out = row_peak * inv_rms / 7.0

    arrived(peak_c, PEAK_C)
    top = jnp.maximum(peak[...], peak_c[...])
    peak_d[0] = top
    each(lambda k: start(peak_d.at[0], peak_d.at[k], PEAK_D, chip_dev(k)))

    for k in range(8):
        into = twin(jnp.broadcast_to(rows_in[k : k + 1, :], (128, 128)).T)
        outof = twin(jnp.broadcast_to(rows_out[k : k + 1, :], (128, 128)).T)
        h = res[128 * k : 128 * k + 128, :].astype(F32)
        act[128 * k : 128 * k + 128, :] = (outof * soft(into * h)).astype(BF16)

    arrived(peak_d.at[pl.ds(1, N - 1)], PEAK_D)
    for k in range(1, N):
        top = jnp.maximum(top, peak_d[k])
    column = jnp.broadcast_to(top[:1, :], (128, 128)).T[:32, :]
    scale = twin((column + 1e-06) / 7.0)
    w_all[:, me] = (scale * soft(q_mine / scale)).astype(BF16).reshape(2, 16, 256)
    spread(w_all.at[other, me], W_G, shard_dev)
    spread(w_all.at[core, me], W_H, shard_dev)
    q_all[:, me] = q_mine.astype(BF16).reshape(2, 16, 256)
    scatter(u_send, u_recv, U_R)

    act_t[...] = act[...].astype(F32).T.astype(BF16)
    rb_t[...] = rot[...].T.astype(BF16)
    loads[4].wait()
    wanted = slot * 16 + lax.broadcasted_iota(jnp.int32, (16, 512), 0)
    one_hot = jnp.where(lax.broadcasted_iota(jnp.int32, (16, 512), 1) == wanted, 1.0, 0.0)
    target_mine = dot(one_hot.astype(BF16), target[...], NT)

    arrived(w_all.at[0, pl.ds(0, N - 1)], W_G)

    def quarter(ref, c, h):
        return ref[c, pl.ds(h * 8, 8)].reshape(128, 256)

    def weight_gram():
        arrived(u_recv, U_R)
        u_part[me] = total(u_send[me], u_recv)
        spread(u_part.at[me], U_G, shard_dev)

    out_mine = reduce_dp(
        lambda c, h: dot(quarter(w_all, c, h), act_t[...]),
        out_send, out_c, out_x, out_xr, out_y, out_yr, OUT, weight_gram,
        lambda: arrived(w_all.at[0, pl.ds(0, N - 1)], W_H), False,
    )
    og_all[slot] = (out_mine - target_mine).astype(BF16)
    gather_y(og_all, OG)
    gather_x(og_all, OG)

    def send_quarter(src, dst, which, c, h):
        def step(j, _):
            to = h * 8 + j

            @pl.when(to != me)
            def _():
                k = lax.rem(to + N - me, N)
                start(src.at[c, to], dst.at[c, k - 1], which, (dp, to))

            return 0

        lax.fori_loop(0, 8, step, 0, unroll=True)

    def share_half(src, recv, ref, which, after, c):
        arrived(recv.at[c], which)
        acc = src[c, me].astype(F32)
        for k in range(N - 1):
            acc = acc + recv[c, k].astype(F32)
        ref[c, me] = acc.astype(BF16)
        spread(ref.at[c, me], after, shard_dev)

    def g_part(c, h):
        og = og_all[pl.ds(c * N + h * 8, 8)].reshape(128, 1024)
        g_send[c, pl.ds(h * 8, 8)] = dot(og, act[...]).astype(BF16).reshape(8, 16, 256)

    gather_and_send(og_all, OG, g_part, g_send, g_recv, G_R)
    g_part(other, xo)
    send_quarter(g_send, g_recv, G_R + 1, other, xo)

    def assemble(part, count):
        rows = [
            jnp.concatenate([part[8 * h + b] for b in range(count)], axis=1)
            for h in range(2)
        ]
        return jnp.concatenate(rows, axis=0).astype(BF16)

    def to_twin_half(ref, which):
        half = ref.at[pl.ds(core * N, N)]
        to_twin(half, half, which)

    arrived(u_part.at[pl.ds(0, N - 1)], U_G)
    u_all[slot] = assemble(u_part, 4)
    spread(u_all.at[slot], UD_G, chip_dev)
    share_half(g_send, g_recv, g_all, G_R, G_G, core)
    share_half(g_send, g_recv, g_all, G_R + 1, G_G + 1, other)
    arrived(u_all.at[pl.ds(0, N - 1)], UD_G)
    to_twin_half(u_all, UD_C)

    def gradient():
        spread(q_all.at[:, me], Q_G, shard_dev)
        g_full = g_all[...].reshape(512, 256)
        grad = gains[...] * dot(weight[...], g_full)
        grad_out[...] = grad
        pltpu.make_async_copy(grad_out, grad_to, local.at[5]).start()
        square = jnp.sum((grad * grad).reshape(64, 8, 256), axis=0)
        sq[...] = square[:, :128] + square[:, 128:]
        to_twin(sq, sq_c, SQ_C)

    arrived(g_all.at[0, pl.ds(0, N - 1)], G_G)
    v_mine = reduce_dp(
        lambda c, h: dot(quarter(g_all, c, h), rb_t[...]),
        v_send, v_c, v_x, v_xr, v_y, v_yr, V, gradient,
        lambda: arrived(g_all.at[0, pl.ds(0, N - 1)], G_G + 1), True,
    ).astype(BF16)
    v_all[slot] = v_mine

    def blocks(ref, gram):
        for h in range(2):
            for b in range(8):
                block = 128 * (b % 4)
                ref[8 * h + b] = gram[8 * h : 8 * h + 8, block : block + 128]

    gather_y(v_all, VG)
    blocks(n_send, dot(v_mine, stb, NT))
    scatter(n_send, n_recv, N_R)
    gather_x(v_all, VG)
    arrived(n_recv, N_R)
    n_part[me] = total(n_send[me], n_recv)
    spread(n_part.at[me], N_G, shard_dev)

    def p_part(c, h):
        block = v_all[pl.ds(c * N + h * 8, 8)].reshape(128, 512)
        p_send[c, pl.ds(h * 8, 8)] = dot(block, rb[...]).astype(BF16).reshape(8, 16, 256)

    gather_and_send(v_all, VG, p_part, p_send, p_recv, P_R)
    vt = v_all[...].reshape(512, 512)
    blocks(m_send, dot(v_mine, vt, NT))
    scatter(m_send, m_recv, M_R)
    p_part(other, xo)
    send_quarter(p_send, p_recv, P_R + 1, other, xo)
    arrived(sq_c, SQ_C)
    sq_d[0] = sq[...] + sq_c[...]
    each(lambda k: start(sq_d.at[0], sq_d.at[k], SQ_D, chip_dev(k)))

    arrived(n_part.at[pl.ds(0, N - 1)], N_G)
    n_all[slot] = assemble(n_part, 4)
    gather_y(n_all, NG)
    arrived(m_recv, M_R)
    m_part[me] = total(m_send[me], m_recv)
    spread(m_part.at[me], M_G, shard_dev)
    flush()
    share_half(p_send, p_recv, p_all, P_R, P_G, core)
    gather_x(n_all, NG)
    arrived(sq_d.at[pl.ds(1, N - 1)], SQ_D)
    square = sq_d[0]
    for k in range(1, N):
        square = square + sq_d[k]
    sq_s[0] = square
    each(lambda k: start(sq_s.at[0], sq_s.at[k], SQ_S, shard_dev(k)))
    share_half(p_send, p_recv, p_all, P_R + 1, P_G + 1, other)
    arrived(m_part.at[pl.ds(0, N - 1)], M_G)
    m_all[slot] = assemble(m_part, 4)
    gather_y(m_all, MG)
    gather_near(n_all, NG)
    gather_far(n_all, NG)
    v_full = vt.astype(F32).T.astype(BF16)
    gather_x(m_all, MG)
    gather_near(m_all, MG)
    gather_far(m_all, MG)

    arrived(sq_s.at[pl.ds(1, N - 1)], SQ_S)
    for k in range(1, N):
        square = square + sq_s[k]
    square = jnp.sum(jnp.sum(square, axis=1, keepdims=True), axis=0, keepdims=True)
    step = 0.4 * math.sqrt(512) * lax.rsqrt(D * square + 1e-06)
    arrived(u_all.at[pl.ds(0, N)], UD_C)
    arrived(q_all.at[:, pl.ds(0, N - 1)], Q_G)
    q_full = q_all[...].reshape(512, 256)
    uu = u_all[...].reshape(512, 512)
    gather_other(n_all, NG)
    vu = n_all[...].reshape(512, 512)
    right = 2.0 * q_full.astype(F32) + step * dot(vu, q_full, TN)
    flush()
    gather_other(m_all, MG)
    vv = m_all[...].reshape(512, 512)
    left = step * dot(vv, q_full)
    arrived(p_all.at[0, pl.ds(0, N - 1)], P_G)
    arrived(p_all.at[0, pl.ds(0, N - 1)], P_G + 1)
    p_full = p_all[...].reshape(512, 256)
    left = left + 2.0 * p_full.astype(F32) - step * dot(vu, p_full)
    right = right - step * dot(uu, p_full)
    left, right = left.astype(BF16), right.astype(BF16)
    for c in range(4):
        rows = slice(128 * c, 128 * c + 128)
        applied = gains[rows] * dot(weight[rows], left) - dot(v_full[rows], right)
        next_out[rows] = rot[rows] - 0.5 * step * applied
        pltpu.make_async_copy(next_out.at[rows], next_to.at[rows], local.at[6]).start()

    flush()
    pltpu.make_async_copy(grad_out, grad_to, local.at[5]).wait()
    pltpu.make_async_copy(next_out, next_to, local.at[6]).wait()


def hand_over(grad_in, next_in, grad_to, next_to, held, come, gone):
    pairs = ((grad_in, grad_to), (next_in, next_to))

    def copies(n, c):
        rows = pl.ds(128 * c, 128)
        src, dst = pairs[n]
        here = held.at[n, rows]
        return (
            pltpu.make_async_copy(src.at[rows], here, come.at[n, c]),
            pltpu.make_async_copy(here, dst.at[rows], gone.at[n, c]),
        )

    steps = [copies(n, c) for c in range(4) for n in range(2)]
    for first, _ in steps:
        first.start()
    for first, second in steps:
        first.wait()
        second.start()
    for _, second in steps:
        second.wait()


def shards(residual, norm_gain, value_weight, rotation, target):
    hbm = pl.BlockSpec(memory_space=pltpu.HBM)
    scratch = [
        ((1024, 256), BF16), ((1, 512), F32), ((512, 512), BF16), ((512, 256), F32), ((1024, 512), BF16),
        ((512, 256), F32), ((512, 256), F32),
        ((512, 256), F32),
        ((512, 512), BF16),
        ((512, 256), BF16), ((256, 512), BF16),
        ((1024, 256), BF16), ((256, 1024), BF16),
        ((16, 128), F32), ((16, 128), F32), ((N, 16, 128), F32),
        ((N, 48, 256), BF16), ((N - 1, 48, 256), BF16), ((2, N, 16, 256), BF16), ((2, N, 16, 256), BF16),
        ((8, 128), F32), ((8, 128), F32), ((N, 8, 128), F32),
        ((2, 128, 1024), BF16), ((2, 128, 1024), BF16), ((8, 16, 1024), BF16), ((8, 16, 1024), BF16),
        ((8, 16, 1024), F32), ((7, 16, 1024), BF16),
        ((2 * N, 16, 1024), BF16),
        ((2, N, 16, 256), BF16), ((2, N - 1, 16, 256), BF16), ((2, N, 16, 256), BF16),
        ((2, 128, 512), BF16), ((2, 128, 512), BF16), ((8, 16, 512), BF16), ((8, 16, 512), BF16),
        ((8, 16, 512), F32), ((7, 16, 512), BF16),
        ((2 * N, 16, 512), BF16),
        ((2, N, 16, 256), BF16), ((2, N - 1, 16, 256), BF16), ((2, N, 16, 256), BF16),
        ((8, 128), F32), ((8, 128), F32), ((N, 8, 128), F32), ((N, 8, 128), F32),
        ((N, 8, 128), F32), ((N - 1, 8, 128), F32), ((N, 8, 128), F32), ((2 * N, 16, 512), BF16),
        ((N, 8, 128), F32), ((N - 1, 8, 128), F32), ((N, 8, 128), F32), ((2 * N, 16, 512), BF16),
        ((N, 8, 128), F32), ((N - 1, 8, 128), F32), ((N, 8, 128), F32), ((2 * N, 16, 512), BF16),
    ]
    buffers = [pltpu.VMEM(shape, kind) for shape, kind in scratch]
    results = [jax.ShapeDtypeStruct((512, 256), F32)] * 2
    computed = pl.pallas_call(
        kernel,
        out_shape=results,
        in_specs=[hbm] * 5,
        out_specs=[hbm] * 2,
        scratch_shapes=buffers[:7] + [pltpu.SemaphoreType.DMA((7,))] + buffers[7:]
        + [pltpu.SemaphoreType.DMA((COUNT,)), pltpu.SemaphoreType.DMA((COUNT,))],
        compiler_params=pltpu.CompilerParams(
            collective_id=0, has_side_effects=True, vmem_limit_bytes=LIMIT
        ),
        cost_estimate=pl.CostEstimate(
            flops=2 * 10**9, bytes_accessed=4 * 2**20, transcendentals=0
        ),
    )(residual, norm_gain.reshape(1, -1), value_weight, rotation, target)
    return pl.pallas_call(
        hand_over,
        out_shape=results,
        in_specs=[hbm] * 2,
        out_specs=[hbm] * 2,
        scratch_shapes=[pltpu.VMEM((2, 512, 256), F32)]
        + [pltpu.SemaphoreType.DMA((2, 4))] * 2,
        compiler_params=pltpu.CompilerParams(vmem_limit_bytes=LIMIT),
        cost_estimate=pl.CostEstimate(flops=0, bytes_accessed=2 * 2**20, transcendentals=0),
    )(*computed)


def solution(mesh):
    in_specs = (P("shard", "dp"), P("shard"), P("shard", None), P("shard", "dp"), P("shard", None))
    out_specs = (P("shard", "dp"), P("shard", "dp"))
    return jax.shard_map(
        lambda *a: tuple(shards(*a)), mesh=mesh, in_specs=in_specs, out_specs=out_specs, check_vma=False
    )
```

```python
import math

import jax
import jax.numpy as jnp
from jax import lax
from jax.experimental import pallas as pl
from jax.experimental.pallas import tpu as pltpu
from jax.sharding import PartitionSpec as P

D = 8192
LIMIT = 63 * 2**20
N = 16
MESH = pl.DeviceIdType.MESH
F32 = jnp.float32
BF16 = jnp.bfloat16

SINE = (
    0.9999999944722865,
    -6.579735439437006,
    12.987842893121643,
    -12.207428862935943,
    6.687066146603468,
    -2.366367060643953,
    0.5091905906829214,
)

NN = (((1,), (0,)), ((), ()))
NT = (((1,), (1,)), ((), ()))
TN = (((0,), (0,)), ((), ()))


def dot(a, b, dims=NN):
    return lax.dot_general(a, b, dims, preferred_element_type=F32)


def soft(v):
    r = v - jnp.floor(v + 0.5)
    s = r * r
    p = jnp.full_like(s, SINE[-1])
    for c in SINE[-2::-1]:
        p = p * s + c
    return v - r * p


def twin(a):
    return jnp.concatenate([a, a], axis=1)


(
    STAT_C, STAT_D, Q_R, PEAK_C, PEAK_D, Q_G,
    SQ_C, SQ_D, SQ_S, U_R, U_G, UD_G, UD_C, M_R, M_G, N_R, N_G,
) = range(17)
OUT, V = 20, 31
OG, VG, MG = 42, 53, 64
G_R, P_R = 75, 77
NG = 83
W_G, G_G, P_G = 94, 110, 126
COUNT = 142
FAR = (4, 3, 5, 2, 6, 1, 7)
NEAR = FAR[::-1]


def kernel(
    res_in, gain_in, weight_in, rot_in, target_in, grad_to, next_to,
    res, gain, weight, rot, target, grad_out, next_out, local,
    gains, wt, rb, rb_t, act, act_t, stat, stat_c, stat_d,
    q_send, q_recv, q_all, w_all,
    peak, peak_c, peak_d,
    out_send, out_c, out_x, out_xr, out_y, out_yr, og_all,
    g_send, g_recv, g_all,
    v_send, v_c, v_x, v_xr, v_y, v_yr, v_all,
    p_send, p_recv, p_all,
    sq, sq_c, sq_d, sq_s,
    u_send, u_recv, u_part, u_all,
    m_send, m_recv, m_part, m_all,
    n_send, n_recv, n_part, n_all,
    sends, recvs,
):
    dp, me = lax.axis_index("dp"), lax.axis_index("shard")
    chip, core = lax.div(dp, 2), lax.rem(dp, 2)
    y, xl = lax.div(chip, 2), lax.rem(chip, 2)
    z, xh = lax.div(me, 2), lax.rem(me, 2)
    other, xo = 1 - core, 1 - xl
    slot = core * N + xl * 8 + y
    twin_id = (chip * 2 + other, me)
    x_id = ((y * 2 + xo) * 2 + core, me)

    loads = []
    for n, (src, dst) in enumerate(
        ((weight_in, weight), (rot_in, rot), (gain_in, gain), (res_in, res), (target_in, target))
    ):
        rows = src.shape[0]
        cuts = 4 if rows > 1 else 1
        for c in range(cuts):
            part = pl.ds(c * (rows // cuts), rows // cuts)
            pltpu.make_async_copy(src.at[part], dst.at[part], local.at[n]).start()
        loads.append(pltpu.make_async_copy(src, dst, local.at[n]))

    def y_id(k):
        return ((lax.rem(y + k, 8) * 2 + xl) * 2 + core, me)

    def shard_id(k):
        return lax.rem(me + k, N)

    def chip_id(k):
        return lax.rem(chip + k, N)

    def shard_dev(k):
        return (dp, shard_id(k))

    def chip_dev(k):
        return (chip_id(k) * 2 + core, me)

    def each(body):
        def step(k, _):
            body(k)
            return 0

        lax.fori_loop(1, N, step, 0, unroll=True)

    def start(src, dst, which, device):
        pltpu.make_async_remote_copy(
            src_ref=src, dst_ref=dst, send_sem=sends.at[which], recv_sem=recvs.at[which],
            device_id=device, device_id_type=MESH,
        ).start()

    sent = []

    def arrived(ref, which):
        pltpu.make_async_copy(ref, ref, recvs.at[which]).wait()
        sent.append((ref, which))

    def flush():
        for ref, which in sent:
            pltpu.make_async_copy(ref, ref, sends.at[which]).wait()
        sent.clear()

    def scatter(src, dst, which):
        each(lambda k: start(src.at[shard_id(k)], dst.at[k - 1], which, shard_dev(k)))

    def spread(ref, which, device):
        each(lambda k: start(ref, ref, which, device(k)))

    def to_twin(src, dst, which):
        start(src, dst, which, twin_id)

    def reduce_dp(part, send, from_twin, x_send, x_recv, y_send, y_recv, base, between, ready, own_first):
        width = send.shape[2]
        if own_first:
            own = [part(core, xo), part(core, xl)]
            ready()
        for n, h in enumerate((xo, xl)):
            send[n] = part(other, h).astype(BF16)
            to_twin(send.at[n], from_twin.at[n], base + n)
        if not own_first:
            ready()
            own = [part(core, xo), part(core, xl)]
        arrived(from_twin.at[0], base)
        both = own[0] + from_twin[0].astype(F32)
        x_send[...] = both.astype(BF16).reshape(8, 16, width)
        for k in FAR + (0,):
            start(x_send.at[lax.rem(y + k, 8)], x_recv.at[k], base + 2 + k, x_id)
        arrived(from_twin.at[1], base + 1)
        both = own[1] + from_twin[1].astype(F32)
        y_send[...] = both.reshape(8, 16, width)
        for k in FAR:
            arrived(x_recv.at[k], base + 2 + k)
            x_recv[k] = (y_send[lax.rem(y + k, 8)] + x_recv[k].astype(F32)).astype(BF16)
            start(x_recv.at[k], y_recv.at[k - 1], base + 10, y_id(k))
        between()
        arrived(x_recv.at[0], base + 2)
        acc = y_send[y] + x_recv[0].astype(F32)
        arrived(y_recv, base + 10)
        for k in range(7):
            acc = acc + y_recv[k].astype(F32)
        return acc

    def gather_y(ref, base):
        own = ref.at[slot]
        for k in FAR:
            start(own, own, base + k, y_id(k))
        start(own, own, base + 8, x_id)

    def gather_x(ref, base):
        for k in NEAR:
            block = ref.at[core * N + xl * 8 + lax.rem(y + 8 - k, 8)]
            arrived(block, base + k)
            start(block, block, base + 8, x_id)

    def gather_near(ref, base):
        near = ref.at[pl.ds(core * N + xl * 8, 8)]
        to_twin(near, near, base + 9)

    def gather_far(ref, base):
        far = ref.at[pl.ds(core * N + xo * 8, 8)]
        arrived(far, base + 8)
        to_twin(far, far, base + 10)

    def gather_other(ref, base):
        arrived(ref.at[pl.ds(0, 8)], base + 9)
        arrived(ref.at[pl.ds(0, 8)], base + 10)

    def gather_and_send(ref, base, make, src, dst, which):
        gather_near(ref, base)
        make(core, xl)
        send_quarter(src, dst, which, core, xl)
        gather_far(ref, base)
        make(core, xo)
        send_quarter(src, dst, which, core, xo)
        arrived(ref.at[pl.ds(0, 8)], base + 9)
        make(other, xl)
        send_quarter(src, dst, which + 1, other, xl)
        arrived(ref.at[pl.ds(0, 8)], base + 10)

    def share(ref, base, c):
        own = ref.at[c, me]
        for k in FAR:
            start(own, own, base + k, (dp, lax.rem(z + k, 8) * 2 + xh))
        start(own, own, base, (dp, z * 2 + 1 - xh))

    def forward(ref, base, c):
        for k in NEAR:
            block = ref.at[c, lax.rem(z + 8 - k, 8) * 2 + xh]
            arrived(block, base + k)
            start(block, block, base, (dp, z * 2 + 1 - xh))

    def settled(ref, base):
        arrived(ref.at[0, pl.ds(0, 8)], base)

    def total(own, recv):
        acc = own.astype(F32)
        for k in range(N - 1):
            acc = acc + recv[k].astype(F32)
        return acc

    barrier = pltpu.get_barrier_semaphore()
    pl.semaphore_signal(barrier, inc=1, device_id=twin_id, device_id_type=MESH)

    def greet(k):
        pl.semaphore_signal(barrier, inc=1, device_id=shard_dev(k), device_id_type=MESH)
        pl.semaphore_signal(barrier, inc=1, device_id=chip_dev(k), device_id_type=MESH)

    each(greet)

    loads[0].wait()
    loads[2].wait()
    wt[...] = weight[...].astype(F32).T.astype(BF16)
    norm = gain[...] * (1.0 / math.sqrt(D))
    for c in range(4):
        rows = slice(128 * c, 128 * c + 128)
        gains[rows] = twin(jnp.broadcast_to(norm[:, rows], (128, 128)).T)
    loads[1].wait()
    scaled = rot[...] * gains[...]
    first = scaled.astype(BF16)
    second = (scaled - first.astype(F32)).astype(BF16)
    q = (dot(wt[...], first) + dot(wt[...], second)).reshape(2, N, 16, 256)
    high = q.astype(BF16)
    q_send[:, :16] = high[0]
    q_send[:, 16:32] = high[1]
    high = high.astype(F32)
    rest = jnp.floor((q - high) * (15 * 256.0) / (jnp.abs(high) + 1e-30) + 0.5)
    rest = jnp.clip(rest, -7.0, 7.0)
    q_send[:, 32:] = (rest[0] * 16.0 + rest[1]).astype(BF16)
    pl.semaphore_wait(barrier, 2 * N - 1)
    scatter(q_send, q_recv, Q_R)

    loads[3].wait()
    for k in range(8):
        h = res[128 * k : 128 * k + 128, :].astype(F32)
        a, b = h[:, :128], h[:, 128:]
        stat[k : k + 1, :] = jnp.sum((a * a + b * b).T, axis=0, keepdims=True)
        stat[8 + k : 9 + k, :] = jnp.max(
            jnp.maximum(jnp.abs(a), jnp.abs(b)).T, axis=0, keepdims=True
        )
    to_twin(stat, stat_c, STAT_C)
    rb[...] = rot[...].astype(BF16)
    stb = (wt[...].astype(F32) * norm).astype(BF16)
    mine = wt[pl.ds(pl.multiple_of(slot * 16, 16), 16), :].astype(F32) * norm
    u_gram = dot(mine.astype(BF16), stb, NT)
    for h in range(2):
        for b in range(4):
            block = u_gram[8 * h : 8 * h + 8, 128 * b : 128 * b + 128]
            u_send[8 * h + b] = block
            u_send[8 * h + 4 + b] = block
    arrived(stat_c, STAT_C)

    def combine(a, b):
        return jnp.concatenate([a[:8] + b[:8], jnp.maximum(a[8:], b[8:])], axis=0)

    both = combine(stat[...], stat_c[...])
    stat_d[0] = both
    each(lambda k: start(stat_d.at[0], stat_d.at[k], STAT_D, chip_dev(k)))

    arrived(q_recv, Q_R)

    def decode(a):
        high, rest = a[:32].astype(F32), a[32:].astype(F32)
        upper = jnp.floor(rest * 0.0625 + 0.5)
        rest = jnp.concatenate([upper, rest - 16.0 * upper], axis=0)
        return high + rest * (jnp.abs(high) * (1.0 / (15 * 256)))

    q_mine = decode(q_send[me])
    for k in range(N - 1):
        q_mine = q_mine + decode(q_recv[k])
    top = jnp.maximum(jnp.abs(q_mine[:, :128]), jnp.abs(q_mine[:, 128:]))
    top = jnp.max(jnp.concatenate([top] * 4, axis=0).T, axis=0, keepdims=True)
    peak[...] = jnp.broadcast_to(top, (8, 128))
    to_twin(peak, peak_c, PEAK_C)

    arrived(stat_d.at[pl.ds(1, N - 1)], STAT_D)
    for k in range(1, N):
        both = combine(both, stat_d[k])
    row_peak = both[8:] + 1e-06
    inv_rms = lax.rsqrt(both[:8] / D + 1e-05)
    rows_in = 7.0 / row_peak
    rows_out = row_peak * inv_rms / 7.0

    arrived(peak_c, PEAK_C)
    top = jnp.maximum(peak[...], peak_c[...])
    peak_d[0] = top
    each(lambda k: start(peak_d.at[0], peak_d.at[k], PEAK_D, chip_dev(k)))

    for k in range(8):
        into = twin(jnp.broadcast_to(rows_in[k : k + 1, :], (128, 128)).T)
        outof = twin(jnp.broadcast_to(rows_out[k : k + 1, :], (128, 128)).T)
        h = res[128 * k : 128 * k + 128, :].astype(F32)
        act[128 * k : 128 * k + 128, :] = (outof * soft(into * h)).astype(BF16)

    arrived(peak_d.at[pl.ds(1, N - 1)], PEAK_D)
    for k in range(1, N):
        top = jnp.maximum(top, peak_d[k])
    column = jnp.broadcast_to(top[:1, :], (128, 128)).T[:32, :]
    scale = twin((column + 1e-06) / 7.0)
    w_all[:, me] = (scale * soft(q_mine / scale)).astype(BF16).reshape(2, 16, 256)
    share(w_all, W_G, other)
    share(w_all, W_G + 8, core)
    q_all[:, me] = q_mine.astype(BF16).reshape(2, 16, 256)
    scatter(u_send, u_recv, U_R)

    act_t[...] = act[...].astype(F32).T.astype(BF16)
    forward(w_all, W_G, other)
    rb_t[...] = rot[...].T.astype(BF16)
    loads[4].wait()
    wanted = slot * 16 + lax.broadcasted_iota(jnp.int32, (16, 512), 0)
    one_hot = jnp.where(lax.broadcasted_iota(jnp.int32, (16, 512), 1) == wanted, 1.0, 0.0)
    target_mine = dot(one_hot.astype(BF16), target[...], NT)

    forward(w_all, W_G + 8, core)
    settled(w_all, W_G)

    def quarter(ref, c, h):
        return ref[c, pl.ds(h * 8, 8)].reshape(128, 256)

    def weight_gram():
        arrived(u_recv, U_R)
        u_part[me] = total(u_send[me], u_recv)
        spread(u_part.at[me], U_G, shard_dev)

    out_mine = reduce_dp(
        lambda c, h: dot(quarter(w_all, c, h), act_t[...]),
        out_send, out_c, out_x, out_xr, out_y, out_yr, OUT, weight_gram,
        lambda: settled(w_all, W_G + 8), False,
    )
    og_all[slot] = (out_mine - target_mine).astype(BF16)
    gather_y(og_all, OG)
    gather_x(og_all, OG)

    def send_quarter(src, dst, which, c, h):
        def step(j, _):
            to = h * 8 + j

            @pl.when(to != me)
            def _():
                k = lax.rem(to + N - me, N)
                start(src.at[c, to], dst.at[c, k - 1], which, (dp, to))

            return 0

        lax.fori_loop(0, 8, step, 0, unroll=True)

    def share_half(src, recv, ref, which, after, c):
        arrived(recv.at[c], which)
        acc = src[c, me].astype(F32)
        for k in range(N - 1):
            acc = acc + recv[c, k].astype(F32)
        ref[c, me] = acc.astype(BF16)
        share(ref, after, c)

    def g_part(c, h):
        og = og_all[pl.ds(c * N + h * 8, 8)].reshape(128, 1024)
        g_send[c, pl.ds(h * 8, 8)] = dot(og, act[...]).astype(BF16).reshape(8, 16, 256)

    gather_and_send(og_all, OG, g_part, g_send, g_recv, G_R)
    g_part(other, xo)
    send_quarter(g_send, g_recv, G_R + 1, other, xo)

    def assemble(part, count):
        rows = [
            jnp.concatenate([part[8 * h + b] for b in range(count)], axis=1)
            for h in range(2)
        ]
        return jnp.concatenate(rows, axis=0).astype(BF16)

    def to_twin_half(ref, which):
        half = ref.at[pl.ds(core * N, N)]
        to_twin(half, half, which)

    arrived(u_part.at[pl.ds(0, N - 1)], U_G)
    u_all[slot] = assemble(u_part, 4)
    spread(u_all.at[slot], UD_G, chip_dev)
    share_half(g_send, g_recv, g_all, G_R, G_G, core)
    share_half(g_send, g_recv, g_all, G_R + 1, G_G + 8, other)
    forward(g_all, G_G, core)
    forward(g_all, G_G + 8, other)
    arrived(u_all.at[pl.ds(0, N - 1)], UD_G)
    to_twin_half(u_all, UD_C)

    def gradient():
        spread(q_all.at[:, me], Q_G, shard_dev)
        g_full = g_all[...].reshape(512, 256)
        grad = gains[...] * dot(weight[...], g_full)
        grad_out[...] = grad
        pltpu.make_async_copy(grad_out, grad_to, local.at[5]).start()
        square = jnp.sum((grad * grad).reshape(64, 8, 256), axis=0)
        sq[...] = square[:, :128] + square[:, 128:]
        to_twin(sq, sq_c, SQ_C)

    settled(g_all, G_G)
    v_mine = reduce_dp(
        lambda c, h: dot(quarter(g_all, c, h), rb_t[...]),
        v_send, v_c, v_x, v_xr, v_y, v_yr, V, gradient,
        lambda: settled(g_all, G_G + 8), True,
    ).astype(BF16)
    v_all[slot] = v_mine

    def blocks(ref, gram):
        for h in range(2):
            for b in range(8):
                block = 128 * (b % 4)
                ref[8 * h + b] = gram[8 * h : 8 * h + 8, block : block + 128]

    gather_y(v_all, VG)
    blocks(n_send, dot(v_mine, stb, NT))
    scatter(n_send, n_recv, N_R)
    gather_x(v_all, VG)
    arrived(n_recv, N_R)
    n_part[me] = total(n_send[me], n_recv)
    spread(n_part.at[me], N_G, shard_dev)

    def p_part(c, h):
        block = v_all[pl.ds(c * N + h * 8, 8)].reshape(128, 512)
        p_send[c, pl.ds(h * 8, 8)] = dot(block, rb[...]).astype(BF16).reshape(8, 16, 256)

    gather_and_send(v_all, VG, p_part, p_send, p_recv, P_R)
    vt = v_all[...].reshape(512, 512)
    blocks(m_send, dot(v_mine, vt, NT))
    scatter(m_send, m_recv, M_R)
    p_part(other, xo)
    send_quarter(p_send, p_recv, P_R + 1, other, xo)
    arrived(sq_c, SQ_C)
    sq_d[0] = sq[...] + sq_c[...]
    each(lambda k: start(sq_d.at[0], sq_d.at[k], SQ_D, chip_dev(k)))

    arrived(n_part.at[pl.ds(0, N - 1)], N_G)
    n_all[slot] = assemble(n_part, 4)
    gather_y(n_all, NG)
    arrived(m_recv, M_R)
    m_part[me] = total(m_send[me], m_recv)
    spread(m_part.at[me], M_G, shard_dev)
    flush()
    share_half(p_send, p_recv, p_all, P_R, P_G, core)
    gather_x(n_all, NG)
    arrived(sq_d.at[pl.ds(1, N - 1)], SQ_D)
    square = sq_d[0]
    for k in range(1, N):
        square = square + sq_d[k]
    sq_s[0] = square
    each(lambda k: start(sq_s.at[0], sq_s.at[k], SQ_S, shard_dev(k)))
    share_half(p_send, p_recv, p_all, P_R + 1, P_G + 8, other)
    forward(p_all, P_G, core)
    arrived(m_part.at[pl.ds(0, N - 1)], M_G)
    m_all[slot] = assemble(m_part, 4)
    gather_y(m_all, MG)
    forward(p_all, P_G + 8, other)
    gather_near(n_all, NG)
    gather_far(n_all, NG)
    v_full = vt.astype(F32).T.astype(BF16)
    gather_x(m_all, MG)
    gather_near(m_all, MG)
    gather_far(m_all, MG)

    arrived(sq_s.at[pl.ds(1, N - 1)], SQ_S)
    for k in range(1, N):
        square = square + sq_s[k]
    square = jnp.sum(jnp.sum(square, axis=1, keepdims=True), axis=0, keepdims=True)
    step = 0.4 * math.sqrt(512) * lax.rsqrt(D * square + 1e-06)
    arrived(u_all.at[pl.ds(0, N)], UD_C)
    arrived(q_all.at[:, pl.ds(0, N - 1)], Q_G)
    q_full = q_all[...].reshape(512, 256)
    uu = u_all[...].reshape(512, 512)
    gather_other(n_all, NG)
    vu = n_all[...].reshape(512, 512)
    right = 2.0 * q_full.astype(F32) + step * dot(vu, q_full, TN)
    flush()
    gather_other(m_all, MG)
    vv = m_all[...].reshape(512, 512)
    left = step * dot(vv, q_full)
    settled(p_all, P_G)
    settled(p_all, P_G + 8)
    p_full = p_all[...].reshape(512, 256)
    left = left + 2.0 * p_full.astype(F32) - step * dot(vu, p_full)
    right = right - step * dot(uu, p_full)
    left, right = left.astype(BF16), right.astype(BF16)
    for c in range(4):
        rows = slice(128 * c, 128 * c + 128)
        applied = gains[rows] * dot(weight[rows], left) - dot(v_full[rows], right)
        next_out[rows] = rot[rows] - 0.5 * step * applied
        pltpu.make_async_copy(next_out.at[rows], next_to.at[rows], local.at[6]).start()

    flush()
    pltpu.make_async_copy(grad_out, grad_to, local.at[5]).wait()
    pltpu.make_async_copy(next_out, next_to, local.at[6]).wait()


def hand_over(grad_in, next_in, grad_to, next_to, held, come, gone):
    pairs = ((grad_in, grad_to), (next_in, next_to))

    def copies(n, c):
        rows = pl.ds(128 * c, 128)
        src, dst = pairs[n]
        here = held.at[n, rows]
        return (
            pltpu.make_async_copy(src.at[rows], here, come.at[n, c]),
            pltpu.make_async_copy(here, dst.at[rows], gone.at[n, c]),
        )

    steps = [copies(n, c) for c in range(4) for n in range(2)]
    for first, _ in steps:
        first.start()
    for first, second in steps:
        first.wait()
        second.start()
    for _, second in steps:
        second.wait()


def shards(residual, norm_gain, value_weight, rotation, target):
    hbm = pl.BlockSpec(memory_space=pltpu.HBM)
    scratch = [
        ((1024, 256), BF16), ((1, 512), F32), ((512, 512), BF16), ((512, 256), F32), ((1024, 512), BF16),
        ((512, 256), F32), ((512, 256), F32),
        ((512, 256), F32),
        ((512, 512), BF16),
        ((512, 256), BF16), ((256, 512), BF16),
        ((1024, 256), BF16), ((256, 1024), BF16),
        ((16, 128), F32), ((16, 128), F32), ((N, 16, 128), F32),
        ((N, 48, 256), BF16), ((N - 1, 48, 256), BF16), ((2, N, 16, 256), BF16), ((2, N, 16, 256), BF16),
        ((8, 128), F32), ((8, 128), F32), ((N, 8, 128), F32),
        ((2, 128, 1024), BF16), ((2, 128, 1024), BF16), ((8, 16, 1024), BF16), ((8, 16, 1024), BF16),
        ((8, 16, 1024), F32), ((7, 16, 1024), BF16),
        ((2 * N, 16, 1024), BF16),
        ((2, N, 16, 256), BF16), ((2, N - 1, 16, 256), BF16), ((2, N, 16, 256), BF16),
        ((2, 128, 512), BF16), ((2, 128, 512), BF16), ((8, 16, 512), BF16), ((8, 16, 512), BF16),
        ((8, 16, 512), F32), ((7, 16, 512), BF16),
        ((2 * N, 16, 512), BF16),
        ((2, N, 16, 256), BF16), ((2, N - 1, 16, 256), BF16), ((2, N, 16, 256), BF16),
        ((8, 128), F32), ((8, 128), F32), ((N, 8, 128), F32), ((N, 8, 128), F32),
        ((N, 8, 128), F32), ((N - 1, 8, 128), F32), ((N, 8, 128), F32), ((2 * N, 16, 512), BF16),
        ((N, 8, 128), F32), ((N - 1, 8, 128), F32), ((N, 8, 128), F32), ((2 * N, 16, 512), BF16),
        ((N, 8, 128), F32), ((N - 1, 8, 128), F32), ((N, 8, 128), F32), ((2 * N, 16, 512), BF16),
    ]
    buffers = [pltpu.VMEM(shape, kind) for shape, kind in scratch]
    results = [jax.ShapeDtypeStruct((512, 256), F32)] * 2
    computed = pl.pallas_call(
        kernel,
        out_shape=results,
        in_specs=[hbm] * 5,
        out_specs=[hbm] * 2,
        scratch_shapes=buffers[:7] + [pltpu.SemaphoreType.DMA((7,))] + buffers[7:]
        + [pltpu.SemaphoreType.DMA((COUNT,)), pltpu.SemaphoreType.DMA((COUNT,))],
        compiler_params=pltpu.CompilerParams(
            collective_id=0, has_side_effects=True, vmem_limit_bytes=LIMIT
        ),
        cost_estimate=pl.CostEstimate(
            flops=2 * 10**9, bytes_accessed=4 * 2**20, transcendentals=0
        ),
    )(residual, norm_gain.reshape(1, -1), value_weight, rotation, target)
    return pl.pallas_call(
        hand_over,
        out_shape=results,
        in_specs=[hbm] * 2,
        out_specs=[hbm] * 2,
        scratch_shapes=[pltpu.VMEM((2, 512, 256), F32)]
        + [pltpu.SemaphoreType.DMA((2, 4))] * 2,
        compiler_params=pltpu.CompilerParams(vmem_limit_bytes=LIMIT),
        cost_estimate=pl.CostEstimate(flops=0, bytes_accessed=2 * 2**20, transcendentals=0),
    )(*computed)


def solution(mesh):
    in_specs = (P("shard", "dp"), P("shard"), P("shard", None), P("shard", "dp"), P("shard", None))
    out_specs = (P("shard", "dp"), P("shard", "dp"))
    return jax.shard_map(
        lambda *a: tuple(shards(*a)), mesh=mesh, in_specs=in_specs, out_specs=out_specs, check_vma=False
    )
```

```python
import math

import jax
import jax.numpy as jnp
from jax import lax
from jax.experimental import pallas as pl
from jax.experimental.pallas import tpu as pltpu
from jax.sharding import PartitionSpec as P

D = 8192
LIMIT = 63 * 2**20
N = 16
MESH = pl.DeviceIdType.MESH
F32 = jnp.float32
BF16 = jnp.bfloat16

SINE = (
    0.9999999944722865,
    -6.579735439437006,
    12.987842893121643,
    -12.207428862935943,
    6.687066146603468,
    -2.366367060643953,
    0.5091905906829214,
)

NN = (((1,), (0,)), ((), ()))
NT = (((1,), (1,)), ((), ()))
TN = (((0,), (0,)), ((), ()))


def dot(a, b, dims=NN):
    return lax.dot_general(a, b, dims, preferred_element_type=F32)


def soft(v):
    r = v - jnp.floor(v + 0.5)
    s = r * r
    p = jnp.full_like(s, SINE[-1])
    for c in SINE[-2::-1]:
        p = p * s + c
    return v - r * p


def twin(a):
    return jnp.concatenate([a, a], axis=1)


(
    STAT_C, STAT_D, Q_R, PEAK_D, W_G, Q_G,
    SQ_C, SQ_D, SQ_S, U_R, U_G, UD_G, UD_C, M_R, M_G, N_R, N_G, W_H,
) = range(18)
OUT, V = 20, 31
OG, VG, MG = 42, 53, 64
G_R, G_G, P_R, P_G = 75, 77, 79, 81
NG = 83
COUNT = 94
FAR = (4, 3, 5, 2, 6, 1, 7)
NEAR = FAR[::-1]


def kernel(
    res_in, gain_in, weight_in, rot_in, target_in, grad_to, next_to,
    res, gain, weight, rot, target, grad_out, next_out, local,
    gains, wt, rb, rb_t, act, act_t, stat, stat_c, stat_d,
    q_send, q_recv, q_all, w_all,
    peak, peak_d,
    out_send, out_c, out_x, out_xr, out_y, out_yr, og_all,
    g_send, g_recv, g_all,
    v_send, v_c, v_x, v_xr, v_y, v_yr, v_all,
    p_send, p_recv, p_all,
    sq, sq_c, sq_d, sq_s,
    u_send, u_recv, u_part, u_all,
    m_send, m_recv, m_part, m_all,
    n_send, n_recv, n_part, n_all,
    sends, recvs,
):
    dp, me = lax.axis_index("dp"), lax.axis_index("shard")
    chip, core = lax.div(dp, 2), lax.rem(dp, 2)
    y, xl = lax.div(chip, 2), lax.rem(chip, 2)
    other, xo = 1 - core, 1 - xl
    slot = core * N + xl * 8 + y
    twin_id = (chip * 2 + other, me)
    x_id = ((y * 2 + xo) * 2 + core, me)

    loads = []
    for n, (src, dst) in enumerate(
        ((weight_in, weight), (rot_in, rot), (gain_in, gain), (res_in, res), (target_in, target))
    ):
        rows = src.shape[0]
        cuts = 4 if rows > 1 else 1
        for c in range(cuts):
            part = pl.ds(c * (rows // cuts), rows // cuts)
            pltpu.make_async_copy(src.at[part], dst.at[part], local.at[n]).start()
        loads.append(pltpu.make_async_copy(src, dst, local.at[n]))

    def y_id(k):
        return ((lax.rem(y + k, 8) * 2 + xl) * 2 + core, me)

    def shard_id(k):
        return lax.rem(me + k, N)

    def chip_id(k):
        return lax.rem(chip + k, N)

    def shard_dev(k):
        return (dp, shard_id(k))

    def chip_dev(k):
        return (chip_id(k) * 2 + core, me)

    def each(body):
        def step(k, _):
            body(k)
            return 0

        lax.fori_loop(1, N, step, 0, unroll=True)

    def start(src, dst, which, device):
        pltpu.make_async_remote_copy(
            src_ref=src, dst_ref=dst, send_sem=sends.at[which], recv_sem=recvs.at[which],
            device_id=device, device_id_type=MESH,
        ).start()

    sent = []

    def arrived(ref, which):
        pltpu.make_async_copy(ref, ref, recvs.at[which]).wait()
        sent.append((ref, which))

    def flush():
        for ref, which in sent:
            pltpu.make_async_copy(ref, ref, sends.at[which]).wait()
        sent.clear()

    def scatter(src, dst, which):
        each(lambda k: start(src.at[shard_id(k)], dst.at[k - 1], which, shard_dev(k)))

    def spread(ref, which, device):
        each(lambda k: start(ref, ref, which, device(k)))

    def to_twin(src, dst, which):
        start(src, dst, which, twin_id)

    def reduce_dp(part, send, from_twin, x_send, x_recv, y_send, y_recv, base, between, ready, own_first):
        width = send.shape[2]
        if own_first:
            own = [part(core, xo), part(core, xl)]
            ready()
        for n, h in enumerate((xo, xl)):
            send[n] = part(other, h).astype(BF16)
            to_twin(send.at[n], from_twin.at[n], base + n)
        if not own_first:
            ready()
            own = [part(core, xo), part(core, xl)]
        arrived(from_twin.at[0], base)
        both = own[0] + from_twin[0].astype(F32)
        x_send[...] = both.astype(BF16).reshape(8, 16, width)
        for k in FAR + (0,):
            start(x_send.at[lax.rem(y + k, 8)], x_recv.at[k], base + 2 + k, x_id)
        arrived(from_twin.at[1], base + 1)
        both = own[1] + from_twin[1].astype(F32)
        y_send[...] = both.reshape(8, 16, width)
        for k in FAR:
            arrived(x_recv.at[k], base + 2 + k)
            x_recv[k] = (y_send[lax.rem(y + k, 8)] + x_recv[k].astype(F32)).astype(BF16)
            start(x_recv.at[k], y_recv.at[k - 1], base + 10, y_id(k))
        between()
        arrived(x_recv.at[0], base + 2)
        acc = y_send[y] + x_recv[0].astype(F32)
        arrived(y_recv, base + 10)
        for k in range(7):
            acc = acc + y_recv[k].astype(F32)
        return acc

    def gather_y(ref, base):
        own = ref.at[slot]
        for k in FAR:
            start(own, own, base + k, y_id(k))
        start(own, own, base + 8, x_id)

    def gather_x(ref, base):
        for k in NEAR:
            block = ref.at[core * N + xl * 8 + lax.rem(y + 8 - k, 8)]
            arrived(block, base + k)
            start(block, block, base + 8, x_id)

    def gather_direct(ref, base):
        own = ref.at[slot]
        for k in FAR:
            start(own, own, base + 1, y_id(k))
        for k in FAR + (0,):
            start(own, own, base + 8, ((lax.rem(y + k, 8) * 2 + xo) * 2 + core, me))

    def arrived_near(ref, base):
        arrived(ref.at[pl.ds(0, 7)], base + 1)

    def gather_near(ref, base):
        near = ref.at[pl.ds(core * N + xl * 8, 8)]
        to_twin(near, near, base + 9)

    def gather_far(ref, base):
        far = ref.at[pl.ds(core * N + xo * 8, 8)]
        arrived(far, base + 8)
        to_twin(far, far, base + 10)

    def gather_other(ref, base):
        arrived(ref.at[pl.ds(0, 8)], base + 9)
        arrived(ref.at[pl.ds(0, 8)], base + 10)

    def gather_and_send(ref, base, make, src, dst, which):
        gather_near(ref, base)
        make(core, xl)
        send_quarter(src, dst, which, core, xl)
        gather_far(ref, base)
        make(core, xo)
        send_quarter(src, dst, which, core, xo)
        arrived(ref.at[pl.ds(0, 8)], base + 9)
        make(other, xl)
        send_quarter(src, dst, which + 1, other, xl)
        arrived(ref.at[pl.ds(0, 8)], base + 10)

    def total(own, recv):
        acc = own.astype(F32)
        for k in range(N - 1):
            acc = acc + recv[k].astype(F32)
        return acc

    barrier = pltpu.get_barrier_semaphore()
    pl.semaphore_signal(barrier, inc=1, device_id=twin_id, device_id_type=MESH)

    def greet(k):
        pl.semaphore_signal(barrier, inc=1, device_id=shard_dev(k), device_id_type=MESH)
        pl.semaphore_signal(barrier, inc=1, device_id=chip_dev(k), device_id_type=MESH)
        there = (chip_id(k) * 2 + other, me)
        pl.semaphore_signal(barrier, inc=1, device_id=there, device_id_type=MESH)

    each(greet)

    loads[0].wait()
    loads[2].wait()
    wt[...] = weight[...].astype(F32).T.astype(BF16)
    norm = gain[...] * (1.0 / math.sqrt(D))
    for c in range(4):
        rows = slice(128 * c, 128 * c + 128)
        gains[rows] = twin(jnp.broadcast_to(norm[:, rows], (128, 128)).T)
    loads[1].wait()
    scaled = rot[...] * gains[...]
    first = scaled.astype(BF16)
    second = (scaled - first.astype(F32)).astype(BF16)
    q = (dot(wt[...], first) + dot(wt[...], second)).reshape(2, N, 16, 256)
    high = q.astype(BF16)
    q_send[:, :16] = high[0]
    q_send[:, 16:32] = high[1]
    high = high.astype(F32)
    rest = jnp.floor((q - high) * (15 * 256.0) / (jnp.abs(high) + 1e-30) + 0.5)
    rest = jnp.clip(rest, -7.0, 7.0)
    q_send[:, 32:] = (rest[0] * 16.0 + rest[1]).astype(BF16)
    pl.semaphore_wait(barrier, 3 * N - 2)
    scatter(q_send, q_recv, Q_R)

    loads[3].wait()
    for k in range(8):
        h = res[128 * k : 128 * k + 128, :].astype(F32)
        a, b = h[:, :128], h[:, 128:]
        stat[k : k + 1, :] = jnp.sum((a * a + b * b).T, axis=0, keepdims=True)
        stat[8 + k : 9 + k, :] = jnp.max(
            jnp.maximum(jnp.abs(a), jnp.abs(b)).T, axis=0, keepdims=True
        )
    to_twin(stat, stat_c, STAT_C)
    rb[...] = rot[...].astype(BF16)
    stb = (wt[...].astype(F32) * norm).astype(BF16)
    mine = wt[pl.ds(pl.multiple_of(slot * 16, 16), 16), :].astype(F32) * norm
    u_gram = dot(mine.astype(BF16), stb, NT)
    for h in range(2):
        for b in range(4):
            block = u_gram[8 * h : 8 * h + 8, 128 * b : 128 * b + 128]
            u_send[8 * h + b] = block
            u_send[8 * h + 4 + b] = block
    arrived(stat_c, STAT_C)

    def combine(a, b):
        return jnp.concatenate([a[:8] + b[:8], jnp.maximum(a[8:], b[8:])], axis=0)

    both = combine(stat[...], stat_c[...])
    stat_d[0] = both
    each(lambda k: start(stat_d.at[0], stat_d.at[k], STAT_D, chip_dev(k)))

    arrived(q_recv, Q_R)

    def decode(a):
        high, rest = a[:32].astype(F32), a[32:].astype(F32)
        upper = jnp.floor(rest * 0.0625 + 0.5)
        rest = jnp.concatenate([upper, rest - 16.0 * upper], axis=0)
        return high + rest * (jnp.abs(high) * (1.0 / (15 * 256)))

    q_mine = decode(q_send[me])
    for k in range(N - 1):
        q_mine = q_mine + decode(q_recv[k])
    top = jnp.maximum(jnp.abs(q_mine[:, :128]), jnp.abs(q_mine[:, 128:]))
    top = jnp.max(jnp.concatenate([top] * 4, axis=0).T, axis=0, keepdims=True)
    peak[...] = jnp.broadcast_to(top, (8, 128))
    row = peak.at[pl.ds(0, 1)]
    for k in range(N):
        there = chip_id(k) * 2 + other
        start(row, peak_d.at[N + k, pl.ds(0, 1)], PEAK_D, (there, me))
    each(lambda k: start(row, peak_d.at[k, pl.ds(0, 1)], PEAK_D, chip_dev(k)))

    arrived(stat_d.at[pl.ds(1, N - 1)], STAT_D)
    for k in range(1, N):
        both = combine(both, stat_d[k])
    row_peak = both[8:] + 1e-06
    inv_rms = lax.rsqrt(both[:8] / D + 1e-05)
    rows_in = 7.0 / row_peak
    rows_out = row_peak * inv_rms / 7.0

    for k in range(8):
        into = twin(jnp.broadcast_to(rows_in[k : k + 1, :], (128, 128)).T)
        outof = twin(jnp.broadcast_to(rows_out[k : k + 1, :], (128, 128)).T)
        h = res[128 * k : 128 * k + 128, :].astype(F32)
        act[128 * k : 128 * k + 128, :] = (outof * soft(into * h)).astype(BF16)

    arrived(peak_d.at[pl.ds(1, 2 * N - 1), pl.ds(0, 1)], PEAK_D)
    for k in range(1, 2 * N):
        top = jnp.maximum(top, peak_d[k, :1, :])
    column = jnp.broadcast_to(top, (128, 128)).T[:32, :]
    scale = twin((column + 1e-06) / 7.0)
    w_all[:, me] = (scale * soft(q_mine / scale)).astype(BF16).reshape(2, 16, 256)
    spread(w_all.at[other, me], W_G, shard_dev)
    spread(w_all.at[core, me], W_H, shard_dev)
    q_all[:, me] = q_mine.astype(BF16).reshape(2, 16, 256)
    scatter(u_send, u_recv, U_R)

    act_t[...] = act[...].astype(F32).T.astype(BF16)
    rb_t[...] = rot[...].T.astype(BF16)
    loads[4].wait()
    wanted = slot * 16 + lax.broadcasted_iota(jnp.int32, (16, 512), 0)
    one_hot = jnp.where(lax.broadcasted_iota(jnp.int32, (16, 512), 1) == wanted, 1.0, 0.0)
    target_mine = dot(one_hot.astype(BF16), target[...], NT)

    arrived(w_all.at[0, pl.ds(0, N - 1)], W_G)

    def quarter(ref, c, h):
        return ref[c, pl.ds(h * 8, 8)].reshape(128, 256)

    def weight_gram():
        arrived(u_recv, U_R)
        u_part[me] = total(u_send[me], u_recv)
        spread(u_part.at[me], U_G, shard_dev)

    out_mine = reduce_dp(
        lambda c, h: dot(quarter(w_all, c, h), act_t[...]),
        out_send, out_c, out_x, out_xr, out_y, out_yr, OUT, weight_gram,
        lambda: arrived(w_all.at[0, pl.ds(0, N - 1)], W_H), False,
    )
    og_all[slot] = (out_mine - target_mine).astype(BF16)
    gather_y(og_all, OG)
    gather_x(og_all, OG)

    def send_quarter(src, dst, which, c, h):
        def step(j, _):
            to = h * 8 + j

            @pl.when(to != me)
            def _():
                k = lax.rem(to + N - me, N)
                start(src.at[c, to], dst.at[c, k - 1], which, (dp, to))

            return 0

        lax.fori_loop(0, 8, step, 0, unroll=True)

    def share_half(src, recv, ref, which, after, c):
        arrived(recv.at[c], which)
        acc = src[c, me].astype(F32)
        for k in range(N - 1):
            acc = acc + recv[c, k].astype(F32)
        ref[c, me] = acc.astype(BF16)
        spread(ref.at[c, me], after, shard_dev)

    def g_part(c, h):
        og = og_all[pl.ds(c * N + h * 8, 8)].reshape(128, 1024)
        g_send[c, pl.ds(h * 8, 8)] = dot(og, act[...]).astype(BF16).reshape(8, 16, 256)

    gather_and_send(og_all, OG, g_part, g_send, g_recv, G_R)
    g_part(other, xo)
    send_quarter(g_send, g_recv, G_R + 1, other, xo)

    def assemble(part, count):
        rows = [
            jnp.concatenate([part[8 * h + b] for b in range(count)], axis=1)
            for h in range(2)
        ]
        return jnp.concatenate(rows, axis=0).astype(BF16)

    def to_twin_half(ref, which):
        half = ref.at[pl.ds(core * N, N)]
        to_twin(half, half, which)

    arrived(u_part.at[pl.ds(0, N - 1)], U_G)
    u_all[slot] = assemble(u_part, 4)
    spread(u_all.at[slot], UD_G, chip_dev)
    share_half(g_send, g_recv, g_all, G_R, G_G, core)
    share_half(g_send, g_recv, g_all, G_R + 1, G_G + 1, other)
    arrived(u_all.at[pl.ds(0, N - 1)], UD_G)
    to_twin_half(u_all, UD_C)

    def gradient():
        spread(q_all.at[:, me], Q_G, shard_dev)
        g_full = g_all[...].reshape(512, 256)
        grad = gains[...] * dot(weight[...], g_full)
        grad_out[...] = grad
        pltpu.make_async_copy(grad_out, grad_to, local.at[5]).start()
        square = jnp.sum((grad * grad).reshape(64, 8, 256), axis=0)
        sq[...] = square[:, :128] + square[:, 128:]
        to_twin(sq, sq_c, SQ_C)

    arrived(g_all.at[0, pl.ds(0, N - 1)], G_G)
    v_mine = reduce_dp(
        lambda c, h: dot(quarter(g_all, c, h), rb_t[...]),
        v_send, v_c, v_x, v_xr, v_y, v_yr, V, gradient,
        lambda: arrived(g_all.at[0, pl.ds(0, N - 1)], G_G + 1), True,
    ).astype(BF16)
    v_all[slot] = v_mine

    def blocks(ref, gram):
        for h in range(2):
            for b in range(8):
                block = 128 * (b % 4)
                ref[8 * h + b] = gram[8 * h : 8 * h + 8, block : block + 128]

    gather_direct(v_all, VG)
    blocks(n_send, dot(v_mine, stb, NT))
    scatter(n_send, n_recv, N_R)
    arrived_near(v_all, VG)
    arrived(n_recv, N_R)
    n_part[me] = total(n_send[me], n_recv)
    spread(n_part.at[me], N_G, shard_dev)

    def p_part(c, h):
        block = v_all[pl.ds(c * N + h * 8, 8)].reshape(128, 512)
        p_send[c, pl.ds(h * 8, 8)] = dot(block, rb[...]).astype(BF16).reshape(8, 16, 256)

    gather_and_send(v_all, VG, p_part, p_send, p_recv, P_R)
    vt = v_all[...].reshape(512, 512)
    blocks(m_send, dot(v_mine, vt, NT))
    scatter(m_send, m_recv, M_R)
    p_part(other, xo)
    send_quarter(p_send, p_recv, P_R + 1, other, xo)
    arrived(sq_c, SQ_C)
    sq_d[0] = sq[...] + sq_c[...]
    each(lambda k: start(sq_d.at[0], sq_d.at[k], SQ_D, chip_dev(k)))

    arrived(n_part.at[pl.ds(0, N - 1)], N_G)
    n_all[slot] = assemble(n_part, 4)
    gather_direct(n_all, NG)
    arrived(m_recv, M_R)
    m_part[me] = total(m_send[me], m_recv)
    spread(m_part.at[me], M_G, shard_dev)
    flush()
    share_half(p_send, p_recv, p_all, P_R, P_G, core)
    arrived_near(n_all, NG)
    arrived(sq_d.at[pl.ds(1, N - 1)], SQ_D)
    square = sq_d[0]
    for k in range(1, N):
        square = square + sq_d[k]
    sq_s[0] = square
    each(lambda k: start(sq_s.at[0], sq_s.at[k], SQ_S, shard_dev(k)))
    share_half(p_send, p_recv, p_all, P_R + 1, P_G + 1, other)
    arrived(m_part.at[pl.ds(0, N - 1)], M_G)
    m_all[slot] = assemble(m_part, 4)
    gather_direct(m_all, MG)
    gather_near(n_all, NG)
    gather_far(n_all, NG)
    v_full = vt.astype(F32).T.astype(BF16)
    arrived_near(m_all, MG)
    gather_near(m_all, MG)
    gather_far(m_all, MG)

    arrived(sq_s.at[pl.ds(1, N - 1)], SQ_S)
    for k in range(1, N):
        square = square + sq_s[k]
    square = jnp.sum(jnp.sum(square, axis=1, keepdims=True), axis=0, keepdims=True)
    step = 0.4 * math.sqrt(512) * lax.rsqrt(D * square + 1e-06)
    arrived(u_all.at[pl.ds(0, N)], UD_C)
    arrived(q_all.at[:, pl.ds(0, N - 1)], Q_G)
    q_full = q_all[...].reshape(512, 256)
    uu = u_all[...].reshape(512, 512)
    gather_other(n_all, NG)
    vu = n_all[...].reshape(512, 512)
    right = 2.0 * q_full.astype(F32) + step * dot(vu, q_full, TN)
    flush()
    gather_other(m_all, MG)
    vv = m_all[...].reshape(512, 512)
    left = step * dot(vv, q_full)
    arrived(p_all.at[0, pl.ds(0, N - 1)], P_G)
    arrived(p_all.at[0, pl.ds(0, N - 1)], P_G + 1)
    p_full = p_all[...].reshape(512, 256)
    left = left + 2.0 * p_full.astype(F32) - step * dot(vu, p_full)
    right = right - step * dot(uu, p_full)
    left, right = left.astype(BF16), right.astype(BF16)
    for c in range(4):
        rows = slice(128 * c, 128 * c + 128)
        applied = gains[rows] * dot(weight[rows], left) - dot(v_full[rows], right)
        next_out[rows] = rot[rows] - 0.5 * step * applied
        pltpu.make_async_copy(next_out.at[rows], next_to.at[rows], local.at[6]).start()

    flush()
    pltpu.make_async_copy(grad_out, grad_to, local.at[5]).wait()
    pltpu.make_async_copy(next_out, next_to, local.at[6]).wait()


def hand_over(grad_in, next_in, grad_to, next_to, held, come, gone):
    pairs = ((grad_in, grad_to), (next_in, next_to))

    def copies(n, c):
        rows = pl.ds(128 * c, 128)
        src, dst = pairs[n]
        here = held.at[n, rows]
        return (
            pltpu.make_async_copy(src.at[rows], here, come.at[n, c]),
            pltpu.make_async_copy(here, dst.at[rows], gone.at[n, c]),
        )

    steps = [copies(n, c) for c in range(4) for n in range(2)]
    for first, _ in steps:
        first.start()
    for first, second in steps:
        first.wait()
        second.start()
    for _, second in steps:
        second.wait()


def shards(residual, norm_gain, value_weight, rotation, target):
    hbm = pl.BlockSpec(memory_space=pltpu.HBM)
    scratch = [
        ((1024, 256), BF16), ((1, 512), F32), ((512, 512), BF16), ((512, 256), F32), ((1024, 512), BF16),
        ((512, 256), F32), ((512, 256), F32),
        ((512, 256), F32),
        ((512, 512), BF16),
        ((512, 256), BF16), ((256, 512), BF16),
        ((1024, 256), BF16), ((256, 1024), BF16),
        ((16, 128), F32), ((16, 128), F32), ((N, 16, 128), F32),
        ((N, 48, 256), BF16), ((N - 1, 48, 256), BF16), ((2, N, 16, 256), BF16), ((2, N, 16, 256), BF16),
        ((8, 128), F32), ((2 * N, 8, 128), F32),
        ((2, 128, 1024), BF16), ((2, 128, 1024), BF16), ((8, 16, 1024), BF16), ((8, 16, 1024), BF16),
        ((8, 16, 1024), F32), ((7, 16, 1024), BF16),
        ((2 * N, 16, 1024), BF16),
        ((2, N, 16, 256), BF16), ((2, N - 1, 16, 256), BF16), ((2, N, 16, 256), BF16),
        ((2, 128, 512), BF16), ((2, 128, 512), BF16), ((8, 16, 512), BF16), ((8, 16, 512), BF16),
        ((8, 16, 512), F32), ((7, 16, 512), BF16),
        ((2 * N, 16, 512), BF16),
        ((2, N, 16, 256), BF16), ((2, N - 1, 16, 256), BF16), ((2, N, 16, 256), BF16),
        ((8, 128), F32), ((8, 128), F32), ((N, 8, 128), F32), ((N, 8, 128), F32),
        ((N, 8, 128), F32), ((N - 1, 8, 128), F32), ((N, 8, 128), F32), ((2 * N, 16, 512), BF16),
        ((N, 8, 128), F32), ((N - 1, 8, 128), F32), ((N, 8, 128), F32), ((2 * N, 16, 512), BF16),
        ((N, 8, 128), F32), ((N - 1, 8, 128), F32), ((N, 8, 128), F32), ((2 * N, 16, 512), BF16),
    ]
    buffers = [pltpu.VMEM(shape, kind) for shape, kind in scratch]
    results = [jax.ShapeDtypeStruct((512, 256), F32)] * 2
    computed = pl.pallas_call(
        kernel,
        out_shape=results,
        in_specs=[hbm] * 5,
        out_specs=[hbm] * 2,
        scratch_shapes=buffers[:7] + [pltpu.SemaphoreType.DMA((7,))] + buffers[7:]
        + [pltpu.SemaphoreType.DMA((COUNT,)), pltpu.SemaphoreType.DMA((COUNT,))],
        compiler_params=pltpu.CompilerParams(
            collective_id=0, has_side_effects=True, vmem_limit_bytes=LIMIT
        ),
        cost_estimate=pl.CostEstimate(
            flops=2 * 10**9, bytes_accessed=4 * 2**20, transcendentals=0
        ),
    )(residual, norm_gain.reshape(1, -1), value_weight, rotation, target)
    return pl.pallas_call(
        hand_over,
        out_shape=results,
        in_specs=[hbm] * 2,
        out_specs=[hbm] * 2,
        scratch_shapes=[pltpu.VMEM((2, 512, 256), F32)]
        + [pltpu.SemaphoreType.DMA((2, 4))] * 2,
        compiler_params=pltpu.CompilerParams(vmem_limit_bytes=LIMIT),
        cost_estimate=pl.CostEstimate(flops=0, bytes_accessed=2 * 2**20, transcendentals=0),
    )(*computed)


def solution(mesh):
    in_specs = (P("shard", "dp"), P("shard"), P("shard", None), P("shard", "dp"), P("shard", None))
    out_specs = (P("shard", "dp"), P("shard", "dp"))
    return jax.shard_map(
        lambda *a: tuple(shards(*a)), mesh=mesh, in_specs=in_specs, out_specs=out_specs, check_vma=False
    )
```

```python
import math

import jax
import jax.numpy as jnp
from jax import lax
from jax.experimental import pallas as pl
from jax.experimental.pallas import tpu as pltpu
from jax.sharding import PartitionSpec as P

D = 8192
LIMIT = 63 * 2**20
N = 16
MESH = pl.DeviceIdType.MESH
F32 = jnp.float32
BF16 = jnp.bfloat16

SINE = (
    0.9999999944722865,
    -6.579735439437006,
    12.987842893121643,
    -12.207428862935943,
    6.687066146603468,
    -2.366367060643953,
    0.5091905906829214,
)

NN = (((1,), (0,)), ((), ()))
NT = (((1,), (1,)), ((), ()))
TN = (((0,), (0,)), ((), ()))


def dot(a, b, dims=NN):
    return lax.dot_general(a, b, dims, preferred_element_type=F32)


def soft(v):
    r = v - jnp.floor(v + 0.5)
    s = r * r
    p = jnp.full_like(s, SINE[-1])
    for c in SINE[-2::-1]:
        p = p * s + c
    return v - r * p


def twin(a):
    return jnp.concatenate([a, a], axis=1)


(
    STAT_C, STAT_D, Q_R, PEAK_D, W_G, Q_G,
    SQ_C, SQ_D, SQ_S, U_R, U_G, UD_G, UD_C, M_R, M_G, N_R, N_G, W_H,
) = range(18)
OUT, V = 20, 31
OG, VG, MG = 42, 53, 64
G_R, G_G, P_R, P_G = 75, 77, 79, 81
NG = 83
COUNT = 94
FAR = (4, 3, 5, 2, 6, 1, 7)
NEAR = FAR[::-1]
ORDER = (8, 9, 7, 10, 6, 11, 5, 12, 4, 13, 3, 14, 2, 15, 1)


def kernel(
    res_in, gain_in, weight_in, rot_in, target_in, grad_to, next_to,
    res, gain, weight, rot, target, grad_out, next_out, local,
    gains, wt, rb, rb_t, act, act_t, stat, stat_c, stat_d,
    q_send, q_recv, q_all, w_all,
    peak, peak_d,
    out_send, out_c, out_x, out_xr, out_y, out_yr, og_all,
    g_send, g_recv, g_all,
    v_send, v_c, v_x, v_xr, v_y, v_yr, v_all,
    p_send, p_recv, p_all,
    sq, sq_c, sq_d, sq_s,
    u_send, u_recv, u_part, u_all,
    m_send, m_recv, m_part, m_all,
    n_send, n_recv, n_part, n_all,
    sends, recvs,
):
    dp, me = lax.axis_index("dp"), lax.axis_index("shard")
    chip, core = lax.div(dp, 2), lax.rem(dp, 2)
    y, xl = lax.div(chip, 2), lax.rem(chip, 2)
    other, xo = 1 - core, 1 - xl
    slot = core * N + xl * 8 + y
    twin_id = (chip * 2 + other, me)
    x_id = ((y * 2 + xo) * 2 + core, me)

    loads = []
    for n, (src, dst) in enumerate(
        ((weight_in, weight), (rot_in, rot), (gain_in, gain), (res_in, res), (target_in, target))
    ):
        rows = src.shape[0]
        cuts = 4 if rows > 1 else 1
        for c in range(cuts):
            part = pl.ds(c * (rows // cuts), rows // cuts)
            pltpu.make_async_copy(src.at[part], dst.at[part], local.at[n]).start()
        loads.append(pltpu.make_async_copy(src, dst, local.at[n]))

    def y_id(k):
        return ((lax.rem(y + k, 8) * 2 + xl) * 2 + core, me)

    def shard_id(k):
        return lax.rem(me + k, N)

    def chip_id(k):
        return lax.rem(chip + k, N)

    def shard_dev(k):
        return (dp, shard_id(k))

    def chip_dev(k):
        return (chip_id(k) * 2 + core, me)

    def each(body):
        for k in ORDER:
            body(k)

    def start(src, dst, which, device):
        pltpu.make_async_remote_copy(
            src_ref=src, dst_ref=dst, send_sem=sends.at[which], recv_sem=recvs.at[which],
            device_id=device, device_id_type=MESH,
        ).start()

    sent = []

    def arrived(ref, which):
        pltpu.make_async_copy(ref, ref, recvs.at[which]).wait()
        sent.append((ref, which))

    def flush():
        for ref, which in sent:
            pltpu.make_async_copy(ref, ref, sends.at[which]).wait()
        sent.clear()

    def scatter(src, dst, which):
        each(lambda k: start(src.at[shard_id(k)], dst.at[k - 1], which, shard_dev(k)))

    def spread(ref, which, device):
        each(lambda k: start(ref, ref, which, device(k)))

    def to_twin(src, dst, which):
        start(src, dst, which, twin_id)

    def reduce_dp(part, send, from_twin, x_send, x_recv, y_send, y_recv, base, between, ready, own_first):
        width = send.shape[2]
        if own_first:
            own = [part(core, xo), part(core, xl)]
            ready()
        for n, h in enumerate((xo, xl)):
            send[n] = part(other, h).astype(BF16)
            to_twin(send.at[n], from_twin.at[n], base + n)
        if not own_first:
            ready()
            own = [part(core, xo), part(core, xl)]
        arrived(from_twin.at[0], base)
        both = own[0] + from_twin[0].astype(F32)
        x_send[...] = both.astype(BF16).reshape(8, 16, width)
        for k in FAR + (0,):
            start(x_send.at[lax.rem(y + k, 8)], x_recv.at[k], base + 2 + k, x_id)
        arrived(from_twin.at[1], base + 1)
        both = own[1] + from_twin[1].astype(F32)
        y_send[...] = both.reshape(8, 16, width)
        for k in FAR:
            arrived(x_recv.at[k], base + 2 + k)
            x_recv[k] = (y_send[lax.rem(y + k, 8)] + x_recv[k].astype(F32)).astype(BF16)
            start(x_recv.at[k], y_recv.at[k - 1], base + 10, y_id(k))
        between()
        arrived(x_recv.at[0], base + 2)
        acc = y_send[y] + x_recv[0].astype(F32)
        arrived(y_recv, base + 10)
        for k in range(7):
            acc = acc + y_recv[k].astype(F32)
        return acc

    def gather_y(ref, base):
        own = ref.at[slot]
        for k in FAR:
            start(own, own, base + k, y_id(k))
        start(own, own, base + 8, x_id)

    def gather_x(ref, base):
        for k in NEAR:
            block = ref.at[core * N + xl * 8 + lax.rem(y + 8 - k, 8)]
            arrived(block, base + k)
            start(block, block, base + 8, x_id)

    def gather_direct(ref, base):
        own = ref.at[slot]
        for k in FAR:
            start(own, own, base + 1, y_id(k))
        for k in FAR + (0,):
            start(own, own, base + 8, ((lax.rem(y + k, 8) * 2 + xo) * 2 + core, me))

    def arrived_near(ref, base):
        arrived(ref.at[pl.ds(0, 7)], base + 1)

    def gather_near(ref, base):
        near = ref.at[pl.ds(core * N + xl * 8, 8)]
        to_twin(near, near, base + 9)

    def gather_far(ref, base):
        far = ref.at[pl.ds(core * N + xo * 8, 8)]
        arrived(far, base + 8)
        to_twin(far, far, base + 10)

    def gather_other(ref, base):
        arrived(ref.at[pl.ds(0, 8)], base + 9)
        arrived(ref.at[pl.ds(0, 8)], base + 10)

    def gather_and_send(ref, base, make, src, dst, which):
        gather_near(ref, base)
        make(core, xl)
        send_quarter(src, dst, which, core, xl)
        gather_far(ref, base)
        make(core, xo)
        send_quarter(src, dst, which, core, xo)
        arrived(ref.at[pl.ds(0, 8)], base + 9)
        make(other, xl)
        send_quarter(src, dst, which + 1, other, xl)
        arrived(ref.at[pl.ds(0, 8)], base + 10)

    def total(own, recv):
        acc = own.astype(F32)
        for k in range(N - 1):
            acc = acc + recv[k].astype(F32)
        return acc

    barrier = pltpu.get_barrier_semaphore()
    pl.semaphore_signal(barrier, inc=1, device_id=twin_id, device_id_type=MESH)

    def greet(k):
        pl.semaphore_signal(barrier, inc=1, device_id=shard_dev(k), device_id_type=MESH)
        pl.semaphore_signal(barrier, inc=1, device_id=chip_dev(k), device_id_type=MESH)
        there = (chip_id(k) * 2 + other, me)
        pl.semaphore_signal(barrier, inc=1, device_id=there, device_id_type=MESH)

    each(greet)

    loads[0].wait()
    loads[2].wait()
    wt[...] = weight[...].astype(F32).T.astype(BF16)
    norm = gain[...] * (1.0 / math.sqrt(D))
    for c in range(4):
        rows = slice(128 * c, 128 * c + 128)
        gains[rows] = twin(jnp.broadcast_to(norm[:, rows], (128, 128)).T)
    loads[1].wait()
    scaled = rot[...] * gains[...]
    first = scaled.astype(BF16)
    second = (scaled - first.astype(F32)).astype(BF16)
    q = (dot(wt[...], first) + dot(wt[...], second)).reshape(2, N, 16, 256)
    high = q.astype(BF16)
    q_send[:, :16] = high[0]
    q_send[:, 16:32] = high[1]
    high = high.astype(F32)
    rest = jnp.floor((q - high) * (15 * 256.0) / (jnp.abs(high) + 1e-30) + 0.5)
    rest = jnp.clip(rest, -7.0, 7.0)
    q_send[:, 32:] = (rest[0] * 16.0 + rest[1]).astype(BF16)
    pl.semaphore_wait(barrier, 3 * N - 2)
    scatter(q_send, q_recv, Q_R)

    loads[3].wait()
    for k in range(8):
        h = res[128 * k : 128 * k + 128, :].astype(F32)
        a, b = h[:, :128], h[:, 128:]
        stat[k : k + 1, :] = jnp.sum((a * a + b * b).T, axis=0, keepdims=True)
        stat[8 + k : 9 + k, :] = jnp.max(
            jnp.maximum(jnp.abs(a), jnp.abs(b)).T, axis=0, keepdims=True
        )
    to_twin(stat, stat_c, STAT_C)
    rb[...] = rot[...].astype(BF16)
    stb = (wt[...].astype(F32) * norm).astype(BF16)
    mine = wt[pl.ds(pl.multiple_of(slot * 16, 16), 16), :].astype(F32) * norm
    u_gram = dot(mine.astype(BF16), stb, NT)
    for h in range(2):
        for b in range(4):
            block = u_gram[8 * h : 8 * h + 8, 128 * b : 128 * b + 128]
            u_send[8 * h + b] = block
            u_send[8 * h + 4 + b] = block
    arrived(stat_c, STAT_C)

    def combine(a, b):
        return jnp.concatenate([a[:8] + b[:8], jnp.maximum(a[8:], b[8:])], axis=0)

    both = combine(stat[...], stat_c[...])
    stat_d[0] = both
    each(lambda k: start(stat_d.at[0], stat_d.at[k], STAT_D, chip_dev(k)))

    arrived(q_recv, Q_R)

    def decode(a):
        high, rest = a[:32].astype(F32), a[32:].astype(F32)
        upper = jnp.floor(rest * 0.0625 + 0.5)
        rest = jnp.concatenate([upper, rest - 16.0 * upper], axis=0)
        return high + rest * (jnp.abs(high) * (1.0 / (15 * 256)))

    q_mine = decode(q_send[me])
    for k in range(N - 1):
        q_mine = q_mine + decode(q_recv[k])
    top = jnp.maximum(jnp.abs(q_mine[:, :128]), jnp.abs(q_mine[:, 128:]))
    top = jnp.max(jnp.concatenate([top] * 4, axis=0).T, axis=0, keepdims=True)
    peak[...] = jnp.broadcast_to(top, (8, 128))
    row = peak.at[pl.ds(0, 1)]
    for k in range(N):
        there = chip_id(k) * 2 + other
        start(row, peak_d.at[N + k, pl.ds(0, 1)], PEAK_D, (there, me))
    each(lambda k: start(row, peak_d.at[k, pl.ds(0, 1)], PEAK_D, chip_dev(k)))

    arrived(stat_d.at[pl.ds(1, N - 1)], STAT_D)
    for k in range(1, N):
        both = combine(both, stat_d[k])
    row_peak = both[8:] + 1e-06
    inv_rms = lax.rsqrt(both[:8] / D + 1e-05)
    rows_in = 7.0 / row_peak
    rows_out = row_peak * inv_rms / 7.0

    for k in range(8):
        into = twin(jnp.broadcast_to(rows_in[k : k + 1, :], (128, 128)).T)
        outof = twin(jnp.broadcast_to(rows_out[k : k + 1, :], (128, 128)).T)
        h = res[128 * k : 128 * k + 128, :].astype(F32)
        act[128 * k : 128 * k + 128, :] = (outof * soft(into * h)).astype(BF16)

    arrived(peak_d.at[pl.ds(1, 2 * N - 1), pl.ds(0, 1)], PEAK_D)
    for k in range(1, 2 * N):
        top = jnp.maximum(top, peak_d[k, :1, :])
    column = jnp.broadcast_to(top, (128, 128)).T[:32, :]
    scale = twin((column + 1e-06) / 7.0)
    w_all[:, me] = (scale * soft(q_mine / scale)).astype(BF16).reshape(2, 16, 256)
    spread(w_all.at[other, me], W_G, shard_dev)
    spread(w_all.at[core, me], W_H, shard_dev)
    q_all[:, me] = q_mine.astype(BF16).reshape(2, 16, 256)
    scatter(u_send, u_recv, U_R)

    act_t[...] = act[...].astype(F32).T.astype(BF16)
    rb_t[...] = rot[...].T.astype(BF16)
    loads[4].wait()
    wanted = slot * 16 + lax.broadcasted_iota(jnp.int32, (16, 512), 0)
    one_hot = jnp.where(lax.broadcasted_iota(jnp.int32, (16, 512), 1) == wanted, 1.0, 0.0)
    target_mine = dot(one_hot.astype(BF16), target[...], NT)

    arrived(w_all.at[0, pl.ds(0, N - 1)], W_G)

    def quarter(ref, c, h):
        return ref[c, pl.ds(h * 8, 8)].reshape(128, 256)

    def weight_gram():
        arrived(u_recv, U_R)
        u_part[me] = total(u_send[me], u_recv)
        spread(u_part.at[me], U_G, shard_dev)

    out_mine = reduce_dp(
        lambda c, h: dot(quarter(w_all, c, h), act_t[...]),
        out_send, out_c, out_x, out_xr, out_y, out_yr, OUT, weight_gram,
        lambda: arrived(w_all.at[0, pl.ds(0, N - 1)], W_H), False,
    )
    og_all[slot] = (out_mine - target_mine).astype(BF16)
    gather_y(og_all, OG)
    gather_x(og_all, OG)

    def send_quarter(src, dst, which, c, h):
        def step(j, _):
            to = h * 8 + lax.rem(me + j, 8)

            @pl.when(to != me)
            def _():
                k = lax.rem(to + N - me, N)
                start(src.at[c, to], dst.at[c, k - 1], which, (dp, to))

            return 0

        lax.fori_loop(0, 8, step, 0, unroll=True)

    def share_half(src, recv, ref, which, after, c):
        arrived(recv.at[c], which)
        acc = src[c, me].astype(F32)
        for k in range(N - 1):
            acc = acc + recv[c, k].astype(F32)
        ref[c, me] = acc.astype(BF16)
        spread(ref.at[c, me], after, shard_dev)

    def g_part(c, h):
        og = og_all[pl.ds(c * N + h * 8, 8)].reshape(128, 1024)
        g_send[c, pl.ds(h * 8, 8)] = dot(og, act[...]).astype(BF16).reshape(8, 16, 256)

    gather_and_send(og_all, OG, g_part, g_send, g_recv, G_R)
    g_part(other, xo)
    send_quarter(g_send, g_recv, G_R + 1, other, xo)

    def assemble(part, count):
        rows = [
            jnp.concatenate([part[8 * h + b] for b in range(count)], axis=1)
            for h in range(2)
        ]
        return jnp.concatenate(rows, axis=0).astype(BF16)

    def to_twin_half(ref, which):
        half = ref.at[pl.ds(core * N, N)]
        to_twin(half, half, which)

    arrived(u_part.at[pl.ds(0, N - 1)], U_G)
    u_all[slot] = assemble(u_part, 4)
    spread(u_all.at[slot], UD_G, chip_dev)
    share_half(g_send, g_recv, g_all, G_R, G_G, core)
    share_half(g_send, g_recv, g_all, G_R + 1, G_G + 1, other)
    arrived(u_all.at[pl.ds(0, N - 1)], UD_G)
    to_twin_half(u_all, UD_C)

    def gradient():
        spread(q_all.at[:, me], Q_G, shard_dev)
        g_full = g_all[...].reshape(512, 256)
        grad = gains[...] * dot(weight[...], g_full)
        grad_out[...] = grad
        pltpu.make_async_copy(grad_out, grad_to, local.at[5]).start()
        square = jnp.sum((grad * grad).reshape(64, 8, 256), axis=0)
        sq[...] = square[:, :128] + square[:, 128:]
        to_twin(sq, sq_c, SQ_C)

    arrived(g_all.at[0, pl.ds(0, N - 1)], G_G)
    v_mine = reduce_dp(
        lambda c, h: dot(quarter(g_all, c, h), rb_t[...]),
        v_send, v_c, v_x, v_xr, v_y, v_yr, V, gradient,
        lambda: arrived(g_all.at[0, pl.ds(0, N - 1)], G_G + 1), True,
    ).astype(BF16)
    v_all[slot] = v_mine

    def blocks(ref, gram):
        for h in range(2):
            for b in range(8):
                block = 128 * (b % 4)
                ref[8 * h + b] = gram[8 * h : 8 * h + 8, block : block + 128]

    gather_direct(v_all, VG)
    blocks(n_send, dot(v_mine, stb, NT))
    scatter(n_send, n_recv, N_R)
    arrived_near(v_all, VG)
    arrived(n_recv, N_R)
    n_part[me] = total(n_send[me], n_recv)
    spread(n_part.at[me], N_G, shard_dev)

    def p_part(c, h):
        block = v_all[pl.ds(c * N + h * 8, 8)].reshape(128, 512)
        p_send[c, pl.ds(h * 8, 8)] = dot(block, rb[...]).astype(BF16).reshape(8, 16, 256)

    gather_and_send(v_all, VG, p_part, p_send, p_recv, P_R)
    vt = v_all[...].reshape(512, 512)
    blocks(m_send, dot(v_mine, vt, NT))
    scatter(m_send, m_recv, M_R)
    p_part(other, xo)
    send_quarter(p_send, p_recv, P_R + 1, other, xo)
    arrived(sq_c, SQ_C)
    sq_d[0] = sq[...] + sq_c[...]
    each(lambda k: start(sq_d.at[0], sq_d.at[k], SQ_D, chip_dev(k)))

    arrived(n_part.at[pl.ds(0, N - 1)], N_G)
    n_all[slot] = assemble(n_part, 4)
    gather_direct(n_all, NG)
    arrived(m_recv, M_R)
    m_part[me] = total(m_send[me], m_recv)
    spread(m_part.at[me], M_G, shard_dev)
    flush()
    share_half(p_send, p_recv, p_all, P_R, P_G, core)
    arrived_near(n_all, NG)
    arrived(sq_d.at[pl.ds(1, N - 1)], SQ_D)
    square = sq_d[0]
    for k in range(1, N):
        square = square + sq_d[k]
    sq_s[0] = square
    each(lambda k: start(sq_s.at[0], sq_s.at[k], SQ_S, shard_dev(k)))
    share_half(p_send, p_recv, p_all, P_R + 1, P_G + 1, other)
    arrived(m_part.at[pl.ds(0, N - 1)], M_G)
    m_all[slot] = assemble(m_part, 4)
    gather_direct(m_all, MG)
    gather_near(n_all, NG)
    gather_far(n_all, NG)
    v_full = vt.astype(F32).T.astype(BF16)
    arrived_near(m_all, MG)
    gather_near(m_all, MG)
    gather_far(m_all, MG)

    arrived(sq_s.at[pl.ds(1, N - 1)], SQ_S)
    for k in range(1, N):
        square = square + sq_s[k]
    square = jnp.sum(jnp.sum(square, axis=1, keepdims=True), axis=0, keepdims=True)
    step = 0.4 * math.sqrt(512) * lax.rsqrt(D * square + 1e-06)
    arrived(u_all.at[pl.ds(0, N)], UD_C)
    arrived(q_all.at[:, pl.ds(0, N - 1)], Q_G)
    q_full = q_all[...].reshape(512, 256)
    uu = u_all[...].reshape(512, 512)
    gather_other(n_all, NG)
    vu = n_all[...].reshape(512, 512)
    right = 2.0 * q_full.astype(F32) + step * dot(vu, q_full, TN)
    flush()
    gather_other(m_all, MG)
    vv = m_all[...].reshape(512, 512)
    left = step * dot(vv, q_full)
    arrived(p_all.at[0, pl.ds(0, N - 1)], P_G)
    arrived(p_all.at[0, pl.ds(0, N - 1)], P_G + 1)
    p_full = p_all[...].reshape(512, 256)
    left = left + 2.0 * p_full.astype(F32) - step * dot(vu, p_full)
    right = right - step * dot(uu, p_full)
    left, right = left.astype(BF16), right.astype(BF16)
    for c in range(4):
        rows = slice(128 * c, 128 * c + 128)
        applied = gains[rows] * dot(weight[rows], left) - dot(v_full[rows], right)
        next_out[rows] = rot[rows] - 0.5 * step * applied
        pltpu.make_async_copy(next_out.at[rows], next_to.at[rows], local.at[6]).start()

    flush()
    pltpu.make_async_copy(grad_out, grad_to, local.at[5]).wait()
    pltpu.make_async_copy(next_out, next_to, local.at[6]).wait()


def hand_over(grad_in, next_in, grad_to, next_to, held, come, gone):
    pairs = ((grad_in, grad_to), (next_in, next_to))

    def copies(n, c):
        rows = pl.ds(128 * c, 128)
        src, dst = pairs[n]
        here = held.at[n, rows]
        return (
            pltpu.make_async_copy(src.at[rows], here, come.at[n, c]),
            pltpu.make_async_copy(here, dst.at[rows], gone.at[n, c]),
        )

    steps = [copies(n, c) for c in range(4) for n in range(2)]
    for first, _ in steps:
        first.start()
    for first, second in steps:
        first.wait()
        second.start()
    for _, second in steps:
        second.wait()


def shards(residual, norm_gain, value_weight, rotation, target):
    hbm = pl.BlockSpec(memory_space=pltpu.HBM)
    scratch = [
        ((1024, 256), BF16), ((1, 512), F32), ((512, 512), BF16), ((512, 256), F32), ((1024, 512), BF16),
        ((512, 256), F32), ((512, 256), F32),
        ((512, 256), F32),
        ((512, 512), BF16),
        ((512, 256), BF16), ((256, 512), BF16),
        ((1024, 256), BF16), ((256, 1024), BF16),
        ((16, 128), F32), ((16, 128), F32), ((N, 16, 128), F32),
        ((N, 48, 256), BF16), ((N - 1, 48, 256), BF16), ((2, N, 16, 256), BF16), ((2, N, 16, 256), BF16),
        ((8, 128), F32), ((2 * N, 8, 128), F32),
        ((2, 128, 1024), BF16), ((2, 128, 1024), BF16), ((8, 16, 1024), BF16), ((8, 16, 1024), BF16),
        ((8, 16, 1024), F32), ((7, 16, 1024), BF16),
        ((2 * N, 16, 1024), BF16),
        ((2, N, 16, 256), BF16), ((2, N - 1, 16, 256), BF16), ((2, N, 16, 256), BF16),
        ((2, 128, 512), BF16), ((2, 128, 512), BF16), ((8, 16, 512), BF16), ((8, 16, 512), BF16),
        ((8, 16, 512), F32), ((7, 16, 512), BF16),
        ((2 * N, 16, 512), BF16),
        ((2, N, 16, 256), BF16), ((2, N - 1, 16, 256), BF16), ((2, N, 16, 256), BF16),
        ((8, 128), F32), ((8, 128), F32), ((N, 8, 128), F32), ((N, 8, 128), F32),
        ((N, 8, 128), F32), ((N - 1, 8, 128), F32), ((N, 8, 128), F32), ((2 * N, 16, 512), BF16),
        ((N, 8, 128), F32), ((N - 1, 8, 128), F32), ((N, 8, 128), F32), ((2 * N, 16, 512), BF16),
        ((N, 8, 128), F32), ((N - 1, 8, 128), F32), ((N, 8, 128), F32), ((2 * N, 16, 512), BF16),
    ]
    buffers = [pltpu.VMEM(shape, kind) for shape, kind in scratch]
    results = [jax.ShapeDtypeStruct((512, 256), F32)] * 2
    computed = pl.pallas_call(
        kernel,
        out_shape=results,
        in_specs=[hbm] * 5,
        out_specs=[hbm] * 2,
        scratch_shapes=buffers[:7] + [pltpu.SemaphoreType.DMA((7,))] + buffers[7:]
        + [pltpu.SemaphoreType.DMA((COUNT,)), pltpu.SemaphoreType.DMA((COUNT,))],
        compiler_params=pltpu.CompilerParams(
            collective_id=0, has_side_effects=True, vmem_limit_bytes=LIMIT
        ),
        cost_estimate=pl.CostEstimate(
            flops=2 * 10**9, bytes_accessed=4 * 2**20, transcendentals=0
        ),
    )(residual, norm_gain.reshape(1, -1), value_weight, rotation, target)
    return pl.pallas_call(
        hand_over,
        out_shape=results,
        in_specs=[hbm] * 2,
        out_specs=[hbm] * 2,
        scratch_shapes=[pltpu.VMEM((2, 512, 256), F32)]
        + [pltpu.SemaphoreType.DMA((2, 4))] * 2,
        compiler_params=pltpu.CompilerParams(vmem_limit_bytes=LIMIT),
        cost_estimate=pl.CostEstimate(flops=0, bytes_accessed=2 * 2**20, transcendentals=0),
    )(*computed)


def solution(mesh):
    in_specs = (P("shard", "dp"), P("shard"), P("shard", None), P("shard", "dp"), P("shard", None))
    out_specs = (P("shard", "dp"), P("shard", "dp"))
    return jax.shard_map(
        lambda *a: tuple(shards(*a)), mesh=mesh, in_specs=in_specs, out_specs=out_specs, check_vma=False
    )
```
